32 devices in a mesh: dp: 4 (over x, core), expert: 4 (over z), tensor: 2 (over y).
Axes of the slice: x: 2, y: 2, z: 4, core: 2. Of those that a mesh axis runs over, the one named last changes fastest.
Arguments:
- x_in: bfloat16 [4096, 1536], P(('dp', 'expert')), may hold values from -6 to 6
- segments: int32 [4096], P('dp'), may hold values from 0 to 1023, as said below
- chosen: int32 [4096, 8], P(('dp', 'expert')), may hold values from 0 to 39, all different within a row; in each aligned block of 256 rows (0 to 255, 256 to 511, ...) at most 80 rows name the same one
- out_grad: bfloat16 [4096, 1536], P(('dp', 'expert')), may hold values from -6 to 6
- norm1_gain: float32 [1536], replicated, may hold values from 0.5 to 1.5
- w_query: bfloat16 [1536, 1536], P(None, 'tensor'), may hold values from -0.3125 to 0.3125
- w_key: bfloat16 [1536, 512], P(None, 'tensor'), may hold values from -0.15625 to 0.15625
- w_value: bfloat16 [1536, 512], P(None, 'tensor'), may hold values from -0.15625 to 0.15625
- w_out: bfloat16 [1536, 1536], P('tensor'), may hold values from -0.625 to 0.625
- norm2_gain: float32 [1536], replicated, may hold values from 0.5 to 1.5
- w_router: bfloat16 [1536, 40], replicated, may hold values from -0.078125 to 0.078125
- w_gate: bfloat16 [40, 1536, 512], P('expert', None, 'tensor'), may hold values from -0.15625 to 0.15625
- w_up: bfloat16 [40, 1536, 512], P('expert', None, 'tensor'), may hold values from -0.15625 to 0.15625
- w_down: bfloat16 [40, 512, 1536], P('expert', 'tensor'), may hold values from -1 to 1
Outputs:
- block_out: bfloat16 [4096, 1536], P(('dp', 'expert'), 'tensor')
- input_grad: float32 [4096, 1536], P(('dp', 'expert'))
- grad_norm1: float32 [1536], P(('dp', 'expert'))
- grad_query: float32 [1536, 1536], P(('dp', 'expert'), 'tensor')
- grad_key: float32 [1536, 512], P(('dp', 'expert'), 'tensor')
- grad_value: float32 [1536, 512], P(('dp', 'expert'), 'tensor')
- grad_out: float32 [1536, 1536], P('tensor', ('dp', 'expert'))
- grad_norm2: float32 [1536], P(('dp', 'expert'))
- grad_router: float32 [1536, 40], P(('dp', 'expert'))
- grad_gate: float32 [40, 1536, 512], P('expert', 'dp', 'tensor')
- grad_up: float32 [40, 1536, 512], P('expert', 'dp', 'tensor')
- grad_down: float32 [40, 512, 1536], P('expert', 'tensor', 'dp')
The draws below stay inside these ranges and needn't reach their ends.
Inputs may be any that keep to these rules, and one draw needn't show every extreme that they name: `segments`: document numbers never fall along a sequence, and the last token of every sequence carries 1024 - 1; documents do not attend to each other. `chosen`: each token names 8 different experts; among the tokens of one device no expert is named by more than 80 of them.
All inputs are finite; a program needn't handle non-finite values.
Results may differ from the reference program's by a relative error of at most 0.022.
Values may be sent and summed in bfloat16 or wider, within the bound.
No kernel may reach another device: no remote copies, remote signals or barrier semaphores. Data moves between devices by JAX's collectives and lax.ppermute only.
A program may use at most 320 MiB of HBM per device.

```python
import math
import jax
import jax.numpy as jnp
import numpy as np
from jax import lax

D = 1536
HEADS = 24
KV_HEADS = 8
HEAD_DIM = 64
FF = 512
TOPK = 8
TOK_DEV = 256
EXPERTS = 40
LENGTH = 1024
SEQS = 4
TOKENS = 4096
MOST = 80


def draw_segments(key, part):
    key = jax.random.fold_in(key, 7)
    keys = jax.random.split(key, 3)
    span = LENGTH // 8
    first_cut = jax.random.randint(keys[0], (SEQS, 1), 1, span)
    last_cut = LENGTH - jax.random.randint(keys[1], (SEQS, 1), 1, span)
    positions = jnp.arange(LENGTH, dtype=jnp.int32)[None, :]
    extra_cuts = jax.random.randint(keys[2], (SEQS, LENGTH), 0, 6) == 0
    outside = (positions < first_cut) | (positions > last_cut)
    starts = (positions == first_cut) | (positions == last_cut) | extra_cuts & outside
    starts = starts & (positions > 0)
    numbers = jnp.cumsum(starts.astype(jnp.int32), axis=1)
    shift = LENGTH - 1 - numbers[:, LENGTH - 1:LENGTH]
    return (numbers + shift).reshape(-1)


def block_levels(own_key, extent, cuts, low, high):
    def one(position, blocks):
        steps = jax.random.uniform(jax.random.fold_in(jax.random.fold_in(own_key, 6), position), (blocks,), jnp.float32, low / len(cuts), high / len(cuts))
        return jnp.repeat(jnp.exp(steps), extent[position] // blocks).reshape((-1,) + (1,) * (len(extent) - position - 1))

    level = one(*cuts[0])
    for cut in cuts[1:]:
        level = level * one(*cut)
    return level


def assign_block(own_key, own, number, rows, amount, top, limit, slope):
    sequence = jax.random.permutation(own_key, amount)
    crowded, common = load_shares(amount, rows * top, limit, slope, True), load_shares(amount, rows * top, limit, slope, False)
    places = jnp.arange(amount)

    def named(sizes, rotation):
        used = int((sizes > 0).sum())
        fixed = max(1, used // 4)
        shifted = fixed + (places - fixed + rotation * (used - fixed)) % max(1, amount - fixed)
        return jnp.zeros((amount,), jnp.int32).at[sequence[jnp.where(places < fixed, places, shifted)]].set(jnp.asarray(sizes, jnp.int32))

    sizes = jnp.where(number % 4 == 0, named(crowded, number // 4), named(common, number - number // 4 - 1))
    mixed = jax.random.permutation(jax.random.fold_in(own, 3), amount)
    giver, taker = mixed[0:amount // 2 * 2:2], mixed[1:amount // 2 * 2:2]
    margin = jnp.minimum(sizes[giver] - 1, limit - sizes[taker]) // 2
    margin = jnp.where((giver == sequence[0]) | (taker == sequence[0]) | (sizes[taker] == 0), 0, jnp.maximum(margin, 0))
    shifted = jax.random.randint(jax.random.fold_in(own, 4), (amount // 2,), 0, 1 << 20) % (margin + 1)
    sizes = sizes.at[giver].add(-shifted).at[taker].add(shifted)
    items = jnp.searchsorted(jnp.cumsum(sizes), jnp.arange(rows * top), side="right").astype(jnp.int32)
    listing = items.reshape(top, rows).T
    listing = listing[jax.random.permutation(jax.random.fold_in(own, 1), rows)]
    rotation = jax.random.randint(jax.random.fold_in(own, 2), (rows, 1), 0, top)
    return jnp.take_along_axis(listing, (jnp.arange(top)[None, :] + rotation) % top, axis=1)


def load_shares(count, total, reach, lean, full):
    portions = [(1 << 20) // math.isqrt(grade ** lean) + 1 for grade in range(1, count + 1)]
    largest = reach if full else min(reach, max(-(-total // count), total * portions[0] // sum(portions)))
    least = 1 if total - largest >= count - 1 else 0
    counts, surplus = [largest] + [least] * (count - 1), total - largest - least * (count - 1)
    while surplus > 0:
        free = [i for i in range(1, count) if counts[i] < largest] or [i for i in range(1, count) if counts[i] < reach]
        mass, budget = sum([portions[i] for i in free]), surplus
        for i in free:
            more = min(reach - counts[i], max(1, budget * portions[i] // mass), surplus)
            counts[i] = counts[i] + more
            surplus = surplus - more
    return np.array(counts)


def bell_draw(rng, dims, deviation, most, cuts=(), kind=jnp.bfloat16):
    entries = deviation * jax.random.normal(rng, dims, jnp.float32)
    if cuts:
        entries = entries * block_levels(rng, dims, cuts, -0.22, 0.18)
    return jnp.clip(entries, -most, most).astype(kind)


def setup_inputs(seed: int = 0) -> dict:
    key_of = jax.random.split(jax.random.key(seed), 15)
    x_in = bell_draw(key_of[0], (TOKENS, D), 1.0, 6.0, ((0, 16),))
    segments = draw_segments(jax.random.fold_in(key_of[14], 71), 0)
    chosen_keys = jax.random.split(jax.random.fold_in(key_of[2], 1), TOKENS // TOK_DEV)
    chosen_turns = jax.random.permutation(jax.random.fold_in(key_of[2], 3), TOKENS // TOK_DEV)
    chosen = jax.vmap(lambda own, number: assign_block(jax.random.fold_in(key_of[2], 2), own, number, TOK_DEV, EXPERTS, TOPK, MOST, 2))(chosen_keys, chosen_turns).reshape((TOKENS, TOPK))
    out_grad = bell_draw(key_of[3], (TOKENS, D), 1.0, 6.0, ((0, 16),))
    norm1_gain = jnp.clip(1.0 + 0.1 * jax.random.normal(key_of[4], (D,), jnp.float32), 0.5, 1.5)
    w_query = bell_draw(key_of[5], (D, HEADS * HEAD_DIM), (D // 4) ** -0.5, 0.3125, ((1, 2),))
    w_key = bell_draw(key_of[6], (D, KV_HEADS * HEAD_DIM), D ** -0.5, 0.15625, ((1, 2),))
    w_value = bell_draw(key_of[7], (D, KV_HEADS * HEAD_DIM), D ** -0.5, 0.15625, ((1, 2),))
    w_out = bell_draw(key_of[8], (HEADS * HEAD_DIM, D), (HEADS * HEAD_DIM // 16) ** -0.5, 0.625, ((0, 2),))
    norm2_gain = jnp.clip(1.0 + 0.1 * jax.random.normal(key_of[9], (D,), jnp.float32), 0.5, 1.5)
    w_router = bell_draw(key_of[10], (D, EXPERTS), (4 * D) ** -0.5, 0.078125)
    w_gate = bell_draw(key_of[11], (EXPERTS, D, FF), D ** -0.5, 0.15625, ((0, 4), (2, 2)))
    w_up = bell_draw(key_of[12], (EXPERTS, D, FF), D ** -0.5, 0.15625, ((0, 4), (2, 2)))
    w_down = bell_draw(key_of[13], (EXPERTS, FF, D), (FF // 16) ** -0.5, 1.0, ((0, 4), (1, 2)))
    return {"x_in": x_in, "segments": segments, "chosen": chosen, "out_grad": out_grad, "norm1_gain": norm1_gain, "w_query": w_query, "w_key": w_key, "w_value": w_value, "w_out": w_out, "norm2_gain": norm2_gain, "w_router": w_router, "w_gate": w_gate, "w_up": w_up, "w_down": w_down}


EPSILON = 1e-05
ROPE_BASE = 10000.0
MASKED = -1e+30
HIGHEST = lax.Precision.HIGHEST

@jax.custom_vjp
def low(v):
    return lax.optimization_barrier(v.astype(jnp.bfloat16)).astype(jnp.float32)

@jax.custom_vjp
def low_back(v):
    return v

def low_keep(v):
    return (low(v), None)

def low_pass(kept, grad):
    return (grad,)

def back_keep(v):
    return (v, None)

def back_low(kept, grad):
    return (low(grad),)
low.defvjp(low_keep, low_pass)
low_back.defvjp(back_keep, back_low)

def rotate(values, positions, direction):
    half_dim = HEAD_DIM // 2
    inverse = ROPE_BASE ** (-2.0 * jnp.arange(half_dim, dtype=jnp.float32) / HEAD_DIM)
    angles = positions.astype(jnp.float32)[:, None] * inverse[None, :]
    cosine = jnp.cos(angles)[:, None, :]
    sine = direction * jnp.sin(angles)[:, None, :]
    first_half = values[..., :half_dim]
    second_half = values[..., half_dim:]
    return jnp.concatenate([first_half * cosine - second_half * sine, second_half * cosine + first_half * sine], axis=-1)

def rms_normed(values, gain):
    norm_scale = lax.rsqrt(lax.optimization_barrier(jnp.mean(values * values, axis=-1, keepdims=True)) + EPSILON)
    return values * norm_scale * gain

def matmul(left, right):
    return jnp.dot(left, right, precision=HIGHEST)

def attend_head(q_head, k_head, v_head, key_mask):
    scores = low_back(jnp.einsum('qgd,kd->gqk', q_head, k_head, precision=HIGHEST) * HEAD_DIM ** (-0.5))
    scores = jnp.where(key_mask[None], scores, MASKED)
    attention_probs = low(jax.nn.softmax(scores, axis=-1))
    return jnp.einsum('gqk,kd->qgd', attention_probs, v_head, precision=HIGHEST)

def experts_row(normed_two, expert_row, gate_weights, gate_w, up_w, down_w):
    block_count = normed_two.shape[0] // TOK_DEV
    per_block = TOK_DEV * TOPK
    flat_expert = expert_row.reshape(block_count, per_block)
    flat_hot = (flat_expert[:, :, None] == jnp.arange(EXPERTS, dtype=jnp.int32)).astype(jnp.int32)
    slot_index = lax.optimization_barrier(jnp.sum(jnp.cumsum(flat_hot, axis=1) * flat_hot, axis=2)) - 1
    dest_index = flat_expert * MOST + slot_index
    pair_ids = jnp.arange(block_count * per_block, dtype=jnp.int32).reshape(block_count, per_block)
    table = jnp.full((block_count, EXPERTS * MOST), -1, jnp.int32)
    table = table.at[jnp.arange(block_count, dtype=jnp.int32)[:, None], dest_index].set(pair_ids)
    table = table.reshape(block_count, EXPERTS, MOST).transpose(1, 0, 2).reshape(EXPERTS, block_count * MOST)
    is_valid = table >= 0
    safe_ids = jnp.where(is_valid, table, 0)
    token_ids = safe_ids // TOPK
    expert_in = normed_two[token_ids]
    gate_pre = low_back(jnp.einsum('erd,edf->erf', expert_in, gate_w, precision=HIGHEST))
    up_pre = low_back(jnp.einsum('erd,edf->erf', expert_in, up_w, precision=HIGHEST))
    activated = low(jax.nn.silu(gate_pre) * up_pre)
    expert_out = low_back(jnp.einsum('erf,efd->erd', activated, down_w, precision=HIGHEST))
    weight_rows = jnp.where(is_valid, gate_weights.reshape(-1)[safe_ids], 0.0)
    contrib = expert_out * weight_rows[:, :, None]
    total_out = jnp.zeros_like(normed_two)
    return total_out.at[token_ids.reshape(-1)].add(contrib.reshape(-1, normed_two.shape[1]))

def layer_row(x_row, segment_row, expert_row, gain_one, query_w, key_w, value_w, out_w, gain_two, router_w, gate_w, up_w, down_w):
    seq_length = x_row.shape[0]
    positions = jnp.arange(seq_length, dtype=jnp.int32)
    key_mask = (segment_row[:, None] == segment_row[None, :]) & (positions[:, None] >= positions[None, :])
    normed_one = low(rms_normed(x_row, gain_one))
    query_pre = low_back(matmul(normed_one, query_w)).reshape(seq_length, HEADS, HEAD_DIM)
    key_pre = low_back(matmul(normed_one, key_w)).reshape(seq_length, KV_HEADS, HEAD_DIM)
    value_all = low_back(low(matmul(normed_one, value_w))).reshape(seq_length, KV_HEADS, HEAD_DIM)
    query_rot = low(rotate(query_pre, positions, 1.0)).reshape(seq_length, KV_HEADS, HEADS // KV_HEADS, HEAD_DIM)
    key_rot = low(rotate(key_pre, positions, 1.0))
    attend_saved = jax.checkpoint(attend_head)
    head_outputs = lax.map(lambda operands: attend_saved(operands[0], operands[1], operands[2], key_mask), (query_rot.transpose(1, 0, 2, 3), key_rot.transpose(1, 0, 2), value_all.transpose(1, 0, 2)))
    attended = low_back(low(head_outputs.transpose(1, 0, 2, 3).reshape(seq_length, HEADS * HEAD_DIM)))
    hidden_one = x_row + low_back(matmul(attended, out_w))
    normed_two = low(rms_normed(hidden_one, gain_two))
    logits = low_back(matmul(normed_two, router_w))
    gate_weights = jax.nn.softmax(jnp.take_along_axis(logits, expert_row, axis=1), axis=-1)
    return hidden_one + experts_row(normed_two, expert_row, gate_weights, gate_w, up_w, down_w)

def reference(x_in, segments, chosen, out_grad, norm1_gain, w_query, w_key, w_value, w_out, norm2_gain, w_router, w_gate, w_up, w_down):
    row_step = jax.checkpoint(layer_row)

    def forward(inputs, gain_one, query_w, key_w, value_w, out_w, gain_two, router_w, gate_w, up_w, down_w):

        def one_row(operands):
            return row_step(operands[0], operands[1], operands[2], gain_one, query_w, key_w, value_w, out_w, gain_two, router_w, gate_w, up_w, down_w)
        mapped = lax.map(one_row, (inputs.reshape(SEQS, LENGTH, D), segments.reshape(SEQS, LENGTH), chosen.reshape(SEQS, LENGTH, TOPK)))
        return mapped.reshape(TOKENS, D)
    primals = (x_in.astype(jnp.float32), norm1_gain, w_query.astype(jnp.float32), w_key.astype(jnp.float32), w_value.astype(jnp.float32), w_out.astype(jnp.float32), norm2_gain, w_router.astype(jnp.float32), w_gate.astype(jnp.float32), w_up.astype(jnp.float32), w_down.astype(jnp.float32))
    result, pullback = jax.vjp(forward, *primals)
    grads = pullback(out_grad.astype(jnp.float32))
    return (result.astype(jnp.bfloat16), grads[0], grads[1], grads[2], grads[3], grads[4], grads[5], grads[6], grads[7], grads[8], grads[9], grads[10])
```

```python
import jax
import jax.numpy as jnp
from jax import lax
from jax.sharding import PartitionSpec as P

HEAD_DIM = 64


EPSILON = 1e-05
ROPE_BASE = 10000.0
MASKED = -1e30


def rotate(values, positions, direction):
    head_size = values.shape[-1]
    half_dim = head_size // 2
    inverse = ROPE_BASE ** (-2.0 * jnp.arange(half_dim, dtype=jnp.float32) / head_size)
    angles = positions.astype(jnp.float32)[:, None] * inverse[None, :]
    cosine = jnp.cos(angles)[:, None, :]
    sine = direction * jnp.sin(angles)[:, None, :]
    first_half = values[..., :half_dim]
    second_half = values[..., half_dim:]
    return jnp.concatenate(
        [first_half * cosine - second_half * sine, second_half * cosine + first_half * sine],
        axis=-1,
    )


def norm_forward(values, gain):
    norm_scale = lax.rsqrt(jnp.mean(values * values, axis=1, keepdims=True) + EPSILON)
    return (norm_scale, values * norm_scale * gain)


def norm_backward(values, norm_scale, gain, grad_normed):
    weighted = grad_normed * gain
    inner = jnp.mean(weighted * values, axis=1, keepdims=True)
    grad_values = norm_scale * weighted - values * (norm_scale * norm_scale * norm_scale) * inner
    grad_gain = jnp.sum(grad_normed * values * norm_scale, axis=0)
    return (grad_values, grad_gain)


def swap(values, axis, bit=1):
    count = lax.axis_size(axis)
    return lax.ppermute(values, axis, [(i, i ^ bit) for i in range(count)])


def fetch(values, offset):
    count = lax.axis_size("expert")
    return lax.ppermute(values, "expert", [(i, (i - offset) % count) for i in range(count)])


def deliver(values, offset):
    count = lax.axis_size("expert")
    return lax.ppermute(values, "expert", [(i, (i + offset) % count) for i in range(count)])


def gather_blocks(rows, side):
    half = rows.shape[0] // 2
    own = lax.dynamic_slice_in_dim(rows, side * half, half)
    other = lax.dynamic_slice_in_dim(rows, (1 - side) * half, half)
    blocks = [(own, other)]
    for offset in range(1, lax.axis_size("expert")):
        far = fetch(own, offset)
        blocks.append((far, swap(far, "tensor")))
    return jnp.stack([jnp.concatenate(pair, axis=0) for pair in blocks])


def reduce_blocks(partial):
    blocks, rows, width = partial.shape
    half = rows // 2
    total = None
    for offset in range(blocks - 1, -1, -1):
        mine = partial[offset, :half].astype(jnp.float32)
        got = swap(partial[offset, half:], "tensor").astype(jnp.float32)
        piece = mine + got
        if offset:
            piece = deliver(piece.astype(jnp.bfloat16), offset).astype(jnp.float32)
        total = piece if total is None else total + piece
    return total


def halve(parts, bit_axis, bit):
    pairs = parts.reshape((parts.shape[0] // 2, 2) + parts.shape[1:])
    own = (lax.axis_index(bit_axis) // bit) % 2
    keep = lax.dynamic_index_in_dim(pairs, own, 1, keepdims=False)
    send = lax.dynamic_index_in_dim(pairs, 1 - own, 1, keepdims=False)
    got = swap(send, bit_axis, bit)
    return keep.astype(jnp.float32) + got.astype(jnp.float32)


def sum_over_dp(parts):
    bit = 1
    while parts.shape[0] > 1:
        parts = halve(parts.astype(jnp.bfloat16), "dp", bit)
        bit *= 2
    return parts[0]


def sum_over_tokens(rows):
    devices = lax.axis_size("dp") * lax.axis_size("expert")
    n_exp = lax.axis_size("expert")
    width = rows.shape[1]
    parts = rows.reshape(lax.axis_size("dp"), -1, width)
    bit = 1
    step = lax.axis_size("dp")
    parts = halve(parts, "dp", bit).astype(jnp.bfloat16)
    m = parts.shape[0]
    parts = parts.reshape(m, n_exp, -1, width)
    place = lax.axis_index("expert")
    total = lax.dynamic_index_in_dim(parts, place, 1, keepdims=False).astype(jnp.float32)
    for offset in range(1, n_exp):
        piece = lax.dynamic_index_in_dim(parts, (place + offset) % n_exp, 1, keepdims=False)
        total = total + deliver(piece, offset).astype(jnp.float32)
    bit = 2
    while total.shape[0] > 1:
        total = halve(total.astype(jnp.bfloat16), "dp", bit)
        bit *= 2
    return total[0]


def body(
    x_in,
    segments,
    chosen,
    out_grad,
    norm1_gain,
    w_query,
    w_key,
    w_value,
    w_out,
    norm2_gain,
    w_router,
    w_gate,
    w_up,
    w_down,
):
    tok_rows, full_width = x_in.shape
    head_size = HEAD_DIM
    kv_local = w_key.shape[1] // head_size
    query_local = w_query.shape[1] // head_size
    groups = query_local // kv_local
    experts_local = w_gate.shape[0]
    expert_devices = lax.axis_size("expert")
    tensor_devices = lax.axis_size("tensor")
    total_experts = experts_local * expert_devices
    top_count = chosen.shape[1]
    dp_devices = lax.axis_size("dp")
    capacity = tok_rows * top_count * 25 // (16 * total_experts)
    place = lax.axis_index("expert")
    side = lax.axis_index("tensor")
    half_width = full_width // tensor_devices
    row_start = lax.axis_index("expert") * tok_rows
    seq_length = segments.shape[0]
    positions = row_start + jnp.arange(tok_rows, dtype=jnp.int32)
    key_positions = jnp.arange(seq_length, dtype=jnp.int32)
    query_segments = lax.dynamic_slice_in_dim(segments, row_start, tok_rows)
    key_mask = (query_segments[:, None] == segments[None, :]) & (
        positions[:, None] >= key_positions[None, :]
    )
    score_scale = head_size ** (-0.5)
    inputs = x_in.astype(jnp.float32)
    scale_one, normed_one = norm_forward(inputs, norm1_gain)
    normed_one = normed_one.astype(jnp.bfloat16)
    query_pre = jnp.dot(normed_one, w_query, preferred_element_type=jnp.float32)
    key_pre = jnp.dot(normed_one, w_key, preferred_element_type=jnp.float32)
    value_pre = jnp.dot(normed_one, w_value, preferred_element_type=jnp.float32)
    query_rot = rotate(query_pre.reshape(tok_rows, query_local, head_size), positions, 1.0).astype(
        jnp.bfloat16
    )
    key_rot = (
        rotate(key_pre.reshape(tok_rows, kv_local, head_size), positions, 1.0)
        .astype(jnp.bfloat16)
        .reshape(tok_rows, kv_local * head_size)
    )
    value_low = value_pre.astype(jnp.bfloat16)
    kv_own = jnp.concatenate([key_rot, value_low], axis=1)
    kv_blocks = [kv_own] + [fetch(kv_own, k) for k in range(1, expert_devices)]
    kv_stack = jnp.stack(kv_blocks)
    kv_all = jnp.take(kv_stack, (jnp.arange(expert_devices) - place) % expert_devices, axis=0).reshape(seq_length, -1)
    keys_all, values_all = kv_all[:, : kv_local * head_size], kv_all[:, kv_local * head_size :]
    cot_in, chosen_in, kv_all = lax.optimization_barrier((out_grad, chosen, kv_all))
    cot_blocks = gather_blocks(cot_in, side)
    chosen_flip = jnp.where(side == 0, chosen_in, jnp.roll(chosen_in, tok_rows // 2, axis=0)).T
    chosen_blocks = jnp.stack([chosen_flip] + [fetch(chosen_flip, k) for k in range(1, expert_devices)])
    expert_ids = jnp.arange(total_experts, dtype=jnp.int32)
    hot_all = jnp.any(chosen_blocks[:, :, :, None] == expert_ids, axis=1)
    hot_local = lax.dynamic_slice_in_dim(hot_all, place * experts_local, experts_local, 2)
    token_row = jnp.arange(tok_rows, dtype=jnp.int32)
    before = (token_row[:, None] > token_row[None, :]).astype(jnp.bfloat16)
    rank = jnp.einsum("ts,kse->kte", before, hot_local.astype(jnp.bfloat16), preferred_element_type=jnp.float32).astype(jnp.int32)
    slot_of = jnp.where(hot_local, rank, -1).transpose(0, 2, 1)
    slot_hit = slot_of[:, :, None, :] == jnp.arange(capacity, dtype=jnp.int32)[:, None]
    pick = slot_hit.astype(jnp.bfloat16)
    pick_flat = pick.reshape(expert_devices, experts_local * capacity, tok_rows)
    cot_slots = jnp.einsum("kst,ktd->ksd", pick_flat, cot_blocks, preferred_element_type=jnp.float32).astype(jnp.bfloat16).reshape(expert_devices, experts_local, capacity, full_width)
    raw_grad = jnp.einsum("kesd,efd->kesf", cot_slots, w_down, preferred_element_type=jnp.float32)
    query_heads = query_rot.reshape(tok_rows, kv_local, groups, head_size).transpose(1, 0, 2, 3)
    key_heads = keys_all.reshape(seq_length, kv_local, head_size).transpose(1, 0, 2)
    value_heads = values_all.reshape(seq_length, kv_local, head_size).transpose(1, 0, 2)

    def head_forward(operands):
        q_head, k_head, v_head = operands
        scores = (
            jnp.einsum("qgd,kd->gqk", q_head, k_head, preferred_element_type=jnp.float32)
            * score_scale
        )
        scores = jnp.where(key_mask[None], scores, MASKED)
        row_peak = jnp.max(scores, axis=2, keepdims=True)
        raw_weights = jnp.exp(scores - row_peak)
        row_total = jnp.sum(raw_weights, axis=2, keepdims=True)
        probs_low = (raw_weights / row_total).astype(jnp.bfloat16)
        head_out = jnp.einsum("gqk,kd->qgd", probs_low, v_head, preferred_element_type=jnp.float32)
        return (head_out, (row_peak + jnp.log(row_total))[:, :, 0])

    attended_heads, log_totals = lax.map(head_forward, (query_heads, key_heads, value_heads))
    attended_low = (
        attended_heads.transpose(1, 0, 2, 3)
        .reshape(tok_rows, query_local * head_size)
        .astype(jnp.bfloat16)
    )
    head_partial = jnp.dot(attended_low, w_out, preferred_element_type=jnp.float32)
    head_low = head_partial.astype(jnp.bfloat16)
    hidden_one = inputs + head_low.astype(jnp.float32) + swap(head_low, "tensor").astype(jnp.float32)
    scale_two, normed_two = norm_forward(hidden_one, norm2_gain)
    normed_two = normed_two.astype(jnp.bfloat16)
    def gates_of(rows, hot):
        logits = jnp.dot(rows, w_router, preferred_element_type=jnp.float32)
        masked = jnp.where(hot, logits, MASKED)
        raw = jnp.where(hot, jnp.exp(masked - jnp.max(masked, axis=-1, keepdims=True)), 0.0)
        return raw / jnp.sum(raw, axis=-1, keepdims=True)

    token_blocks = gather_blocks(normed_two, side)
    gates_all = gates_of(token_blocks, hot_all)
    gates_local = lax.dynamic_slice_in_dim(gates_all, place * experts_local, experts_local, 2).transpose(0, 2, 1)
    gate_slots = jnp.sum(jnp.where(slot_hit, gates_local[:, :, None, :], 0.0), axis=3)[..., None]
    row_slots = jnp.einsum("kst,ktd->ksd", pick_flat, token_blocks, preferred_element_type=jnp.float32).astype(jnp.bfloat16).reshape(expert_devices, experts_local, capacity, full_width)
    gate_pre = jnp.einsum("kesd,edf->kesf", row_slots, w_gate, preferred_element_type=jnp.float32)
    up_pre = jnp.einsum("kesd,edf->kesf", row_slots, w_up, preferred_element_type=jnp.float32)
    sigmoid_gate = jax.nn.sigmoid(gate_pre)
    swish_gate = gate_pre * sigmoid_gate
    activated = swish_gate * up_pre
    dgate_slots = jnp.sum(activated * raw_grad, axis=3)
    gated = (gate_slots * activated).astype(jnp.bfloat16)
    activated_grad = gate_slots * raw_grad
    gate_pre_grad = (activated_grad * up_pre * sigmoid_gate * (1.0 + gate_pre * (1.0 - sigmoid_gate))).astype(jnp.bfloat16)
    up_pre_grad = (activated_grad * swish_gate).astype(jnp.bfloat16)
    in_grad = (
        jnp.einsum("kesf,edf->kesd", gate_pre_grad, w_gate, preferred_element_type=jnp.float32)
        + jnp.einsum("kesf,edf->kesd", up_pre_grad, w_up, preferred_element_type=jnp.float32)
    ).astype(jnp.bfloat16).reshape(expert_devices, experts_local * capacity, full_width)
    in_grad_part = jnp.einsum("kst,ksd->ktd", pick_flat, in_grad, preferred_element_type=jnp.float32).astype(jnp.bfloat16)
    dgate_part = jnp.sum(jnp.where(slot_hit, dgate_slots[..., None], 0.0), axis=2)
    dgate_own = dgate_part + jnp.roll(swap(dgate_part, "tensor"), tok_rows // 2, axis=2)
    dgate_stack = jnp.stack([dgate_own[0]] + [deliver(dgate_own[k], k) for k in range(1, expert_devices)])
    dgate_dense = jnp.take(dgate_stack, (place - jnp.arange(expert_devices)) % expert_devices, axis=0).reshape(total_experts, tok_rows)
    dgate_dense = jnp.where(side == 0, dgate_dense, jnp.roll(dgate_dense, tok_rows // 2, axis=1)).T
    hot_own = jnp.any(chosen[:, :, None] == expert_ids, axis=1)
    gates_own = gates_of(normed_two, hot_own)
    logit_grads = (gates_own * (dgate_dense - jnp.sum(gates_own * dgate_dense, axis=1, keepdims=True))).astype(jnp.bfloat16)
    half_sum = reduce_blocks(in_grad_part).astype(jnp.bfloat16)
    half_other = swap(half_sum, "tensor")
    expert_grad = jnp.where(
        side == 0,
        jnp.concatenate([half_sum, half_other], axis=0),
        jnp.concatenate([half_other, half_sum], axis=0),
    ).astype(jnp.float32)
    out_slots = jnp.einsum("kesf,efd->kesd", gated, w_down, preferred_element_type=jnp.float32).astype(jnp.bfloat16).reshape(expert_devices, experts_local * capacity, full_width)
    out_part = jnp.einsum("kst,ksd->ktd", pick_flat, out_slots, preferred_element_type=jnp.float32).astype(jnp.bfloat16)
    out_mine = lax.dynamic_slice_in_dim(out_part, side * half_width, half_width, 2)
    out_else = lax.dynamic_slice_in_dim(out_part, (1 - side) * half_width, half_width, 2)
    out_got = jnp.roll(swap(out_else, "tensor"), tok_rows // 2, axis=1)
    out_sum = out_mine.astype(jnp.float32) + out_got.astype(jnp.float32)
    out_low = out_sum.astype(jnp.bfloat16)
    mixture_half = out_sum[0]
    for k in range(1, expert_devices):
        mixture_half = mixture_half + deliver(out_low[k], k).astype(jnp.float32)
    mixture_half = jnp.where(side == 0, mixture_half, jnp.roll(mixture_half, tok_rows // 2, axis=0))
    residual_half = lax.dynamic_slice_in_dim(hidden_one, side * half_width, half_width, 1)
    block_out = (residual_half + mixture_half).astype(jnp.bfloat16)
    grad_down = jnp.einsum("kesf,kesd->efd", gated, cot_slots, preferred_element_type=jnp.float32).astype(jnp.bfloat16)
    grad_gate = jnp.einsum("kesd,kesf->edf", row_slots, gate_pre_grad, preferred_element_type=jnp.float32).astype(jnp.bfloat16)
    grad_up = jnp.einsum("kesd,kesf->edf", row_slots, up_pre_grad, preferred_element_type=jnp.float32).astype(jnp.bfloat16)
    inner = w_gate.shape[2]
    grad_gate = sum_over_dp(grad_gate.reshape(experts_local, dp_devices, -1, inner).transpose(1, 0, 2, 3))
    grad_up = sum_over_dp(grad_up.reshape(experts_local, dp_devices, -1, inner).transpose(1, 0, 2, 3))
    grad_down = sum_over_dp(grad_down.reshape(experts_local, inner, dp_devices, -1).transpose(2, 0, 1, 3))
    grad_router = jnp.einsum("rd,re->de", normed_two, logit_grads, preferred_element_type=jnp.float32)
    normed_two_grad = jnp.einsum("re,de->rd", logit_grads, w_router, preferred_element_type=jnp.float32)
    out_cot = out_grad.astype(jnp.float32)
    normed_two_grad = normed_two_grad + expert_grad
    hidden_grad, gain_two_grad = norm_backward(hidden_one, scale_two, norm2_gain, normed_two_grad)
    hidden_grad = hidden_grad + out_cot
    branch_cot = hidden_grad.astype(jnp.bfloat16)
    grad_out = jnp.einsum("rd,rh->dh", branch_cot, attended_low, preferred_element_type=jnp.float32)
    early = sum_over_tokens(
        jnp.concatenate([grad_out, grad_router, gain_two_grad[:, None]], axis=1).astype(jnp.bfloat16)
    )
    attended_grad = jnp.einsum(
        "rd,hd->rh", branch_cot, w_out, preferred_element_type=jnp.float32
    ).astype(jnp.bfloat16)
    grad_heads = attended_grad.reshape(tok_rows, kv_local, groups, head_size).transpose(1, 0, 2, 3)

    def head_backward(operands):
        q_head, k_head, v_head, d_head, o_head, lse_head = operands
        scores = (
            jnp.einsum("qgd,kd->gqk", q_head, k_head, preferred_element_type=jnp.float32)
            * score_scale
        )
        scores = jnp.where(key_mask[None], scores, MASKED)
        attention_probs = jnp.exp(scores - lse_head[:, :, None])
        probs_low = attention_probs.astype(jnp.bfloat16)
        value_part = jnp.einsum(
            "gqk,qgd->kd", probs_low, d_head, preferred_element_type=jnp.float32
        )
        probs_grad = jnp.einsum("qgd,kd->gqk", d_head, v_head, preferred_element_type=jnp.float32)
        delta_rows = jnp.sum(d_head.astype(jnp.float32) * o_head, axis=2).transpose(1, 0)
        scores_grad = (attention_probs * (probs_grad - delta_rows[:, :, None])).astype(jnp.bfloat16)
        query_part = (
            jnp.einsum("gqk,kd->qgd", scores_grad, k_head, preferred_element_type=jnp.float32)
            * score_scale
        )
        key_part = (
            jnp.einsum("gqk,qgd->kd", scores_grad, q_head, preferred_element_type=jnp.float32)
            * score_scale
        )
        return (query_part, key_part, value_part)

    query_grads, key_grads_all, value_grads_all = lax.map(
        head_backward, (query_heads, key_heads, value_heads, grad_heads, attended_heads, log_totals)
    )
    key_grad_rows = key_grads_all.transpose(1, 0, 2).reshape(seq_length, kv_local * head_size)
    value_grad_rows = value_grads_all.transpose(1, 0, 2).reshape(seq_length, kv_local * head_size)
    kv_grad = jnp.concatenate([key_grad_rows, value_grad_rows], axis=1).astype(jnp.bfloat16).reshape(expert_devices, tok_rows, -1)
    kv_sum = lax.dynamic_index_in_dim(kv_grad, place, 0, keepdims=False).astype(jnp.float32)
    for k in range(1, expert_devices):
        piece = lax.dynamic_index_in_dim(kv_grad, (place + k) % expert_devices, 0, keepdims=False)
        kv_sum = kv_sum + deliver(piece, k).astype(jnp.float32)
    key_grad_own, value_grad_own = kv_sum[:, : kv_local * head_size], kv_sum[:, kv_local * head_size :]
    query_grad = (
        rotate(
            query_grads.transpose(1, 0, 2, 3).reshape(tok_rows, query_local, head_size),
            positions,
            -1.0,
        )
        .astype(jnp.bfloat16)
        .reshape(tok_rows, query_local * head_size)
    )
    key_grad = (
        rotate(key_grad_own.reshape(tok_rows, kv_local, head_size), positions, -1.0)
        .astype(jnp.bfloat16)
        .reshape(tok_rows, kv_local * head_size)
    )
    value_grad = value_grad_own.astype(jnp.bfloat16)
    grad_query = jnp.einsum("rd,rh->dh", normed_one, query_grad, preferred_element_type=jnp.float32)
    grad_key = jnp.einsum("rd,rh->dh", normed_one, key_grad, preferred_element_type=jnp.float32)
    grad_value = jnp.einsum("rd,rh->dh", normed_one, value_grad, preferred_element_type=jnp.float32)
    normed_one_partial = jnp.einsum(
        "rh,dh->rd", query_grad, w_query, preferred_element_type=jnp.float32
    )
    normed_one_partial = normed_one_partial + jnp.einsum(
        "rh,dh->rd", key_grad, w_key, preferred_element_type=jnp.float32
    )
    normed_one_partial = normed_one_partial + jnp.einsum(
        "rh,dh->rd", value_grad, w_value, preferred_element_type=jnp.float32
    )
    partial_low = normed_one_partial.astype(jnp.bfloat16)
    normed_one_grad = partial_low.astype(jnp.float32) + swap(partial_low, "tensor").astype(jnp.float32)
    input_part, gain_one_grad = norm_backward(inputs, scale_one, norm1_gain, normed_one_grad)
    input_grad = hidden_grad + input_part
    late_query = sum_over_tokens(grad_query.astype(jnp.bfloat16))
    late = sum_over_tokens(
        jnp.concatenate([grad_key, grad_value, gain_one_grad[:, None]], axis=1).astype(jnp.bfloat16)
    )
    kv_width = kv_local * head_size
    q_width = query_local * head_size
    return (
        block_out,
        input_grad,
        late[:, 2 * kv_width],
        late_query,
        late[:, :kv_width],
        late[:, kv_width : 2 * kv_width],
        early[:, :q_width].T,
        early[:, q_width + total_experts],
        early[:, q_width : q_width + total_experts],
        grad_gate,
        grad_up,
        grad_down,
    )


def solution(mesh):
    return jax.shard_map(
        body,
        mesh=mesh,
        in_specs=(
            P(("dp", "expert"), None),
            P("dp"),
            P(("dp", "expert"), None),
            P(("dp", "expert"), None),
            P(),
            P(None, "tensor"),
            P(None, "tensor"),
            P(None, "tensor"),
            P("tensor", None),
            P(),
            P(),
            P("expert", None, "tensor"),
            P("expert", None, "tensor"),
            P("expert", "tensor", None),
        ),
        out_specs=(
            P(("dp", "expert"), "tensor"),
            P(("dp", "expert"), None),
            P(("dp", "expert")),
            P(("dp", "expert"), "tensor"),
            P(("dp", "expert"), "tensor"),
            P(("dp", "expert"), "tensor"),
            P("tensor", ("dp", "expert")),
            P(("dp", "expert")),
            P(("dp", "expert"), None),
            P("expert", "dp", "tensor"),
            P("expert", "dp", "tensor"),
            P("expert", "tensor", "dp"),
        ),
        check_vma=False,
    )
```

```python
import functools

import jax
import jax.numpy as jnp
import numpy as np
from jax import lax
from jax.experimental import pallas as pl
from jax.experimental.pallas import tpu as pltpu
from jax.sharding import PartitionSpec as P

HEAD_DIM = 64
EPSILON = 1e-05
ROPE_BASE = 10000.0
MASKED = -1e30
BF = jnp.bfloat16
F32 = jnp.float32
MIB = 1024 * 1024


def swap(values, axis, bit=1):
    count = lax.axis_size(axis)
    return lax.ppermute(values, axis, [(i, i ^ bit) for i in range(count)])


def fetch(values, offset):
    count = lax.axis_size("expert")
    return lax.ppermute(values, "expert", [(i, (i - offset) % count) for i in range(count)])


def deliver(values, offset):
    count = lax.axis_size("expert")
    return lax.ppermute(values, "expert", [(i, (i + offset) % count) for i in range(count)])


def gather_blocks(rows, side):
    half = rows.shape[0] // 2
    own = lax.dynamic_slice_in_dim(rows, side * half, half)
    other = lax.dynamic_slice_in_dim(rows, (1 - side) * half, half)
    blocks = [(own, other)]
    for offset in range(1, lax.axis_size("expert")):
        far = fetch(own, offset)
        blocks.append((far, swap(far, "tensor")))
    return jnp.stack([jnp.concatenate(pair, axis=0) for pair in blocks])


def reduce_blocks(partial):
    blocks, rows, width = partial.shape
    half = rows // 2
    total = None
    for offset in range(blocks - 1, -1, -1):
        mine = partial[offset, :half].astype(F32)
        got = swap(partial[offset, half:], "tensor").astype(F32)
        piece = mine + got
        if offset:
            piece = deliver(piece.astype(BF), offset).astype(F32)
        total = piece if total is None else total + piece
    return total


def halve(parts, bit_axis, bit):
    pairs = parts.reshape((parts.shape[0] // 2, 2) + parts.shape[1:])
    own = (lax.axis_index(bit_axis) // bit) % 2
    keep = lax.dynamic_index_in_dim(pairs, own, 1, keepdims=False)
    send = lax.dynamic_index_in_dim(pairs, 1 - own, 1, keepdims=False)
    got = swap(send, bit_axis, bit)
    return keep.astype(F32) + got.astype(F32)


def sum_over_dp(parts):
    bit = 1
    while parts.shape[0] > 1:
        parts = halve(parts.astype(BF), "dp", bit)
        bit *= 2
    return parts[0]


def sum_places(keep, send):
    bit = 1
    total = keep.astype(F32) + swap(send, "dp", bit).astype(F32)
    while total.shape[0] > 1:
        bit *= 2
        pairs = total.reshape((total.shape[0] // 2, 2) + total.shape[1:])
        total = pairs[:, 0] + swap(pairs[:, 1].astype(BF), "dp", bit).astype(F32)
    return total[0]


def sum_over_tokens(rows):
    n_exp = lax.axis_size("expert")
    width = rows.shape[1]
    parts = rows.reshape(lax.axis_size("dp"), -1, width)
    parts = halve(parts, "dp", 1).astype(BF)
    parts = parts.reshape(parts.shape[0], n_exp, -1, width)
    place = lax.axis_index("expert")
    total = lax.dynamic_index_in_dim(parts, place, 1, keepdims=False).astype(F32)
    for offset in range(1, n_exp):
        piece = lax.dynamic_index_in_dim(parts, (place + offset) % n_exp, 1, keepdims=False)
        total = total + deliver(piece, offset).astype(F32)
    bit = 2
    while total.shape[0] > 1:
        total = halve(total.astype(BF), "dp", bit)
        bit *= 2
    return total[0]


def nn(left, right):
    return jnp.dot(left, right, preferred_element_type=F32)


def nt(left, right):
    return lax.dot_general(left, right, (((1,), (1,)), ((), ())), preferred_element_type=F32)


def tn(left, right):
    return lax.dot_general(left, right, (((0,), (0,)), ((), ())), preferred_element_type=F32)


def params(mib):
    return pltpu.CompilerParams(vmem_limit_bytes=mib * MIB)


def full(shape):
    return pl.BlockSpec(shape, lambda *_: (0,) * len(shape))


def turned(values, cosine, sine):
    lane = lax.broadcasted_iota(jnp.int32, values.shape, 1)
    quarter = HEAD_DIM // 2
    later = pltpu.roll(values, 2 * HEAD_DIM - quarter, 1)
    earlier = pltpu.roll(values, quarter, 1)
    return values * cosine + jnp.where(lane % HEAD_DIM < quarter, later, earlier) * sine


def project_kernel(x_ref, gain_ref, wq_ref, wk_ref, wv_ref, cos_ref, sin_ref, n_ref, q_ref, kv_ref, s_ref):
    values = x_ref[...].astype(F32)
    scale = lax.rsqrt(jnp.mean(values * values, axis=1, keepdims=True) + EPSILON)
    s_ref[...] = scale
    normed = (values * scale * gain_ref[...]).astype(BF)
    n_ref[...] = normed
    cosine, sine = cos_ref[...], sin_ref[...]
    lanes = 2 * HEAD_DIM
    kv = wk_ref.shape[1]
    keys = nn(normed, wk_ref[...])
    for i in range(0, kv, lanes):
        kv_ref[:, i : i + lanes] = turned(keys[:, i : i + lanes], cosine, sine).astype(BF)
    kv_ref[:, kv:] = nn(normed, wv_ref[...]).astype(BF)
    query = nn(normed, wq_ref[...])
    for i in range(0, query.shape[1], lanes):
        q_ref[:, i : i + lanes] = turned(query[:, i : i + lanes], cosine, sine).astype(BF)


def attend_kernel(groups, q_ref, k_ref, v_ref, bias_ref, o_ref, lse_ref):
    h = HEAD_DIM
    rows = q_ref.shape[0]
    for kv in range(k_ref.shape[1] // h):
        key = k_ref[:, kv * h : kv * h + h]
        value = v_ref[:, kv * h : kv * h + h]
        for g in range(groups):
            head = kv * groups + g
            query = q_ref[:, head * h : head * h + h]
            scores = nt(query, key) * h**-0.5 + bias_ref[...]
            peak = jnp.max(scores, axis=1, keepdims=True)
            raw = jnp.exp(scores - peak)
            total = jnp.sum(raw, axis=1, keepdims=True)
            probs = (raw * (1.0 / total)).astype(BF)
            o_ref[:, head * h : head * h + h] = nn(probs, value)
            lse_ref[0, :, head : head + 1] = peak + jnp.log(total)


def attend_grad_kernel(groups, q_ref, k_ref, v_ref, d_ref, o_ref, lse_ref, bias_ref, dq_ref, dk_ref, dv_ref):
    h = HEAD_DIM
    for kv in range(k_ref.shape[1] // h):
        key = k_ref[:, kv * h : kv * h + h]
        value = v_ref[:, kv * h : kv * h + h]
        key_grad = value_grad = None
        for g in range(groups):
            head = kv * groups + g
            span = slice(head * h, head * h + h)
            query = q_ref[:, span]
            cot = d_ref[:, span]
            scores = nt(query, key) * h**-0.5 + bias_ref[...]
            probs = jnp.exp(scores - lse_ref[0, :, head : head + 1])
            delta = jnp.sum(cot.astype(F32) * o_ref[:, span], axis=1, keepdims=True)
            slope = (probs * (nt(cot, value) - delta)).astype(BF)
            value_part = tn(cot, probs.astype(BF))
            key_part = tn(query, slope)
            dq_ref[:, span] = nn(slope, key) * h**-0.5
            value_grad = value_part if value_grad is None else value_grad + value_part
            key_grad = key_part if key_grad is None else key_grad + key_part
        dk_ref[kv * h : kv * h + h, :] = (key_grad * h**-0.5).astype(BF)
        dv_ref[kv * h : kv * h + h, :] = value_grad.astype(BF)


def cotangent_kernel(pick_ref, cot_ref, wd_ref, cg_ref, dm_ref):
    blocks, _, slots, _ = pick_ref.shape
    for k in range(blocks):
        cg_ref[0, k * slots : (k + 1) * slots, :] = nn(pick_ref[k, 0], cot_ref[k]).astype(BF)
    dm_ref[0] = nt(cg_ref[0], wd_ref[0])


def experts_kernel(
    place_ref, x_ref, hot_ref, router_ref, pick_ref, spread_ref, dm_ref, wg_ref, wu_ref,
    xg_ref, gm_ref, da_ref, db_ref, dg_ref, dn_ref, gates_ref, n_ref,
):
    blocks, _, slots, rows = pick_ref.shape
    step, steps = pl.program_id(0), pl.num_programs(0)

    @pl.when(step == 0)
    def _():
        tokens = x_ref[...].reshape(blocks * rows, x_ref.shape[2])
        hot = hot_ref[...] > 0.0
        logits = jnp.where(hot, nt(router_ref[...], tokens), MASKED)
        raw = jnp.where(hot, jnp.exp(logits - jnp.max(logits, axis=0, keepdims=True)), 0.0)
        gates_ref[...] = raw / jnp.sum(raw, axis=0, keepdims=True)

    gate_row = gates_ref[pl.ds(place_ref[0] * steps + step, 1), :]
    gate_parts = []
    for k in range(blocks):
        pick = pick_ref[k, 0]
        xg_ref[0, k * slots : (k + 1) * slots, :] = nn(pick, x_ref[k]).astype(BF)
        gate_parts.append(
            jnp.sum(pick.astype(F32) * gate_row[:, k * rows : (k + 1) * rows], axis=1, keepdims=True)
        )
    gates = jnp.concatenate(gate_parts, axis=0)
    own = xg_ref[0]
    gate_pre = nn(own, wg_ref[0])
    up_pre = nn(own, wu_ref[0])
    raw_grad = dm_ref[0]
    sigmoid = 1.0 / (1.0 + jnp.exp(-gate_pre))
    swish = gate_pre * sigmoid
    active = swish * up_pre
    dgate = jnp.sum(active * raw_grad, axis=1, keepdims=True)
    gm_ref[0] = (gates * active).astype(BF)
    grad = gates * raw_grad
    da = (grad * up_pre * sigmoid * (1.0 + gate_pre * (1.0 - sigmoid))).astype(BF)
    db = (grad * swish).astype(BF)
    da_ref[0] = da
    db_ref[0] = db
    low = (nt(da, wg_ref[0]) + nt(db, wu_ref[0])).astype(BF)
    at = pl.multiple_of(step * slots, slots)
    for k in range(blocks):
        part = slice(k * slots, (k + 1) * slots)
        n_ref[k, pl.ds(at, slots), :] = low[part]
        dg_ref[0, k : k + 1, :] = jnp.sum(pick_ref[k, 0].astype(F32) * dgate[part], axis=0, keepdims=True)

    @pl.when(step == steps - 1)
    def _():
        for k in range(blocks):
            dn_ref[k] = nn(spread_ref[k], n_ref[k]).astype(BF)


def weights_kernel(own_ref, xg_ref, cg_ref, gm_ref, da_ref, db_ref, gu_keep, gu_send, d_keep, d_send):
    count = 2 * gu_keep.shape[0]
    width = xg_ref.shape[2] // count
    da, db, gm = da_ref[0], db_ref[0], gm_ref[0]
    for number in range(count):
        gu, down = (gu_send, d_send) if number % 2 else (gu_keep, d_keep)
        at = pl.multiple_of((own_ref[0] ^ number) * width, 128)
        rows = xg_ref[0, :, pl.ds(at, width)]
        gu[number // 2, 0, 0] = tn(rows, da).astype(BF)
        gu[number // 2, 0, 1] = tn(rows, db).astype(BF)
        down[number // 2, 0] = tn(gm, cg_ref[0, :, pl.ds(at, width)]).astype(BF)


def combine_kernel(gm_ref, wd_ref, spread_ref, out_ref, r_ref):
    blocks = out_ref.shape[0]
    slots = gm_ref.shape[1] // blocks
    step, steps = pl.program_id(0), pl.num_programs(0)
    low = nn(gm_ref[0], wd_ref[0]).astype(BF)
    at = pl.multiple_of(step * slots, slots)
    for k in range(blocks):
        r_ref[k, pl.ds(at, slots), :] = low[k * slots : (k + 1) * slots]

    @pl.when(step == steps - 1)
    def _():
        for k in range(blocks):
            out_ref[k] = nn(spread_ref[k], r_ref[k]).astype(BF)


def norm_forward(values, gain):
    norm_scale = lax.rsqrt(jnp.mean(values * values, axis=1, keepdims=True) + EPSILON)
    return (norm_scale, values * norm_scale * gain)


def norm_backward(values, norm_scale, gain, grad_normed):
    weighted = grad_normed * gain
    inner = jnp.mean(weighted * values, axis=1, keepdims=True)
    grad_values = norm_scale * weighted - values * (norm_scale * norm_scale * norm_scale) * inner
    grad_gain = jnp.sum(grad_normed * values * norm_scale, axis=0)
    return (grad_values, grad_gain)


def rotary_tables(length):
    half = HEAD_DIM // 2
    inverse = ROPE_BASE ** (-2.0 * np.arange(half) / HEAD_DIM)
    angles = np.arange(length)[:, None] * inverse[None, :]
    cosine, sine = np.cos(angles), np.sin(angles)
    return (
        np.concatenate([cosine, cosine, cosine, cosine], axis=1).astype(np.float32),
        np.concatenate([-sine, sine, -sine, sine], axis=1).astype(np.float32),
    )


def body(
    x_in,
    segments,
    chosen,
    out_grad,
    norm1_gain,
    w_query,
    w_key,
    w_value,
    w_out,
    norm2_gain,
    w_router,
    w_gate,
    w_up,
    w_down,
):
    tok_rows, full_width = x_in.shape
    h = HEAD_DIM
    q_width, kv_width = w_query.shape[1], w_key.shape[1]
    groups = q_width // kv_width
    experts_local, _, inner = w_gate.shape
    n_exp, n_dp = lax.axis_size("expert"), lax.axis_size("dp")
    total_experts = experts_local * n_exp
    top_count = chosen.shape[1]
    capacity = tok_rows * top_count * 25 // (16 * total_experts)
    place, side = lax.axis_index("expert"), lax.axis_index("tensor")
    half_width = full_width // lax.axis_size("tensor")
    row_start = place * tok_rows
    seq_length = segments.shape[0]
    half_rows = tok_rows // 2

    tables = [
        lax.dynamic_slice_in_dim(jnp.asarray(table), row_start, tok_rows)
        for table in rotary_tables(seq_length)
    ]
    cosine, sine = tables
    normed_one, query_rot, kv_own, scale_one = pl.pallas_call(
        project_kernel,
        name="project",
        out_shape=(
            jax.ShapeDtypeStruct((tok_rows, full_width), BF),
            jax.ShapeDtypeStruct((tok_rows, q_width), BF),
            jax.ShapeDtypeStruct((tok_rows, 2 * kv_width), BF),
            jax.ShapeDtypeStruct((tok_rows, 1), F32),
        ),
        compiler_params=params(32),
    )(x_in, norm1_gain[None], w_query, w_key, w_value, cosine, sine)
    kv_stack = jnp.stack([kv_own] + [fetch(kv_own, k) for k in range(1, n_exp)])
    order = (jnp.arange(n_exp) - place) % n_exp
    kv_all = jnp.take(kv_stack, order, axis=0).reshape(seq_length, -1)

    cot_in, chosen_in, kv_all = lax.optimization_barrier((out_grad, chosen, kv_all))
    cot_blocks = gather_blocks(cot_in, side)
    chosen_flip = jnp.where(side == 0, chosen_in, jnp.roll(chosen_in, half_rows, axis=0)).T
    chosen_blocks = jnp.stack([chosen_flip] + [fetch(chosen_flip, k) for k in range(1, n_exp)])
    expert_ids = jnp.arange(total_experts, dtype=jnp.int32)
    hot_all = jnp.any(chosen_blocks[:, :, None, :] == expert_ids[:, None], axis=1)
    hot_rows = hot_all.transpose(1, 0, 2).reshape(total_experts, n_exp * tok_rows).astype(F32)
    hot_local = lax.dynamic_slice_in_dim(hot_all, place * experts_local, experts_local, 1)
    token_row = jnp.arange(tok_rows, dtype=jnp.int32)
    before = (token_row[:, None] < token_row[None, :]).astype(BF)
    rank = jnp.einsum("kes,st->ket", hot_local.astype(BF), before, preferred_element_type=F32)
    slot_of = jnp.where(hot_local, rank.astype(jnp.int32), -1)
    slots = jnp.arange(capacity, dtype=jnp.int32)
    pick = (slot_of[:, :, None, :] == slots[:, None]).astype(BF)
    spread = pick.reshape(n_exp, experts_local * capacity, tok_rows).transpose(0, 2, 1)
    expert_slots = n_exp * capacity

    by_expert = lambda *tail: pl.BlockSpec((1,) + tail, lambda e, *_: (e,) + (0,) * len(tail))
    pick_spec = pl.BlockSpec((n_exp, 1, capacity, tok_rows), lambda e, *_: (0, e, 0, 0))
    blocks_shape = (n_exp, tok_rows, full_width)
    slots_shape = (n_exp, experts_local * capacity, full_width)
    cot_slots, raw_grad = pl.pallas_call(
        cotangent_kernel,
        name="cotangent",
        grid=(experts_local,),
        in_specs=[pick_spec, full(blocks_shape), by_expert(inner, full_width)],
        out_specs=(by_expert(expert_slots, full_width), by_expert(expert_slots, inner)),
        out_shape=(
            jax.ShapeDtypeStruct((experts_local, expert_slots, full_width), BF),
            jax.ShapeDtypeStruct((experts_local, expert_slots, inner), F32),
        ),
        compiler_params=params(40),
    )(pick, cot_blocks, w_down)

    positions = row_start + jnp.arange(tok_rows, dtype=jnp.int32)
    query_segments = lax.dynamic_slice_in_dim(segments, row_start, tok_rows)
    allowed = (query_segments[:, None] == segments[None, :]) & (
        positions[:, None] >= jnp.arange(seq_length, dtype=jnp.int32)[None, :]
    )
    bias = jnp.where(allowed, 0.0, MASKED).astype(F32)
    pair = 2 * h
    columns = lambda n: pl.BlockSpec((tok_rows, n), lambda i: (0, i))
    key_spec = pl.BlockSpec((seq_length, pair), lambda i: (0, i))
    value_spec = pl.BlockSpec((seq_length, pair), lambda i: (0, kv_width // pair + i))
    lse_spec = pl.BlockSpec((1, tok_rows, 2 * groups), lambda i: (i, 0, 0))
    steps = kv_width // pair
    attended, log_totals = pl.pallas_call(
        functools.partial(attend_kernel, groups),
        name="attend",
        grid=(steps,),
        in_specs=[columns(pair * groups), key_spec, value_spec, full((tok_rows, seq_length))],
        out_specs=(columns(pair * groups), lse_spec),
        out_shape=(
            jax.ShapeDtypeStruct((tok_rows, q_width), F32),
            jax.ShapeDtypeStruct((steps, tok_rows, 2 * groups), F32),
        ),
        compiler_params=params(32),
    )(query_rot, kv_all, kv_all, bias)
    attended_low = attended.astype(BF)
    head_low = nn(attended_low, w_out).astype(BF)
    inputs = x_in.astype(F32)
    hidden_one = inputs + head_low.astype(F32) + swap(head_low, "tensor").astype(F32)
    scale_two, normed_two = norm_forward(hidden_one, norm2_gain)
    normed_two = normed_two.astype(BF)

    token_blocks = gather_blocks(normed_two, side)
    low_slots = jax.ShapeDtypeStruct((experts_local, expert_slots, inner), BF)
    row_slots, gated, da, db, dgate_part, in_grad_part = pl.pallas_call(
        experts_kernel,
        name="experts",
        grid_spec=pltpu.PrefetchScalarGridSpec(
            num_scalar_prefetch=1,
            grid=(experts_local,),
            in_specs=[
                full(blocks_shape),
                full((total_experts, n_exp * tok_rows)),
                full((total_experts, full_width)),
                pick_spec,
                full((n_exp, tok_rows, experts_local * capacity)),
                by_expert(expert_slots, inner),
                by_expert(full_width, inner),
                by_expert(full_width, inner),
            ],
            out_specs=(
                by_expert(expert_slots, full_width),
                by_expert(expert_slots, inner),
                by_expert(expert_slots, inner),
                by_expert(expert_slots, inner),
                by_expert(n_exp, tok_rows),
                full(blocks_shape),
            ),
            scratch_shapes=[
                pltpu.VMEM((total_experts, n_exp * tok_rows), F32),
                pltpu.VMEM(slots_shape, BF),
            ],
        ),
        out_shape=(
            jax.ShapeDtypeStruct((experts_local, expert_slots, full_width), BF),
            low_slots,
            low_slots,
            low_slots,
            jax.ShapeDtypeStruct((experts_local, n_exp, tok_rows), F32),
            jax.ShapeDtypeStruct(blocks_shape, BF),
        ),
        compiler_params=params(52),
    )(place[None], token_blocks, hot_rows, w_router.T, pick, spread, raw_grad, w_gate, w_up)

    dgate_part = dgate_part.transpose(1, 0, 2)
    dgate_own = dgate_part + jnp.roll(swap(dgate_part, "tensor"), half_rows, axis=2)
    dgate_stack = jnp.stack([dgate_own[0]] + [deliver(dgate_own[k], k) for k in range(1, n_exp)])
    dgate = jnp.take(dgate_stack, (place - jnp.arange(n_exp)) % n_exp, axis=0)
    dgate = dgate.reshape(total_experts, tok_rows)
    dgate = jnp.where(side == 0, dgate, jnp.roll(dgate, half_rows, axis=1)).T
    hot_own = jnp.any(chosen[:, :, None] == expert_ids, axis=1)
    logits = jnp.where(hot_own, nn(normed_two, w_router), MASKED)
    raw = jnp.where(hot_own, jnp.exp(logits - jnp.max(logits, axis=-1, keepdims=True)), 0.0)
    gates_own = raw / jnp.sum(raw, axis=-1, keepdims=True)
    logit_grads = (
        gates_own * (dgate - jnp.sum(gates_own * dgate, axis=1, keepdims=True))
    ).astype(BF)
    half_sum = reduce_blocks(in_grad_part).astype(BF)
    half_other = swap(half_sum, "tensor")
    expert_grad = jnp.where(
        side == 0,
        jnp.concatenate([half_sum, half_other], axis=0),
        jnp.concatenate([half_other, half_sum], axis=0),
    ).astype(F32)

    slice_width = full_width // n_dp
    if slice_width % 128 == 0:
        expert_parts = []
        step_experts = experts_local // 2
        for first in (0, step_experts):
            count = step_experts if first == 0 else experts_local - step_experts
            some = lambda *tail: pl.BlockSpec(
                (1,) + tail, lambda e, *_: (first + e,) + (0,) * len(tail)
            )
            gu_shape = (n_dp // 2, count, 2, slice_width, inner)
            d_shape = (n_dp // 2, count, inner, slice_width)
            gu_spec = pl.BlockSpec((n_dp // 2, 1) + gu_shape[2:], lambda e, *_: (0, e, 0, 0, 0))
            d_spec = pl.BlockSpec((n_dp // 2, 1) + d_shape[2:], lambda e, *_: (0, e, 0, 0))
            gu_keep, gu_send, d_keep, d_send = pl.pallas_call(
                weights_kernel,
                name="weights",
                grid_spec=pltpu.PrefetchScalarGridSpec(
                    num_scalar_prefetch=1,
                    grid=(count,),
                    in_specs=[
                        some(expert_slots, full_width),
                        some(expert_slots, full_width),
                        some(expert_slots, inner),
                        some(expert_slots, inner),
                        some(expert_slots, inner),
                    ],
                    out_specs=(gu_spec, gu_spec, d_spec, d_spec),
                ),
                out_shape=(
                    jax.ShapeDtypeStruct(gu_shape, BF),
                    jax.ShapeDtypeStruct(gu_shape, BF),
                    jax.ShapeDtypeStruct(d_shape, BF),
                    jax.ShapeDtypeStruct(d_shape, BF),
                ),
                compiler_params=params(40),
            )(lax.axis_index("dp")[None], row_slots, cot_slots, gated, da, db)
            expert_parts.append((sum_places(gu_keep, gu_send), sum_places(d_keep, d_send)))
        gu_sum = jnp.concatenate([part[0] for part in expert_parts], axis=0)
        grad_gate, grad_up = gu_sum[:, 0], gu_sum[:, 1]
        grad_down = jnp.concatenate([part[1] for part in expert_parts], axis=0)
    else:
        sums = lambda spec, a, b: jnp.einsum(spec, a, b, preferred_element_type=F32).astype(BF)
        by_rows = lambda g: g.reshape(experts_local, n_dp, -1, inner).transpose(1, 0, 2, 3)
        grad_gate = sum_over_dp(by_rows(sums("esd,esf->edf", row_slots, da)))
        grad_up = sum_over_dp(by_rows(sums("esd,esf->edf", row_slots, db)))
        grad_down = sums("esf,esd->efd", gated, cot_slots)
        grad_down = sum_over_dp(
            grad_down.reshape(experts_local, inner, n_dp, -1).transpose(2, 0, 1, 3)
        )

    out_part = pl.pallas_call(
        combine_kernel,
        name="combine",
        grid=(experts_local,),
        in_specs=[
            by_expert(expert_slots, inner),
            by_expert(inner, full_width),
            full((n_exp, tok_rows, experts_local * capacity)),
        ],
        out_specs=full(blocks_shape),
        out_shape=jax.ShapeDtypeStruct(blocks_shape, BF),
        scratch_shapes=[pltpu.VMEM(slots_shape, BF)],
        compiler_params=params(40),
    )(gated, w_down, spread)
    out_mine = lax.dynamic_slice_in_dim(out_part, side * half_width, half_width, 2)
    out_else = lax.dynamic_slice_in_dim(out_part, (1 - side) * half_width, half_width, 2)
    out_got = jnp.roll(swap(out_else, "tensor"), half_rows, axis=1)
    out_sum = out_mine.astype(F32) + out_got.astype(F32)
    out_low = out_sum.astype(BF)
    mixture_half = out_sum[0]
    for k in range(1, n_exp):
        mixture_half = mixture_half + deliver(out_low[k], k).astype(F32)
    mixture_half = jnp.where(side == 0, mixture_half, jnp.roll(mixture_half, half_rows, axis=0))
    residual_half = lax.dynamic_slice_in_dim(hidden_one, side * half_width, half_width, 1)
    block_out = (residual_half + mixture_half).astype(BF)

    grad_router = tn(normed_two, logit_grads)
    out_cot = out_grad.astype(F32)
    normed_two_grad = nt(logit_grads, w_router) + expert_grad
    hidden_grad, gain_two_grad = norm_backward(hidden_one, scale_two, norm2_gain, normed_two_grad)
    hidden_grad = hidden_grad + out_cot
    branch_cot = hidden_grad.astype(BF)
    attended_grad = nt(branch_cot, w_out).astype(BF)
    grad_out = tn(branch_cot, attended_low)
    early = sum_over_tokens(
        jnp.concatenate([grad_out, grad_router, gain_two_grad[:, None]], axis=1).astype(BF)
    )

    kv_out = pl.BlockSpec((pair, seq_length), lambda i: (i, 0))
    query_grads, key_grads, value_grads = pl.pallas_call(
        functools.partial(attend_grad_kernel, groups),
        name="attend_grad",
        grid=(steps,),
        in_specs=[
            columns(pair * groups), key_spec, value_spec, columns(pair * groups),
            columns(pair * groups), lse_spec, full((tok_rows, seq_length)),
        ],
        out_specs=(columns(pair * groups), kv_out, kv_out),
        out_shape=(
            jax.ShapeDtypeStruct((tok_rows, q_width), F32),
            jax.ShapeDtypeStruct((kv_width, seq_length), BF),
            jax.ShapeDtypeStruct((kv_width, seq_length), BF),
        ),
        compiler_params=params(32),
    )(query_rot, kv_all, kv_all, attended_grad, attended, log_totals, bias)
    kv_grad = jnp.concatenate([key_grads, value_grads], axis=0)
    block_of = lambda k: lax.dynamic_slice_in_dim(
        kv_grad, ((place + k) % n_exp) * tok_rows, tok_rows, 1
    )
    kv_sum = block_of(0).astype(F32)
    for k in range(1, n_exp):
        kv_sum = kv_sum + deliver(block_of(k), k).astype(F32)
    kv_sum = kv_sum.T

    def turned_back(values):
        wide = values.reshape(tok_rows, -1, 2, h // 2)
        flipped = wide[:, :, ::-1].reshape(tok_rows, -1)
        count = values.shape[1] // (2 * h)
        return values * jnp.tile(cosine, (1, count)) - flipped * jnp.tile(sine, (1, count))

    query_grad = turned_back(query_grads).astype(BF)
    key_grad = turned_back(kv_sum[:, :kv_width]).astype(BF)
    value_grad = kv_sum[:, kv_width:].astype(BF)
    grad_query = tn(normed_one, query_grad)
    grad_key = tn(normed_one, key_grad)
    grad_value = tn(normed_one, value_grad)
    partial_low = (
        nt(query_grad, w_query) + nt(key_grad, w_key) + nt(value_grad, w_value)
    ).astype(BF)
    normed_one_grad = partial_low.astype(F32) + swap(partial_low, "tensor").astype(F32)
    input_part, gain_one_grad = norm_backward(inputs, scale_one, norm1_gain, normed_one_grad)
    input_grad = hidden_grad + input_part
    late_query = sum_over_tokens(grad_query.astype(BF))
    late = sum_over_tokens(
        jnp.concatenate([grad_key, grad_value, gain_one_grad[:, None]], axis=1).astype(BF)
    )
    return (
        block_out,
        input_grad,
        late[:, 2 * kv_width],
        late_query,
        late[:, :kv_width],
        late[:, kv_width : 2 * kv_width],
        early[:, :q_width].T,
        early[:, q_width + total_experts],
        early[:, q_width : q_width + total_experts],
        grad_gate,
        grad_up,
        grad_down,
    )


def solution(mesh):
    return jax.shard_map(
        body,
        mesh=mesh,
        in_specs=(
            P(("dp", "expert"), None),
            P("dp"),
            P(("dp", "expert"), None),
            P(("dp", "expert"), None),
            P(),
            P(None, "tensor"),
            P(None, "tensor"),
            P(None, "tensor"),
            P("tensor", None),
            P(),
            P(),
            P("expert", None, "tensor"),
            P("expert", None, "tensor"),
            P("expert", "tensor", None),
        ),
        out_specs=(
            P(("dp", "expert"), "tensor"),
            P(("dp", "expert"), None),
            P(("dp", "expert")),
            P(("dp", "expert"), "tensor"),
            P(("dp", "expert"), "tensor"),
            P(("dp", "expert"), "tensor"),
            P("tensor", ("dp", "expert")),
            P(("dp", "expert")),
            P(("dp", "expert"), None),
            P("expert", "dp", "tensor"),
            P("expert", "dp", "tensor"),
            P("expert", "tensor", "dp"),
        ),
        check_vma=False,
    )
```

```python
import functools

import jax
import jax.numpy as jnp
import numpy as np
from jax import lax
from jax.experimental import pallas as pl
from jax.experimental.pallas import tpu as pltpu
from jax.sharding import PartitionSpec as P

HEAD_DIM = 64
EPSILON = 1e-05
ROPE_BASE = 10000.0
MASKED = -1e30
BF = jnp.bfloat16
F32 = jnp.float32
MIB = 1024 * 1024


def swap(values, axis, bit=1):
    count = lax.axis_size(axis)
    return lax.ppermute(values, axis, [(i, i ^ bit) for i in range(count)])


def fetch(values, offset):
    count = lax.axis_size("expert")
    return lax.ppermute(values, "expert", [(i, (i - offset) % count) for i in range(count)])


def deliver(values, offset):
    count = lax.axis_size("expert")
    return lax.ppermute(values, "expert", [(i, (i + offset) % count) for i in range(count)])


def halve(parts, bit_axis, bit):
    pairs = parts.reshape((parts.shape[0] // 2, 2) + parts.shape[1:])
    own = (lax.axis_index(bit_axis) // bit) % 2
    keep = lax.dynamic_index_in_dim(pairs, own, 1, keepdims=False)
    send = lax.dynamic_index_in_dim(pairs, 1 - own, 1, keepdims=False)
    got = swap(send, bit_axis, bit)
    return keep.astype(F32) + got.astype(F32)


def sum_over_dp(parts):
    bit = 1
    while parts.shape[0] > 1:
        parts = halve(parts.astype(BF), "dp", bit)
        bit *= 2
    return parts[0]


def exchange(parts):
    return lax.all_to_all(parts, "expert", split_axis=0, concat_axis=0, tiled=True)


def nn(left, right):
    return jnp.dot(left, right, preferred_element_type=F32)


def nt(left, right):
    return lax.dot_general(left, right, (((1,), (1,)), ((), ())), preferred_element_type=F32)


def tn(left, right):
    return lax.dot_general(left, right, (((0,), (0,)), ((), ())), preferred_element_type=F32)


def params(mib):
    return pltpu.CompilerParams(vmem_limit_bytes=mib * MIB)


def cost(micros):
    return pl.CostEstimate(flops=int(micros * 1e3), bytes_accessed=0, transcendentals=0)


def shaped(kind, *dims):
    return jax.ShapeDtypeStruct(dims, kind)


def full(*shape):
    return pl.BlockSpec(shape, lambda *_: (0,) * len(shape))


def after(values, *others):
    return lax.optimization_barrier((values,) + others)[0]


def turned(values, cosine, sine):
    lane = lax.broadcasted_iota(jnp.int32, values.shape, 1)
    quarter = HEAD_DIM // 2
    later = pltpu.roll(values, 2 * HEAD_DIM - quarter, 1)
    earlier = pltpu.roll(values, quarter, 1)
    return values * cosine + jnp.where(lane % HEAD_DIM < quarter, later, earlier) * sine


def project_kernel(x_ref, gain_ref, wq_ref, wk_ref, wv_ref, cos_ref, sin_ref, n_ref, q_ref, kv_ref, s_ref):
    values = x_ref[...].astype(F32)
    scale = lax.rsqrt(jnp.mean(values * values, axis=1, keepdims=True) + EPSILON)
    s_ref[...] = scale
    normed = (values * scale * gain_ref[...]).astype(BF)
    n_ref[...] = normed
    cosine, sine = cos_ref[...], sin_ref[...]
    lanes = 2 * HEAD_DIM
    kv = wk_ref.shape[1]
    keys = nn(normed, wk_ref[...])
    for i in range(0, kv, lanes):
        kv_ref[:, i : i + lanes] = turned(keys[:, i : i + lanes], cosine, sine).astype(BF)
    kv_ref[:, kv:] = nn(normed, wv_ref[...]).astype(BF)
    query = nn(normed, wq_ref[...])
    for i in range(0, query.shape[1], lanes):
        q_ref[:, i : i + lanes] = turned(query[:, i : i + lanes], cosine, sine).astype(BF)


def attend_kernel(groups, blocks, *refs):
    q_ref, kv_refs, bias_ref = refs[0], refs[1 : 1 + blocks], refs[1 + blocks]
    o_ref, low_ref, lse_ref, kv_ref = refs[2 + blocks :]
    h = HEAD_DIM
    rows = kv_refs[0].shape[0]
    for k in range(blocks):
        kv_ref[k * rows : (k + 1) * rows, :] = kv_refs[k][...]
    heads = kv_ref.shape[1] // (2 * h)
    for kv in range(heads):
        key = kv_ref[:, kv * h : kv * h + h]
        value = kv_ref[:, (heads + kv) * h : (heads + kv) * h + h]
        for g in range(groups):
            head = kv * groups + g
            span = slice(head * h, head * h + h)
            scores = nt(q_ref[:, span], key) * h**-0.5 + bias_ref[...]
            peak = jnp.max(scores, axis=1, keepdims=True)
            raw = jnp.exp(scores - peak)
            total = jnp.sum(raw, axis=1, keepdims=True)
            out = nn((raw * (1.0 / total)).astype(BF), value)
            o_ref[:, span] = out
            low_ref[:, span] = out.astype(BF)
            lse_ref[:, head : head + 1] = peak + jnp.log(total)


def attend_grad_kernel(groups, blocks, place_ref, *refs):
    q_ref, kv_refs, d_ref, o_ref, lse_ref, bias_ref = refs[0], refs[1 : 1 + blocks], *refs[1 + blocks : 5 + blocks]
    dq_ref, dkv_ref, kv_ref = refs[5 + blocks :]
    h = HEAD_DIM
    rows = kv_refs[0].shape[0]
    for k in range(blocks):
        kv_ref[k * rows : (k + 1) * rows, :] = kv_refs[k][...]
    heads = kv_ref.shape[1] // (2 * h)
    for kv in range(heads):
        key = kv_ref[:, kv * h : kv * h + h]
        value = kv_ref[:, (heads + kv) * h : (heads + kv) * h + h]
        key_grad = value_grad = None
        for g in range(groups):
            head = kv * groups + g
            span = slice(head * h, head * h + h)
            query = q_ref[:, span]
            cot = d_ref[:, span]
            scores = nt(query, key) * h**-0.5 + bias_ref[...]
            probs = jnp.exp(scores - lse_ref[:, head : head + 1])
            delta = jnp.sum(cot.astype(F32) * o_ref[:, span], axis=1, keepdims=True)
            slope = (probs * (nt(cot, value) - delta)).astype(BF)
            value_part = tn(cot, probs.astype(BF))
            key_part = tn(query, slope)
            dq_ref[:, span] = nn(slope, key) * h**-0.5
            value_grad = value_part if value_grad is None else value_grad + value_part
            key_grad = key_part if key_grad is None else key_grad + key_part
        key_low = (key_grad * h**-0.5).astype(BF)
        value_low = value_grad.astype(BF)
        for k in range(blocks):
            to = lax.rem(place_ref[0] + k, blocks)
            dkv_ref[to, kv * h : kv * h + h, :] = key_low[:, k * rows : (k + 1) * rows]
            dkv_ref[to, (heads + kv) * h : (heads + kv) * h + h, :] = value_low[:, k * rows : (k + 1) * rows]


def middle_kernel(
    side_ref, x_ref, mine_ref, other_ref, w_ref, w_near, w_far, gain_ref, h_ref, s_ref, n_ref, own_ref, far_ref
):
    part = w_near.shape[0]
    hidden = x_ref[...].astype(F32) + nn(mine_ref[...], w_ref[...])
    for w, number in ((w_near, side_ref[1]), (w_far, 1 - side_ref[1])):
        hidden += nn(other_ref[:, pl.ds(pl.multiple_of(number * part, part), part)], w[...])
    h_ref[...] = hidden
    scale = lax.rsqrt(jnp.mean(hidden * hidden, axis=1, keepdims=True) + EPSILON)
    s_ref[...] = scale
    n_ref[...] = (hidden * scale * gain_ref[...]).astype(BF)
    half = own_ref.shape[0]
    own_ref[...] = n_ref[pl.ds(pl.multiple_of(side_ref[0] * half, half), half), :]
    far_ref[...] = n_ref[pl.ds(pl.multiple_of((1 - side_ref[0]) * half, half), half), :]


def make_pick(slot_ref, k, expert, slots):
    row = slot_ref[k, pl.ds(expert, 1), :]
    lines = lax.broadcasted_iota(jnp.int32, (slots, row.shape[1]), 0)
    return jnp.where(lines == row, 1.0, 0.0)


def cotangent_kernel(blocks, slots, *refs):
    slot_ref, halves, wd_ref = refs[0], refs[1 : 1 + 2 * blocks], refs[1 + 2 * blocks]
    cg_ref, dm_ref, x_ref = refs[2 + 2 * blocks :]
    half = x_ref.shape[1] // 2
    step = pl.program_id(0)

    @pl.when(step == 0)
    def _():
        for k in range(blocks):
            x_ref[k, :half, :] = halves[2 * k][:half, :]
            x_ref[k, half:, :] = halves[2 * k + 1][:half, :]

    for k in range(blocks):
        pick = make_pick(slot_ref, k, step, slots).astype(BF)
        cg_ref[0, k * slots : (k + 1) * slots, :] = nn(pick, x_ref[k]).astype(BF)
    dm_ref[0] = nt(cg_ref[0], wd_ref[0])


def split_rows(values):
    line = lax.broadcasted_iota(jnp.int32, (16, values[0].shape[1]), 0)
    out = jnp.zeros(line.shape, F32)
    for i, value in enumerate(values):
        high = value.astype(BF).astype(F32)
        out = jnp.where(line == 2 * i, high, jnp.where(line == 2 * i + 1, value - high, out))
    return out.astype(BF)


def pair_sum_kernel(mine_ref, got_ref, *outs):
    half = mine_ref.shape[1] - 16
    for k, out in enumerate(outs):
        total = mine_ref[k].astype(F32) + got_ref[k].astype(F32)
        out[:half, :] = total[:half].astype(BF)
        out[half:, :] = split_rows([total[half : half + 1] + total[half + 1 : half + 2]])


def gather_sum_kernel(*refs):
    parts, out = refs[:-1], refs[-1]
    half = out.shape[0] - 16
    total = parts[0][...].astype(F32)
    rows = [total[half : half + 1] + total[half + 1 : half + 2]]
    total = total[:half]
    for part in parts[1:]:
        more = part[...].astype(F32)
        total = total + more[:half]
        rows.append(more[half : half + 1] + more[half + 1 : half + 2])
    out[:half, :] = total.astype(BF)
    out[half:, :] = split_rows(rows)


def experts_kernel(blocks, slots, place_ref, slot_ref, *refs):
    halves, (hot_ref, router_ref, dm_ref, wg_ref, wu_ref) = refs[: 2 * blocks], refs[2 * blocks : 5 + 2 * blocks]
    (xg_ref, gm_ref, da_ref, db_ref, mine_ref, else_ref,
     x_ref, gates_ref, n_ref, pick_ref, dg_ref) = refs[5 + 2 * blocks :]
    rows = x_ref.shape[1]
    half = rows // 2
    step, steps = pl.program_id(0), pl.num_programs(0)

    @pl.when(step == 0)
    def _():
        for k in range(blocks):
            x_ref[k, :half, :] = halves[2 * k][...]
            x_ref[k, half:, :] = halves[2 * k + 1][...]
        tokens = x_ref[...].reshape(blocks * rows, x_ref.shape[2])
        hot = hot_ref[...] > 0.0
        logits = jnp.where(hot, nt(router_ref[...], tokens), MASKED)
        raw = jnp.where(hot, jnp.exp(logits - jnp.max(logits, axis=0, keepdims=True)), 0.0)
        gates_ref[...] = raw / jnp.sum(raw, axis=0, keepdims=True)
        dg_ref[...] = jnp.zeros_like(dg_ref)

    gate_row = gates_ref[pl.ds(place_ref[0] * steps + step, 1), :]
    at = pl.multiple_of(step * slots, slots)
    gate_parts, picks = [], []
    for k in range(blocks):
        pick = make_pick(slot_ref, k, step, slots)
        picks.append(pick)
        low = pick.astype(BF)
        pick_ref[k, pl.ds(at, slots), :] = low
        xg_ref[0, k * slots : (k + 1) * slots, :] = nn(low, x_ref[k]).astype(BF)
        gate_parts.append(jnp.sum(pick * gate_row[:, k * rows : (k + 1) * rows], axis=1, keepdims=True))
    gates = jnp.concatenate(gate_parts, axis=0)
    own = xg_ref[0]
    gate_pre = nn(own, wg_ref[0])
    up_pre = nn(own, wu_ref[0])
    raw_grad = dm_ref[0]
    sigmoid = 1.0 / (1.0 + jnp.exp(-gate_pre))
    swish = gate_pre * sigmoid
    active = swish * up_pre
    dgate = jnp.sum(active * raw_grad, axis=1, keepdims=True)
    gm_ref[0] = (gates * active).astype(BF)
    grad = gates * raw_grad
    da = (grad * up_pre * sigmoid * (1.0 + gate_pre * (1.0 - sigmoid))).astype(BF)
    db = (grad * swish).astype(BF)
    da_ref[0] = da
    db_ref[0] = db
    low = (nt(da, wg_ref[0]) + nt(db, wu_ref[0])).astype(BF)
    for k in range(blocks):
        part = slice(k * slots, (k + 1) * slots)
        n_ref[k, pl.ds(at, slots), :] = low[part]
        dg_row = jnp.sum(picks[k] * dgate[part], axis=0, keepdims=True)
        lanes = pl.ds(pl.multiple_of(step * half, half), half)
        dg_ref[2 * k : 2 * k + 1, lanes] = dg_row[:, :half]
        dg_ref[2 * k + 1 : 2 * k + 2, lanes] = dg_row[:, half:]

    @pl.when(step == steps - 1)
    def _():
        for k in range(blocks):
            out = tn(pick_ref[k], n_ref[k]).astype(BF)
            mine_ref[k, :half, :] = out[:half]
            else_ref[k, :half, :] = out[half:]
            mine_ref[k, half:, :] = split_rows([dg_ref[2 * k : 2 * k + 1, :]])
            else_ref[k, half:, :] = split_rows([dg_ref[2 * k + 1 : 2 * k + 2, :]])


def weights_kernel(cg_ref, *refs):
    pairs, out_ref = refs[:8], refs[8]
    count, width = out_ref.shape[0], out_ref.shape[3]
    split = pairs[0].shape[1]
    for number in range(count):
        span = slice(number * width, (number + 1) * width)
        gate = up = down = None
        for i in range(2):
            xg_ref, gm_ref, da_ref, db_ref = pairs[4 * i : 4 * i + 4]
            rows = xg_ref[0, :, span]
            cots = cg_ref[0, i * split : (i + 1) * split, span]
            parts = tn(rows, da_ref[0]), tn(rows, db_ref[0]), tn(cots, gm_ref[0])
            gate, up, down = parts if i == 0 else (gate + parts[0], up + parts[1], down + parts[2])
        out_ref[number, 0, 0] = gate.astype(BF)
        out_ref[number, 0, 1] = up.astype(BF)
        out_ref[number, 0, 2] = down.astype(BF)


def finish_kernel(sum_ref, gate_ref, up_ref, down_ref):
    total = sum_ref[0].astype(F32)
    gate_ref[0] = total[0]
    up_ref[0] = total[1]
    down_ref[0] = total[2].T


def combine_kernel(slots, offsets, where_ref, slot_ref, ga_ref, gb_ref, wd_ref, mine_ref, else_ref, r_ref, pick_ref):
    blocks = mine_ref.shape[0]
    group = blocks // 2
    step, steps = pl.program_id(0), pl.num_programs(0)
    at = pl.multiple_of(step * slots, slots)
    for i, ref in enumerate((ga_ref, gb_ref)):
        low = nn(ref[0], wd_ref[0]).astype(BF)
        for j in range(group):
            k = i * group + j
            r_ref[k, pl.ds(at, slots), :] = low[j * slots : (j + 1) * slots]
            pick_ref[k, pl.ds(at, slots), :] = make_pick(slot_ref, k, step, slots).astype(BF)

    @pl.when(step == steps - 1)
    def _():
        width = mine_ref.shape[2]
        half = mine_ref.shape[1] // 2
        own = pl.ds(pl.multiple_of(where_ref[0] * width, width), width)
        far = pl.ds(pl.multiple_of((1 - where_ref[0]) * width, width), width)
        for k in range(blocks):
            to = lax.rem(where_ref[1] + offsets[k], blocks)
            mine_ref[to] = tn(pick_ref[k], r_ref[k, :, own]).astype(BF)
            out = tn(pick_ref[k], r_ref[k, :, far]).astype(BF)
            else_ref[to, :half] = out[half:]
            else_ref[to, half:] = out[:half]


def norm_grad_kernel(
    local, where_ref, own_ref, far_ref, n_ref, chosen_ref, router_ref, h_ref, s_ref, gain_ref, c_ref, w_ref,
    grad_ref, low_ref, term_ref, do_ref, dl_ref, e_ref, g_ref,
):
    side, place = where_ref[0], where_ref[1]
    half = own_ref.shape[0] - 16
    lanes = router_ref.shape[1]
    sources = 4
    g_ref[...] = jnp.zeros_like(g_ref)
    for part, ref in ((side, own_ref), (1 - side, far_ref)):
        e_ref[pl.ds(pl.multiple_of(part * half, half), half), :] = ref[:half, :]
        tail = ref[half:, :].astype(F32)
        for k in range(sources):
            row = tail[2 * k : 2 * k + 1] + tail[2 * k + 1 : 2 * k + 2]
            source = lax.rem(place + sources - k, sources)
            for e in range(local):
                g_ref[part, pl.ds(source * local + e, 1), :] = row[:, e * half : (e + 1) * half]
    dgate = jnp.concatenate([g_ref[0].T, g_ref[1].T], axis=0)
    lane = lax.broadcasted_iota(jnp.int32, dgate.shape, 1)
    hot = chosen_ref[:, 0:1] == lane
    for i in range(1, chosen_ref.shape[1]):
        hot = hot | (chosen_ref[:, i : i + 1] == lane)
    logits = jnp.where(hot, nn(n_ref[...], router_ref[...]), MASKED)
    raw = jnp.where(hot, jnp.exp(logits - jnp.max(logits, axis=1, keepdims=True)), 0.0)
    gates = raw / jnp.sum(raw, axis=1, keepdims=True)
    logit_grads = (gates * (dgate - jnp.sum(gates * dgate, axis=1, keepdims=True))).astype(BF)
    dl_ref[...] = logit_grads
    grad = nt(logit_grads, router_ref[...]) + e_ref[...].astype(F32)
    hidden, scale = h_ref[...], s_ref[...]
    term_ref[...] = (grad * hidden * scale).astype(BF)
    weighted = grad * gain_ref[...]
    inner = jnp.mean(weighted * hidden, axis=1, keepdims=True)
    total = scale * weighted - hidden * (scale * scale * scale) * inner + c_ref[...].astype(F32)
    grad_ref[...] = total
    low = total.astype(BF)
    low_ref[...] = low
    do_ref[...] = nt(low, w_ref[...]).astype(BF)


def place_slices(own, scratch, keep_ref, send_ref):
    blocks, pairs, rows, _ = keep_ref.shape
    for a in range(2 * pairs):
        out = send_ref if a % 2 else keep_ref
        for b in range(blocks):
            number = (own ^ a) * blocks + b
            out[b, a // 2] = scratch[pl.ds(pl.multiple_of(number * rows, 8), rows), :].astype(BF)


def early_kernel(where_ref, low_ref, o_ref, n_ref, dl_ref, term_ref, keep_ref, send_ref, scratch):
    width = o_ref.shape[1]
    scratch[:, :width] = tn(low_ref[...], o_ref[...])
    lane = lax.broadcasted_iota(jnp.int32, dl_ref.shape, 1)
    ones = jnp.where(lane == dl_ref.shape[1] - 1, 1.0, 0.0).astype(BF)
    scratch[:, width:] = tn(n_ref[...], dl_ref[...]) + tn(term_ref[...], ones)
    place_slices(where_ref[0], scratch, keep_ref, send_ref)


def turned_back(values, cosine, sine):
    return turned(values, cosine, -sine)


def input_kernel(dq_ref, kv_ref, cos_ref, sin_ref, wq_ref, wk_ref, wv_ref, x_ref, s_ref,
                 grads_ref, part_ref, term_ref):
    cosine, sine = cos_ref[...], sin_ref[...]
    lanes = 2 * HEAD_DIM
    q_width, kv_width = wq_ref.shape[1], wk_ref.shape[1]
    total = jnp.sum(kv_ref[...].astype(F32), axis=0).T
    for i in range(0, q_width, lanes):
        grads_ref[:, i : i + lanes] = turned_back(dq_ref[:, i : i + lanes], cosine, sine).astype(BF)
    for i in range(0, kv_width, lanes):
        grads_ref[:, q_width + i : q_width + i + lanes] = turned_back(total[:, i : i + lanes], cosine, sine).astype(BF)
    grads_ref[:, q_width + kv_width :] = total[:, kv_width:].astype(BF)
    part = (
        nt(grads_ref[:, :q_width], wq_ref[...])
        + nt(grads_ref[:, q_width : q_width + kv_width], wk_ref[...])
        + nt(grads_ref[:, q_width + kv_width :], wv_ref[...])
    )
    part_ref[...] = part.astype(BF)
    term = jnp.sum(part * x_ref[...].astype(F32) * s_ref[...], axis=0, keepdims=True)
    line = lax.broadcasted_iota(jnp.int32, term_ref.shape, 0)
    term_ref[...] = jnp.where(line == 0, term, 0.0)


def late_kernel(where_ref, n_ref, grads_ref, term_ref, other_ref, keep_ref, send_ref, scratch):
    width = grads_ref.shape[1]
    scratch[:, :width] = tn(n_ref[...], grads_ref[...])
    ones = jnp.ones((term_ref.shape[0], scratch.shape[1] - width), BF)
    scratch[:, width:] = tn((term_ref[...] + other_ref[...]).astype(BF), ones)
    place_slices(where_ref[0], scratch, keep_ref, send_ref)


def near_sum(keep, send):
    return keep.astype(F32) + swap(send, "dp", 1).astype(F32)


def place_sum(total):
    return jnp.sum(exchange(total.astype(BF)).astype(F32), axis=0)


def far_sum(total, axis):
    bit = 1
    while total.shape[axis] > 1:
        bit *= 2
        lead = total.shape[:axis]
        pairs = total.reshape(lead + (total.shape[axis] // 2, 2) + total.shape[axis + 1 :])
        keep = lax.index_in_dim(pairs, 0, axis + 1, keepdims=False)
        send = lax.index_in_dim(pairs, 1, axis + 1, keepdims=False)
        total = keep + swap(send.astype(BF), "dp", bit).astype(F32)
    return jnp.squeeze(total, axis)


def norm_backward(values, norm_scale, gain, grad_normed):
    weighted = grad_normed * gain
    inner = jnp.mean(weighted * values, axis=1, keepdims=True)
    grad_values = norm_scale * weighted - values * (norm_scale * norm_scale * norm_scale) * inner
    grad_gain = jnp.sum(grad_normed * values * norm_scale, axis=0)
    return (grad_values, grad_gain)


def rotary_tables(length):
    half = HEAD_DIM // 2
    inverse = ROPE_BASE ** (-2.0 * np.arange(half) / HEAD_DIM)
    angles = np.arange(length)[:, None] * inverse[None, :]
    cosine, sine = np.cos(angles), np.sin(angles)
    return (
        np.concatenate([cosine, cosine, cosine, cosine], axis=1).astype(np.float32),
        np.concatenate([-sine, sine, -sine, sine], axis=1).astype(np.float32),
    )


def body(
    x_in,
    segments,
    chosen,
    out_grad,
    norm1_gain,
    w_query,
    w_key,
    w_value,
    w_out,
    norm2_gain,
    w_router,
    w_gate,
    w_up,
    w_down,
):
    tok_rows, full_width = x_in.shape
    h = HEAD_DIM
    q_width, kv_width = w_query.shape[1], w_key.shape[1]
    groups = q_width // kv_width
    experts_local, _, inner = w_gate.shape
    n_exp, n_dp = lax.axis_size("expert"), lax.axis_size("dp")
    total_experts = experts_local * n_exp
    top_count = chosen.shape[1]
    capacity = tok_rows * top_count * 25 // (16 * total_experts)
    place, side = lax.axis_index("expert"), lax.axis_index("tensor")
    half_width = full_width // lax.axis_size("tensor")
    row_start = place * tok_rows
    seq_length = segments.shape[0]
    half_rows = tok_rows // 2

    own_dp = lax.axis_index("dp")
    order = [1, 3, 2, 0] if n_exp == 4 else [*range(1, n_exp), 0]
    group = n_exp // 2
    vmem = lambda *shape: pltpu.VMEM(shape, BF)
    prefetch = pltpu.PrefetchScalarGridSpec

    tables = [
        lax.dynamic_slice_in_dim(jnp.asarray(table), row_start, tok_rows)
        for table in rotary_tables(seq_length)
    ]
    cosine, sine = tables
    normed_one, query_rot, kv_own, scale_one = pl.pallas_call(
        project_kernel,
        name="project",
        out_shape=(
            shaped(BF, tok_rows, full_width),
            shaped(BF, tok_rows, q_width),
            shaped(BF, tok_rows, 2 * kv_width),
            shaped(F32, tok_rows, 1),
        ),
        compiler_params=params(32),
        cost_estimate=cost(2),
    )(x_in, norm1_gain[None], w_query, w_key, w_value, cosine, sine)
    kv_blocks = [kv_own] + [fetch(kv_own, k) for k in range(1, n_exp)]

    turned_segments = lax.dynamic_slice_in_dim(
        jnp.concatenate([segments, segments]), row_start, seq_length
    )
    key_positions = (row_start + jnp.arange(seq_length, dtype=jnp.int32)) % seq_length
    allowed = (turned_segments[:tok_rows, None] == turned_segments[None, :]) & (
        key_positions[:tok_rows, None] >= key_positions[None, :]
    )
    bias = jnp.where(allowed, 0.0, MASKED).astype(F32)
    heads = q_width // h
    out_half = w_out.shape[0] // 2
    own_core = own_dp % 2
    w_near = swap(lax.dynamic_slice_in_dim(w_out, own_core * out_half, out_half), "tensor")
    w_far = swap(w_near, "dp", 1)
    attended, attended_low, log_totals = pl.pallas_call(
        functools.partial(attend_kernel, groups, n_exp),
        name="attend",
        out_shape=(
            shaped(F32, tok_rows, q_width),
            shaped(BF, tok_rows, q_width),
            shaped(F32, tok_rows, heads),
        ),
        scratch_shapes=[vmem(seq_length, 2 * kv_width)],
        compiler_params=params(40),
        cost_estimate=cost(10),
    )(after(query_rot, w_near), *kv_blocks, bias)

    cot_in, chosen_in = out_grad, chosen
    cot_half = lambda s: lax.dynamic_slice_in_dim(cot_in, s * half_rows, half_rows)
    chosen_half = lambda s: jnp.pad(
        lax.dynamic_slice_in_dim(chosen_in, s * half_rows, half_rows).T.astype(BF),
        ((0, 16 - top_count), (0, full_width - half_rows)),
    )
    payload = lambda s: jnp.concatenate([cot_half(s), chosen_half(s)], axis=0)
    cot_own, cot_other = payload(side), payload(1 - side)
    cot_near = {}
    for k in order:
        cot_near[k] = fetch(after(cot_own, *kv_blocks[1:]), k) if k else cot_own
    expert_slots = n_exp * capacity
    by_expert = lambda *tail: pl.BlockSpec((1,) + tail, lambda e, *_: (e,) + (0,) * len(tail))

    middle_in = (x_in, attended_low, swap(attended_low, "tensor"), w_out, w_near, w_far, norm2_gain[None])
    whole = lambda array: full(*array.shape)
    hidden_one, scale_two, normed_two, normed_own, normed_far = pl.pallas_call(
        middle_kernel,
        name="middle",
        grid_spec=prefetch(
            num_scalar_prefetch=1,
            grid=(1,),
            in_specs=[whole(array) for array in middle_in],
            out_specs=(
                full(tok_rows, full_width),
                full(tok_rows, 1),
                full(tok_rows, full_width),
                full(half_rows, full_width),
                full(half_rows, full_width),
            ),
        ),
        out_shape=(
            shaped(F32, tok_rows, full_width),
            shaped(F32, tok_rows, 1),
            shaped(BF, tok_rows, full_width),
            shaped(BF, half_rows, full_width),
            shaped(BF, half_rows, full_width),
        ),
        compiler_params=params(32),
        cost_estimate=cost(2),
    )(jnp.stack([side, own_core]), *middle_in)
    near_rows = {k: fetch(normed_own, k) for k in order[:group]}
    for k in order[group:]:
        near_rows[k] = fetch(after(normed_own, *near_rows.values()), k) if k else normed_own

    cot_pairs = [
        (cot_near[k], swap(after(cot_near[k], normed_own), "tensor") if k else cot_other)
        for k in order
    ]
    chosen_blocks = jnp.stack(
        [
            jnp.concatenate([part[half_rows : half_rows + top_count, :half_rows] for part in pair], axis=1)
            for pair in cot_pairs
        ]
    ).astype(jnp.int32)
    expert_ids = jnp.arange(total_experts, dtype=jnp.int32)
    hot_all = jnp.any(chosen_blocks[:, :, None, :] == expert_ids[:, None], axis=1)
    hot_rows = hot_all.transpose(1, 0, 2).reshape(total_experts, n_exp * tok_rows).astype(F32)
    hot_local = lax.dynamic_slice_in_dim(hot_all, place * experts_local, experts_local, 1)
    token_row = jnp.arange(tok_rows, dtype=jnp.int32)
    before = (token_row[:, None] < token_row[None, :]).astype(BF)
    rank = jnp.einsum("kes,st->ket", hot_local.astype(BF), before, preferred_element_type=F32)
    slot_of = jnp.where(hot_local, rank.astype(jnp.int32), -1)

    cot_slots, raw_grad = pl.pallas_call(
        functools.partial(cotangent_kernel, n_exp, capacity),
        name="cotangent",
        grid=(experts_local,),
        in_specs=[whole(slot_of)]
        + [full(*cot_own.shape)] * (2 * n_exp)
        + [by_expert(inner, full_width)],
        out_specs=(by_expert(expert_slots, full_width), by_expert(expert_slots, inner)),
        out_shape=(
            shaped(BF, experts_local, expert_slots, full_width),
            shaped(F32, experts_local, expert_slots, inner),
        ),
        scratch_shapes=[vmem(n_exp, tok_rows, full_width)],
        compiler_params=params(40),
        cost_estimate=cost(13),
    )(slot_of, *[half for pair in cot_pairs for half in pair], w_down)

    far_rows = {
        k: swap(near_rows[k], "tensor") if k else normed_far for k in order
    }

    def run_experts(number, hold):
        ks = order[number * group : (number + 1) * group]
        token_halves = [half for k in ks for half in (near_rows[k], far_rows[k])]
        token_halves[0] = after(token_halves[0], *hold)
        slots_here = group * capacity
        low_slots = shaped(BF, experts_local, slots_here, inner)
        columns = group * tok_rows
        return pl.pallas_call(
            functools.partial(experts_kernel, group, capacity),
            name="experts",
            grid_spec=prefetch(
                num_scalar_prefetch=1,
                grid=(experts_local,),
                in_specs=[full(group, experts_local, tok_rows)]
                + [full(half_rows, full_width)] * (2 * group)
                + [
                    pl.BlockSpec((total_experts, columns), lambda e, *_: (0, number)),
                    full(total_experts, full_width),
                    pl.BlockSpec((1, slots_here, inner), lambda e, *_: (e, number, 0)),
                    by_expert(full_width, inner),
                    by_expert(full_width, inner),
                ],
                out_specs=(
                    by_expert(slots_here, full_width),
                    by_expert(slots_here, inner),
                    by_expert(slots_here, inner),
                    by_expert(slots_here, inner),
                    full(group, half_rows + 16, full_width),
                    full(group, half_rows + 16, full_width),
                ),
                scratch_shapes=[
                    vmem(group, tok_rows, full_width),
                    pltpu.VMEM((total_experts, columns), F32),
                    vmem(group, experts_local * capacity, full_width),
                    vmem(group, experts_local * capacity, tok_rows),
                    pltpu.VMEM((2 * group, full_width), F32),
                ],
            ),
            out_shape=(
                shaped(BF, experts_local, slots_here, full_width),
                low_slots,
                low_slots,
                low_slots,
                shaped(BF, group, half_rows + 16, full_width),
                shaped(BF, group, half_rows + 16, full_width),
            ),
            compiler_params=params(40),
            cost_estimate=cost(18),
        )(
            place[None], slot_of[number * group : (number + 1) * group], *token_halves,
            hot_rows, w_router.T, raw_grad, w_gate, w_up,
        )

    first = run_experts(0, [far_rows[k] for k in order[group:]])
    second = run_experts(1, [first[4]])

    def pair_sum(made, got):
        return pl.pallas_call(
            pair_sum_kernel,
            name="pair_sum",
            out_shape=(shaped(BF, half_rows + 16, full_width),) * group,
            compiler_params=params(24),
            cost_estimate=cost(1),
        )(made[4], got)

    first_sums = pair_sum(first, swap(first[5], "tensor"))
    second_got = swap(second[5], "tensor")

    out_dims = (n_exp, tok_rows, half_width)

    def combine(*hold):
        return pl.pallas_call(
            functools.partial(combine_kernel, capacity, order),
            name="combine",
            grid_spec=prefetch(
                num_scalar_prefetch=1,
                grid=(experts_local,),
                in_specs=[
                    whole(slot_of),
                    by_expert(group * capacity, inner),
                    by_expert(group * capacity, inner),
                    by_expert(inner, full_width),
                ],
                out_specs=(full(*out_dims), full(*out_dims)),
                scratch_shapes=[
                    vmem(n_exp, experts_local * capacity, full_width),
                    vmem(n_exp, experts_local * capacity, tok_rows),
                ],
            ),
            out_shape=(shaped(BF, *out_dims), shaped(BF, *out_dims)),
            compiler_params=params(48),
            cost_estimate=cost(12),
        )(after(jnp.stack([side, place]), *hold), slot_of, first[1], second[1], w_down)

    out_mine, out_else = combine(*first_sums, second[4])
    terms = {k: deliver(first_sums[i], k) for i, k in enumerate(order[:group])}
    second_got, *arrived = lax.optimization_barrier((second_got, out_mine, *terms.values()))
    terms = dict(zip(terms, arrived[1:]))
    second_sums = pair_sum(second, second_got)
    for i, k in enumerate(order[group:]):
        terms[k] = deliver(second_sums[i], k) if k else second_sums[i]
    out_got = swap(after(out_else, second_sums[0]), "tensor")
    out_low = (out_mine.astype(F32) + out_got.astype(F32)).astype(BF)

    slice_width = full_width // n_dp
    pairs = [*first[:4], *second[:4]]
    weight_grads = pl.pallas_call(
        weights_kernel,
        name="weights",
        grid=(experts_local,),
        in_specs=[by_expert(expert_slots, full_width)] + [by_expert(*array.shape[1:]) for array in pairs],
        out_specs=pl.BlockSpec((n_dp, 1, 3, slice_width, inner), lambda e: (0, e, 0, 0, 0)),
        out_shape=shaped(BF, n_dp, experts_local, 3, slice_width, inner),
        compiler_params=params(40),
        cost_estimate=cost(24),
    )(after(cot_slots, *second_sums), *pairs)
    half_sum = pl.pallas_call(
        gather_sum_kernel,
        name="gather_sum",
        out_shape=shaped(BF, half_rows + 16, full_width),
        compiler_params=params(24),
        cost_estimate=cost(1),
    )(after(terms[0], weight_grads, out_low), *[terms[k] for k in range(1, n_exp)])
    weight_sum = lax.psum_scatter(
        after(weight_grads, half_sum), "dp", scatter_dimension=0, tiled=False
    )
    half_other = swap(half_sum, "tensor")
    out_home = exchange(after(out_low, half_sum))

    tail_lanes = -(-(total_experts + 1) // 128) * 128
    router_wide = jnp.pad(w_router, ((0, 0), (0, tail_lanes - total_experts)))
    back_in = (
        half_sum, half_other, normed_two, chosen, router_wide, hidden_one, scale_two, norm2_gain[None], out_grad, w_out,
    )
    hidden_grad, branch_cot, gain_two_term, attended_grad, logit_grads = pl.pallas_call(
        functools.partial(norm_grad_kernel, experts_local),
        name="norm_grad",
        grid_spec=prefetch(
            num_scalar_prefetch=1,
            grid=(1,),
            in_specs=[whole(array) for array in back_in],
            out_specs=(
                full(tok_rows, full_width),
                full(tok_rows, full_width),
                full(tok_rows, full_width),
                full(tok_rows, q_width),
                full(tok_rows, tail_lanes),
            ),
            scratch_shapes=[vmem(tok_rows, full_width), pltpu.VMEM((2, tail_lanes, half_rows), F32)],
        ),
        out_shape=(
            shaped(F32, tok_rows, full_width),
            shaped(BF, tok_rows, full_width),
            shaped(BF, tok_rows, full_width),
            shaped(BF, tok_rows, q_width),
            shaped(BF, tok_rows, tail_lanes),
        ),
        compiler_params=params(40),
        cost_estimate=cost(4),
    )(jnp.stack([side, place]), *back_in)

    back_args = (query_rot, *kv_blocks, attended_grad, attended, log_totals, bias)
    query_grads, kv_parts = pl.pallas_call(
        functools.partial(attend_grad_kernel, groups, n_exp),
        name="attend_grad",
        grid_spec=prefetch(
            num_scalar_prefetch=1,
            grid=(1,),
            in_specs=[whole(array) for array in back_args],
            out_specs=(full(tok_rows, q_width), full(n_exp, 2 * kv_width, tok_rows)),
            scratch_shapes=[vmem(seq_length, 2 * kv_width)],
        ),
        out_shape=(shaped(F32, tok_rows, q_width), shaped(BF, n_exp, 2 * kv_width, tok_rows)),
        compiler_params=params(40),
        cost_estimate=cost(10),
    )(place[None], *back_args)
    kv_terms = exchange(after(kv_parts, out_home))

    slice_rows = full_width // (n_dp * n_exp)

    def slices_of(kernel, name, width, *arrays):
        dims = (n_exp, n_dp // 2, slice_rows, width)
        return pl.pallas_call(
            kernel,
            name=name,
            grid_spec=prefetch(
                num_scalar_prefetch=1,
                grid=(1,),
                in_specs=[whole(array) for array in arrays],
                out_specs=(full(*dims), full(*dims)),
                scratch_shapes=[pltpu.VMEM((full_width, width), F32)],
            ),
            out_shape=(shaped(BF, *dims), shaped(BF, *dims)),
            compiler_params=params(48),
            cost_estimate=cost(5),
        )(own_dp[None], *arrays)

    early_keep, early_send = slices_of(
        early_kernel, "early", q_width + tail_lanes,
        after(branch_cot, query_grads), attended_low, normed_two, logit_grads, gain_two_term,
    )
    kv_terms, early_keep, early_send = lax.optimization_barrier((kv_terms, early_keep, early_send))
    early = near_sum(early_keep, early_send).astype(BF)
    grads_low, partial_low, gain_one_term = pl.pallas_call(
        input_kernel,
        name="input",
        out_shape=(
            shaped(BF, tok_rows, q_width + 2 * kv_width),
            shaped(BF, tok_rows, full_width),
            shaped(F32, 16, full_width),
        ),
        compiler_params=params(40),
        cost_estimate=cost(4),
    )(query_grads, kv_terms, cosine, sine, w_query, w_key, w_value, x_in, scale_one)
    partial_other = swap(partial_low, "tensor")
    late_keep, late_send = slices_of(
        late_kernel, "late", q_width + 2 * kv_width + 128, normed_one, grads_low, gain_one_term, swap(gain_one_term, "tensor")
    )
    late = near_sum(late_keep, late_send).astype(BF)
    early = place_sum(early)
    late, partial_other, early = lax.optimization_barrier((late, partial_other, early))
    late = place_sum(late)
    early = far_sum(early, 0)
    grad_gate, grad_up, grad_down = pl.pallas_call(
        finish_kernel,
        name="finish",
        grid=(experts_local,),
        in_specs=[by_expert(3, slice_width, inner)],
        out_specs=(
            by_expert(slice_width, inner),
            by_expert(slice_width, inner),
            by_expert(inner, slice_width),
        ),
        out_shape=(
            shaped(F32, experts_local, slice_width, inner),
            shaped(F32, experts_local, slice_width, inner),
            shaped(F32, experts_local, inner, slice_width),
        ),
        compiler_params=params(32),
        cost_estimate=cost(6),
    )(weight_sum)

    late = far_sum(after(late, grad_gate), 0)

    mixture_half = jnp.sum(out_home.astype(F32), axis=0)
    mixture_half = jnp.where(side == 0, mixture_half, jnp.roll(mixture_half, half_rows, axis=0))
    residual_half = lax.dynamic_slice_in_dim(hidden_one, side * half_width, half_width, 1)
    block_out = (residual_half + mixture_half).astype(BF)

    normed_one_grad = partial_low.astype(F32) + partial_other.astype(F32)
    inputs = x_in.astype(F32)
    input_part, _ = norm_backward(inputs, scale_one, norm1_gain, normed_one_grad)
    input_grad = hidden_grad + input_part
    gain_one = late[:, -1]
    return (
        block_out,
        input_grad,
        gain_one,
        late[:, :q_width],
        late[:, q_width : q_width + kv_width],
        late[:, q_width + kv_width : q_width + 2 * kv_width],
        early[:, :q_width].T,
        early[:, -1],
        early[:, q_width : q_width + total_experts],
        grad_gate,
        grad_up,
        grad_down,
    )


def solution(mesh):
    return jax.shard_map(
        body,
        mesh=mesh,
        in_specs=(
            P(("dp", "expert"), None),
            P("dp"),
            P(("dp", "expert"), None),
            P(("dp", "expert"), None),
            P(),
            P(None, "tensor"),
            P(None, "tensor"),
            P(None, "tensor"),
            P("tensor", None),
            P(),
            P(),
            P("expert", None, "tensor"),
            P("expert", None, "tensor"),
            P("expert", "tensor", None),
        ),
        out_specs=(
            P(("dp", "expert"), "tensor"),
            P(("dp", "expert"), None),
            P(("dp", "expert")),
            P(("dp", "expert"), "tensor"),
            P(("dp", "expert"), "tensor"),
            P(("dp", "expert"), "tensor"),
            P("tensor", ("dp", "expert")),
            P(("dp", "expert")),
            P(("dp", "expert"), None),
            P("expert", "dp", "tensor"),
            P("expert", "dp", "tensor"),
            P("expert", "tensor", "dp"),
        ),
        check_vma=False,
    )
```

```python
import functools

import jax
import jax.numpy as jnp
import numpy as np
from jax import lax
from jax.experimental import pallas as pl
from jax.experimental.pallas import tpu as pltpu
from jax.sharding import PartitionSpec as P

HEAD_DIM = 64
EPSILON = 1e-05
ROPE_BASE = 10000.0
MASKED = -1e30
BF = jnp.bfloat16
F32 = jnp.float32
MIB = 1024 * 1024


def swap(values, axis, bit=1):
    count = lax.axis_size(axis)
    return lax.ppermute(values, axis, [(i, i ^ bit) for i in range(count)])


def fetch(values, offset):
    count = lax.axis_size("expert")
    return lax.ppermute(values, "expert", [(i, (i - offset) % count) for i in range(count)])


def deliver(values, offset):
    count = lax.axis_size("expert")
    return lax.ppermute(values, "expert", [(i, (i + offset) % count) for i in range(count)])


def halve(parts, bit_axis, bit):
    pairs = parts.reshape((parts.shape[0] // 2, 2) + parts.shape[1:])
    own = (lax.axis_index(bit_axis) // bit) % 2
    keep = lax.dynamic_index_in_dim(pairs, own, 1, keepdims=False)
    send = lax.dynamic_index_in_dim(pairs, 1 - own, 1, keepdims=False)
    got = swap(send, bit_axis, bit)
    return keep.astype(F32) + got.astype(F32)


def sum_over_dp(parts):
    bit = 1
    while parts.shape[0] > 1:
        parts = halve(parts.astype(BF), "dp", bit)
        bit *= 2
    return parts[0]


def exchange(parts):
    return lax.all_to_all(parts, "expert", split_axis=0, concat_axis=0, tiled=True)


def nn(left, right):
    return jnp.dot(left, right, preferred_element_type=F32)


def nt(left, right):
    return lax.dot_general(left, right, (((1,), (1,)), ((), ())), preferred_element_type=F32)


def tn(left, right):
    return lax.dot_general(left, right, (((0,), (0,)), ((), ())), preferred_element_type=F32)


def params():
    return pltpu.CompilerParams(vmem_limit_bytes=60 * MIB)


def cost(micros):
    return pl.CostEstimate(flops=int(micros * 1e3), bytes_accessed=0, transcendentals=0)


def shaped(kind, *dims):
    return jax.ShapeDtypeStruct(dims, kind)


def full(*shape):
    return pl.BlockSpec(shape, lambda *_: (0,) * len(shape))


def after(values, *others):
    return lax.optimization_barrier((values,) + others)[0]


def turned(values, cosine, sine):
    lane = lax.broadcasted_iota(jnp.int32, values.shape, 1)
    quarter = HEAD_DIM // 2
    later = pltpu.roll(values, 2 * HEAD_DIM - quarter, 1)
    earlier = pltpu.roll(values, quarter, 1)
    return values * cosine + jnp.where(lane % HEAD_DIM < quarter, later, earlier) * sine


def project_kernel(x_ref, gain_ref, wq_ref, wk_ref, wv_ref, cos_ref, sin_ref, n_ref, q_ref, kv_ref, s_ref):
    values = x_ref[...].astype(F32)
    scale = lax.rsqrt(jnp.mean(values * values, axis=1, keepdims=True) + EPSILON)
    s_ref[...] = scale
    normed = (values * scale * gain_ref[...]).astype(BF)
    n_ref[...] = normed
    cosine, sine = cos_ref[...], sin_ref[...]
    lanes = 2 * HEAD_DIM
    kv = wk_ref.shape[1]
    keys = nn(normed, wk_ref[...])
    for i in range(0, kv, lanes):
        kv_ref[:, i : i + lanes] = turned(keys[:, i : i + lanes], cosine, sine).astype(BF)
    kv_ref[:, kv:] = nn(normed, wv_ref[...]).astype(BF)
    query = nn(normed, wq_ref[...])
    for i in range(0, query.shape[1], lanes):
        q_ref[:, i : i + lanes] = turned(query[:, i : i + lanes], cosine, sine).astype(BF)


def attend_kernel(groups, blocks, *refs):
    q_ref, kv_refs, bias_ref = refs[0], refs[1 : 1 + blocks], refs[1 + blocks]
    o_ref, low_ref, lse_ref, kv_ref = refs[2 + blocks :]
    h = HEAD_DIM
    rows = kv_refs[0].shape[0]
    for k in range(blocks):
        kv_ref[k * rows : (k + 1) * rows, :] = kv_refs[k][...]
    heads = kv_ref.shape[1] // (2 * h)
    for kv in range(heads):
        key = kv_ref[:, kv * h : kv * h + h]
        value = kv_ref[:, (heads + kv) * h : (heads + kv) * h + h]
        for g in range(groups):
            head = kv * groups + g
            span = slice(head * h, head * h + h)
            scores = nt(q_ref[:, span], key) * h**-0.5 + bias_ref[...]
            peak = jnp.max(scores, axis=1, keepdims=True)
            raw = jnp.exp(scores - peak)
            total = jnp.sum(raw, axis=1, keepdims=True)
            out = nn((raw * (1.0 / total)).astype(BF), value)
            o_ref[:, span] = out
            low_ref[:, span] = out.astype(BF)
            lse_ref[:, head : head + 1] = peak + jnp.log(total)


def attend_grad_kernel(groups, blocks, place_ref, *refs):
    q_ref, kv_refs, d_ref, o_ref, lse_ref, bias_ref = refs[0], refs[1 : 1 + blocks], *refs[1 + blocks : 5 + blocks]
    dq_ref, dkv_ref, kv_ref = refs[5 + blocks :]
    h = HEAD_DIM
    rows = kv_refs[0].shape[0]
    for k in range(blocks):
        kv_ref[k * rows : (k + 1) * rows, :] = kv_refs[k][...]
    heads = kv_ref.shape[1] // (2 * h)
    for kv in range(heads):
        key = kv_ref[:, kv * h : kv * h + h]
        value = kv_ref[:, (heads + kv) * h : (heads + kv) * h + h]
        key_grad = value_grad = None
        for g in range(groups):
            head = kv * groups + g
            span = slice(head * h, head * h + h)
            query = q_ref[:, span]
            cot = d_ref[:, span]
            scores = nt(query, key) * h**-0.5 + bias_ref[...]
            probs = jnp.exp(scores - lse_ref[:, head : head + 1])
            delta = jnp.sum(cot.astype(F32) * o_ref[:, span], axis=1, keepdims=True)
            slope = (probs * (nt(cot, value) - delta)).astype(BF)
            value_part = tn(cot, probs.astype(BF))
            key_part = tn(query, slope)
            dq_ref[:, span] = nn(slope, key) * h**-0.5
            value_grad = value_part if value_grad is None else value_grad + value_part
            key_grad = key_part if key_grad is None else key_grad + key_part
        key_low = (key_grad * h**-0.5).astype(BF)
        value_low = value_grad.astype(BF)
        for k in range(blocks):
            to = lax.rem(place_ref[0] + k, blocks)
            dkv_ref[to, kv * h : kv * h + h, :] = key_low[:, k * rows : (k + 1) * rows]
            dkv_ref[to, (heads + kv) * h : (heads + kv) * h + h, :] = value_low[:, k * rows : (k + 1) * rows]


def middle_kernel(
    side_ref, x_ref, mine_ref, other_ref, w_ref, w_near, w_far, gain_ref, h_ref, s_ref, n_ref, own_ref, far_ref
):
    part = w_near.shape[0]
    hidden = x_ref[...].astype(F32) + nn(mine_ref[...], w_ref[...])
    for w, number in ((w_near, side_ref[1]), (w_far, 1 - side_ref[1])):
        hidden += nn(other_ref[:, pl.ds(pl.multiple_of(number * part, part), part)], w[...])
    h_ref[...] = hidden
    scale = lax.rsqrt(jnp.mean(hidden * hidden, axis=1, keepdims=True) + EPSILON)
    s_ref[...] = scale
    n_ref[...] = (hidden * scale * gain_ref[...]).astype(BF)
    half = own_ref.shape[0]
    own_ref[...] = n_ref[pl.ds(pl.multiple_of(side_ref[0] * half, half), half), :]
    far_ref[...] = n_ref[pl.ds(pl.multiple_of((1 - side_ref[0]) * half, half), half), :]


def make_pick(slot_ref, k, expert, slots):
    row = slot_ref[k, pl.ds(expert, 1), :]
    lines = lax.broadcasted_iota(jnp.int32, (slots, row.shape[1]), 0)
    return jnp.where(lines == row, 1.0, 0.0)


def cotangent_kernel(blocks, slots, *refs):
    slot_ref, halves, wd_ref = refs[0], refs[1 : 1 + 2 * blocks], refs[1 + 2 * blocks]
    cg_ref, dm_ref, x_ref = refs[2 + 2 * blocks :]
    half = x_ref.shape[1] // 2
    step = pl.program_id(0)

    @pl.when(step == 0)
    def _():
        for k in range(blocks):
            x_ref[k, :half, :] = halves[2 * k][:half, :]
            x_ref[k, half:, :] = halves[2 * k + 1][:half, :]

    for k in range(blocks):
        pick = make_pick(slot_ref, k, step, slots).astype(BF)
        cg_ref[0, k * slots : (k + 1) * slots, :] = nn(pick, x_ref[k]).astype(BF)
    dm_ref[0] = nt(cg_ref[0], wd_ref[0])


def split_rows(values):
    line = lax.broadcasted_iota(jnp.int32, (16, values[0].shape[1]), 0)
    out = jnp.zeros(line.shape, F32)
    for i, value in enumerate(values):
        high = value.astype(BF).astype(F32)
        out = jnp.where(line == 2 * i, high, jnp.where(line == 2 * i + 1, value - high, out))
    return out.astype(BF)


def pair_sum_kernel(mine_ref, got_ref, *outs):
    half = mine_ref.shape[1] - 16
    for k, out in enumerate(outs):
        total = mine_ref[k].astype(F32) + got_ref[k].astype(F32)
        out[:half, :] = total[:half].astype(BF)
        out[half:, :] = split_rows([total[half : half + 1] + total[half + 1 : half + 2]])


def gather_sum_kernel(*refs):
    parts, out = refs[:-1], refs[-1]
    half = out.shape[0] - 16
    total = parts[0][...].astype(F32)
    rows = [total[half : half + 1] + total[half + 1 : half + 2]]
    total = total[:half]
    for part in parts[1:]:
        more = part[...].astype(F32)
        total = total + more[:half]
        rows.append(more[half : half + 1] + more[half + 1 : half + 2])
    out[:half, :] = total.astype(BF)
    out[half:, :] = split_rows(rows)


def experts_kernel(blocks, slots, place_ref, slot_ref, *refs):
    halves, (hot_ref, router_ref, dm_ref, wg_ref, wu_ref) = refs[: 2 * blocks], refs[2 * blocks : 5 + 2 * blocks]
    (xg_ref, gm_ref, da_ref, db_ref, mine_ref, else_ref,
     x_ref, gates_ref, n_ref, pick_ref, dg_ref) = refs[5 + 2 * blocks :]
    rows = x_ref.shape[1]
    half = rows // 2
    step, steps = pl.program_id(0), pl.num_programs(0)

    @pl.when(step == 0)
    def _():
        for k in range(blocks):
            x_ref[k, :half, :] = halves[2 * k][...]
            x_ref[k, half:, :] = halves[2 * k + 1][...]
        tokens = x_ref[...].reshape(blocks * rows, x_ref.shape[2])
        hot = hot_ref[...] > 0.0
        logits = jnp.where(hot, nt(router_ref[...], tokens), MASKED)
        raw = jnp.where(hot, jnp.exp(logits - jnp.max(logits, axis=0, keepdims=True)), 0.0)
        gates_ref[...] = raw / jnp.sum(raw, axis=0, keepdims=True)
        dg_ref[...] = jnp.zeros_like(dg_ref)

    gate_row = gates_ref[pl.ds(place_ref[0] * steps + step, 1), :]
    at = pl.multiple_of(step * slots, slots)
    gate_parts, picks = [], []
    for k in range(blocks):
        pick = make_pick(slot_ref, k, step, slots)
        picks.append(pick)
        low = pick.astype(BF)
        pick_ref[k, pl.ds(at, slots), :] = low
        xg_ref[0, k * slots : (k + 1) * slots, :] = nn(low, x_ref[k]).astype(BF)
        gate_parts.append(jnp.sum(pick * gate_row[:, k * rows : (k + 1) * rows], axis=1, keepdims=True))
    gates = jnp.concatenate(gate_parts, axis=0)
    own = xg_ref[0]
    gate_pre = nn(own, wg_ref[0])
    up_pre = nn(own, wu_ref[0])
    raw_grad = dm_ref[0]
    sigmoid = 1.0 / (1.0 + jnp.exp(-gate_pre))
    swish = gate_pre * sigmoid
    active = swish * up_pre
    dgate = jnp.sum(active * raw_grad, axis=1, keepdims=True)
    gm_ref[0] = (gates * active).astype(BF)
    grad = gates * raw_grad
    da = (grad * up_pre * sigmoid * (1.0 + gate_pre * (1.0 - sigmoid))).astype(BF)
    db = (grad * swish).astype(BF)
    da_ref[0] = da
    db_ref[0] = db
    low = (nt(da, wg_ref[0]) + nt(db, wu_ref[0])).astype(BF)
    for k in range(blocks):
        part = slice(k * slots, (k + 1) * slots)
        n_ref[k, pl.ds(at, slots), :] = low[part]
        dg_row = jnp.sum(picks[k] * dgate[part], axis=0, keepdims=True)
        lanes = pl.ds(pl.multiple_of(step * half, half), half)
        dg_ref[2 * k : 2 * k + 1, lanes] = dg_row[:, :half]
        dg_ref[2 * k + 1 : 2 * k + 2, lanes] = dg_row[:, half:]

    @pl.when(step == steps - 1)
    def _():
        for k in range(blocks):
            out = tn(pick_ref[k], n_ref[k]).astype(BF)
            mine_ref[k, :half, :] = out[:half]
            else_ref[k, :half, :] = out[half:]
            mine_ref[k, half:, :] = split_rows([dg_ref[2 * k : 2 * k + 1, :]])
            else_ref[k, half:, :] = split_rows([dg_ref[2 * k + 1 : 2 * k + 2, :]])


def weights_kernel(own_ref, cg_ref, *refs):
    pairs, outs = refs[:8], refs[8:]
    count, width = len(outs) * outs[0].shape[0], outs[0].shape[3]
    split = pairs[0].shape[1]
    for number in range(count):
        if len(outs) == 1:
            out, place, span = outs[0], number, slice(number * width, (number + 1) * width)
        else:
            out, place = outs[number % 2], number // 2
            span = pl.ds(pl.multiple_of((own_ref[0] ^ number) * width, 128), width)
        gate = up = down = None
        for i in range(2):
            xg_ref, gm_ref, da_ref, db_ref = pairs[4 * i : 4 * i + 4]
            rows = xg_ref[0, :, span]
            cots = cg_ref[0, i * split : (i + 1) * split, span]
            parts = tn(rows, da_ref[0]), tn(rows, db_ref[0]), tn(cots, gm_ref[0])
            gate, up, down = parts if i == 0 else (gate + parts[0], up + parts[1], down + parts[2])
        out[place, 0, 0] = gate.astype(BF)
        out[place, 0, 1] = up.astype(BF)
        out[place, 0, 2] = down.astype(BF)


def finish_kernel(parts, *refs):
    gate_ref, up_ref, down_ref = refs[-3:]
    total = None
    for ref in refs[:parts]:
        term = ref[(0,) * (len(ref.shape) - 3)].astype(F32)
        total = term if total is None else total + term
    gate_ref[0] = total[0]
    up_ref[0] = total[1]
    down_ref[0] = total[2].T


def combine_kernel(slots, offsets, where_ref, slot_ref, ga_ref, gb_ref, wd_ref, mine_ref, else_ref, r_ref, pick_ref):
    blocks = mine_ref.shape[0]
    group = blocks // 2
    step, steps = pl.program_id(0), pl.num_programs(0)
    at = pl.multiple_of(step * slots, slots)
    for i, ref in enumerate((ga_ref, gb_ref)):
        low = nn(ref[0], wd_ref[0]).astype(BF)
        for j in range(group):
            k = i * group + j
            r_ref[k, pl.ds(at, slots), :] = low[j * slots : (j + 1) * slots]
            pick_ref[k, pl.ds(at, slots), :] = make_pick(slot_ref, k, step, slots).astype(BF)

    @pl.when(step == steps - 1)
    def _():
        width = mine_ref.shape[2]
        half = mine_ref.shape[1] // 2
        own = pl.ds(pl.multiple_of(where_ref[0] * width, width), width)
        far = pl.ds(pl.multiple_of((1 - where_ref[0]) * width, width), width)
        for k in range(blocks):
            to = lax.rem(where_ref[1] + offsets[k], blocks)
            mine_ref[to] = tn(pick_ref[k], r_ref[k, :, own]).astype(BF)
            out = tn(pick_ref[k], r_ref[k, :, far]).astype(BF)
            else_ref[to, :half] = out[half:]
            else_ref[to, half:] = out[:half]


def norm_grad_kernel(
    local, top, where_ref, own_ref, far_ref, n_ref, chosen_ref, router_ref, h_ref, s_ref, gain_ref, c_ref, w_ref,
    grad_ref, low_ref, term_ref, do_ref, dl_ref, e_ref, g_ref,
):
    side, place = where_ref[0], where_ref[1]
    half = own_ref.shape[0] - 16
    lanes = router_ref.shape[1]
    sources = 4
    g_ref[...] = jnp.zeros_like(g_ref)
    for part, ref in ((side, own_ref), (1 - side, far_ref)):
        e_ref[pl.ds(pl.multiple_of(part * half, half), half), :] = ref[:half, :]
        tail = ref[half:, :].astype(F32)
        for k in range(sources):
            row = tail[2 * k : 2 * k + 1] + tail[2 * k + 1 : 2 * k + 2]
            source = lax.rem(place + sources - k, sources)
            for e in range(local):
                g_ref[part, pl.ds(source * local + e, 1), :] = row[:, e * half : (e + 1) * half]
    dgate = jnp.concatenate([g_ref[0].T, g_ref[1].T], axis=0)
    lane = lax.broadcasted_iota(jnp.int32, dgate.shape, 1)
    hot = chosen_ref[:, 0:1] == lane
    for i in range(1, top):
        hot = hot | (chosen_ref[:, i : i + 1] == lane)
    logits = jnp.where(hot, nn(n_ref[...], router_ref[...]), MASKED)
    raw = jnp.where(hot, jnp.exp(logits - jnp.max(logits, axis=1, keepdims=True)), 0.0)
    gates = raw / jnp.sum(raw, axis=1, keepdims=True)
    logit_grads = (gates * (dgate - jnp.sum(gates * dgate, axis=1, keepdims=True))).astype(BF)
    dl_ref[...] = logit_grads
    grad = nt(logit_grads, router_ref[...]) + e_ref[...].astype(F32)
    hidden, scale = h_ref[...], s_ref[...]
    term_ref[...] = (grad * hidden * scale).astype(BF)
    weighted = grad * gain_ref[...]
    inner = jnp.mean(weighted * hidden, axis=1, keepdims=True)
    total = scale * weighted - hidden * (scale * scale * scale) * inner + c_ref[...].astype(F32)
    grad_ref[...] = total
    low = total.astype(BF)
    low_ref[...] = low
    do_ref[...] = nt(low, w_ref[...]).astype(BF)


def place_slices(own, scratch, keep_ref, send_ref):
    blocks, pairs, rows, _ = keep_ref.shape
    for a in range(2 * pairs):
        out = send_ref if a % 2 else keep_ref
        for b in range(blocks):
            number = (own ^ a) * blocks + b
            out[b, a // 2] = scratch[pl.ds(pl.multiple_of(number * rows, 8), rows), :].astype(BF)


def early_kernel(
    where_ref, low_ref, o_ref, n_ref, dl_ref, term_ref, first_ref, dq_ref, cos_ref, sin_ref,
    keep_ref, send_ref, turned_ref, scratch,
):
    width, lanes = o_ref.shape[1], 2 * HEAD_DIM
    tail = dl_ref.shape[1]
    for i in range(0, width, lanes):
        turned_ref[:, i : i + lanes] = turned(dq_ref[:, i : i + lanes], cos_ref[...], -sin_ref[...]).astype(BF)
    scratch[:, :width] = tn(low_ref[...], o_ref[...])
    lane = lax.broadcasted_iota(jnp.int32, dl_ref.shape, 1)
    ones = jnp.where(lane == tail - 1, 1.0, 0.0).astype(BF)
    scratch[:, width : width + tail] = tn(n_ref[...], dl_ref[...]) + tn(term_ref[...], ones)
    scratch[:, width + tail :] = tn(first_ref[...], turned_ref[...])
    place_slices(where_ref[0], scratch, keep_ref, send_ref)


def input_kernel(dq_ref, kv_ref, cos_ref, sin_ref, wq_ref, wk_ref, wv_ref, x_ref, s_ref,
                 grads_ref, part_ref, term_ref):
    lanes = 2 * HEAD_DIM
    kv_width = wk_ref.shape[1]
    total = jnp.sum(kv_ref[...].astype(F32), axis=0).T
    for i in range(0, kv_width, lanes):
        grads_ref[:, i : i + lanes] = turned(total[:, i : i + lanes], cos_ref[...], -sin_ref[...]).astype(BF)
    grads_ref[:, kv_width:] = total[:, kv_width:].astype(BF)
    part = (
        nt(dq_ref[...], wq_ref[...])
        + nt(grads_ref[:, :kv_width], wk_ref[...])
        + nt(grads_ref[:, kv_width:], wv_ref[...])
    )
    part_ref[...] = part.astype(BF)
    term = jnp.sum(part * x_ref[...].astype(F32) * s_ref[...], axis=0, keepdims=True)
    line = lax.broadcasted_iota(jnp.int32, term_ref.shape, 0)
    term_ref[...] = jnp.where(line == 0, term, 0.0)


def late_kernel(where_ref, n_ref, grads_ref, term_ref, other_ref, keep_ref, send_ref, scratch):
    width = grads_ref.shape[1]
    scratch[:, :width] = tn(n_ref[...], grads_ref[...])
    ones = jnp.ones((term_ref.shape[0], scratch.shape[1] - width), BF)
    scratch[:, width:] = tn((term_ref[...] + other_ref[...]).astype(BF), ones)
    place_slices(where_ref[0], scratch, keep_ref, send_ref)


def near_sum(keep, send):
    return keep.astype(F32) + swap(send, "dp", 1).astype(F32)


def place_sum(total):
    return jnp.sum(exchange(total.astype(BF)).astype(F32), axis=0)


def far_sum(total, axis):
    bit = 1
    while total.shape[axis] > 1:
        bit *= 2
        lead = total.shape[:axis]
        pairs = total.reshape(lead + (total.shape[axis] // 2, 2) + total.shape[axis + 1 :])
        keep = lax.index_in_dim(pairs, 0, axis + 1, keepdims=False)
        send = lax.index_in_dim(pairs, 1, axis + 1, keepdims=False)
        total = keep + swap(send.astype(BF), "dp", bit).astype(F32)
    return jnp.squeeze(total, axis)


def norm_backward(values, norm_scale, gain, grad_normed):
    weighted = grad_normed * gain
    inner = jnp.mean(weighted * values, axis=1, keepdims=True)
    grad_values = norm_scale * weighted - values * (norm_scale * norm_scale * norm_scale) * inner
    grad_gain = jnp.sum(grad_normed * values * norm_scale, axis=0)
    return (grad_values, grad_gain)


def rotary_tables(length):
    half = HEAD_DIM // 2
    inverse = ROPE_BASE ** (-2.0 * np.arange(half) / HEAD_DIM)
    angles = np.arange(length)[:, None] * inverse[None, :]
    cosine, sine = np.cos(angles), np.sin(angles)
    return (
        np.concatenate([cosine, cosine, cosine, cosine], axis=1).astype(np.float32),
        np.concatenate([-sine, sine, -sine, sine], axis=1).astype(np.float32),
    )


def body(
    x_in,
    segments,
    chosen,
    out_grad,
    norm1_gain,
    w_query,
    w_key,
    w_value,
    w_out,
    norm2_gain,
    w_router,
    w_gate,
    w_up,
    w_down,
):
    tok_rows, full_width = x_in.shape
    h = HEAD_DIM
    q_width, kv_width = w_query.shape[1], w_key.shape[1]
    groups = q_width // kv_width
    experts_local, _, inner = w_gate.shape
    n_exp, n_dp = lax.axis_size("expert"), lax.axis_size("dp")
    total_experts = experts_local * n_exp
    top_count = chosen.shape[1]
    capacity = tok_rows * top_count * 25 // (16 * total_experts)
    place, side = lax.axis_index("expert"), lax.axis_index("tensor")
    half_width = full_width // lax.axis_size("tensor")
    row_start = place * tok_rows
    seq_length = segments.shape[0]
    half_rows = tok_rows // 2

    own_dp = lax.axis_index("dp")
    order = [1, 3, 2, 0] if n_exp == 4 else [*range(1, n_exp), 0]
    group = n_exp // 2
    vmem = lambda *shape: pltpu.VMEM(shape, BF)
    prefetch = pltpu.PrefetchScalarGridSpec

    tables = [
        lax.dynamic_slice_in_dim(jnp.asarray(table), row_start, tok_rows)
        for table in rotary_tables(seq_length)
    ]
    cosine, sine = tables
    normed_one, query_rot, kv_own, scale_one = pl.pallas_call(
        project_kernel,
        name="project",
        out_shape=(
            shaped(BF, tok_rows, full_width),
            shaped(BF, tok_rows, q_width),
            shaped(BF, tok_rows, 2 * kv_width),
            shaped(F32, tok_rows, 1),
        ),
        compiler_params=params(),
        cost_estimate=cost(2),
    )(x_in, norm1_gain[None], w_query, w_key, w_value, cosine, sine)
    kv_blocks = [kv_own] + [fetch(kv_own, k) for k in range(1, n_exp)]

    turned_segments = lax.dynamic_slice_in_dim(
        jnp.concatenate([segments, segments]), row_start, seq_length
    )
    key_positions = (row_start + jnp.arange(seq_length, dtype=jnp.int32)) % seq_length
    allowed = (turned_segments[:tok_rows, None] == turned_segments[None, :]) & (
        key_positions[:tok_rows, None] >= key_positions[None, :]
    )
    bias = jnp.where(allowed, 0.0, MASKED).astype(F32)
    heads = q_width // h
    out_half = w_out.shape[0] // 2
    own_core = own_dp % 2
    w_near = swap(lax.dynamic_slice_in_dim(w_out, own_core * out_half, out_half), "tensor")
    w_far = swap(w_near, "dp", 1)
    tail_lanes = -(-(total_experts + 1) // 128) * 128
    router_wide = jnp.pad(w_router, ((0, 0), (0, tail_lanes - total_experts)))
    chosen_wide = jnp.pad(chosen, ((0, 0), (0, 128 - top_count)))
    query_rot, router_wide, chosen_wide = lax.optimization_barrier((query_rot, router_wide, chosen_wide))
    attended, attended_low, log_totals = pl.pallas_call(
        functools.partial(attend_kernel, groups, n_exp),
        name="attend",
        out_shape=(
            shaped(F32, tok_rows, q_width),
            shaped(BF, tok_rows, q_width),
            shaped(F32, tok_rows, heads),
        ),
        scratch_shapes=[vmem(seq_length, 2 * kv_width)],
        compiler_params=params(),
        cost_estimate=cost(10),
    )(after(query_rot, w_near), *kv_blocks, bias)

    cot_in, chosen_in = out_grad, chosen
    cot_half = lambda s: lax.dynamic_slice_in_dim(cot_in, s * half_rows, half_rows)
    chosen_half = lambda s: jnp.pad(
        lax.dynamic_slice_in_dim(chosen_in, s * half_rows, half_rows).T.astype(BF),
        ((0, 16 - top_count), (0, full_width - half_rows)),
    )
    payload = lambda s: jnp.concatenate([cot_half(s), chosen_half(s)], axis=0)
    cot_own, cot_other = payload(side), payload(1 - side)
    cot_near = {}
    for k in order:
        cot_near[k] = fetch(after(cot_own, *kv_blocks[1:]), k) if k else cot_own
    expert_slots = n_exp * capacity
    by_expert = lambda *tail: pl.BlockSpec((1,) + tail, lambda e, *_: (e,) + (0,) * len(tail))

    middle_in = (x_in, attended_low, swap(attended_low, "tensor"), w_out, w_near, w_far, norm2_gain[None])
    whole = lambda array: full(*array.shape)
    hidden_one, scale_two, normed_two, normed_own, normed_far = pl.pallas_call(
        middle_kernel,
        name="middle",
        grid_spec=prefetch(
            num_scalar_prefetch=1,
            grid=(1,),
            in_specs=[whole(array) for array in middle_in],
            out_specs=(
                full(tok_rows, full_width),
                full(tok_rows, 1),
                full(tok_rows, full_width),
                full(half_rows, full_width),
                full(half_rows, full_width),
            ),
        ),
        out_shape=(
            shaped(F32, tok_rows, full_width),
            shaped(F32, tok_rows, 1),
            shaped(BF, tok_rows, full_width),
            shaped(BF, half_rows, full_width),
            shaped(BF, half_rows, full_width),
        ),
        compiler_params=params(),
        cost_estimate=cost(2),
    )(jnp.stack([side, own_core]), *middle_in)
    near_rows = {k: fetch(normed_own, k) for k in order[:group]}
    for k in order[group:]:
        near_rows[k] = fetch(after(normed_own, *near_rows.values()), k) if k else normed_own

    cot_pairs = [
        (cot_near[k], swap(after(cot_near[k], normed_own), "tensor") if k else cot_other)
        for k in order
    ]
    chosen_blocks = jnp.stack(
        [
            jnp.concatenate([part[half_rows : half_rows + top_count, :half_rows] for part in pair], axis=1)
            for pair in cot_pairs
        ]
    ).astype(jnp.int32)
    expert_ids = jnp.arange(total_experts, dtype=jnp.int32)
    hot_all = jnp.any(chosen_blocks[:, :, None, :] == expert_ids[:, None], axis=1)
    hot_rows = hot_all.transpose(1, 0, 2).reshape(total_experts, n_exp * tok_rows).astype(F32)
    hot_local = lax.dynamic_slice_in_dim(hot_all, place * experts_local, experts_local, 1)
    token_row = jnp.arange(tok_rows, dtype=jnp.int32)
    before = (token_row[:, None] < token_row[None, :]).astype(BF)
    rank = jnp.einsum("kes,st->ket", hot_local.astype(BF), before, preferred_element_type=F32)
    slot_of = jnp.where(hot_local, rank.astype(jnp.int32), -1)

    cot_slots, raw_grad = pl.pallas_call(
        functools.partial(cotangent_kernel, n_exp, capacity),
        name="cotangent",
        grid=(experts_local,),
        in_specs=[whole(slot_of)]
        + [full(*cot_own.shape)] * (2 * n_exp)
        + [by_expert(inner, full_width)],
        out_specs=(by_expert(expert_slots, full_width), by_expert(expert_slots, inner)),
        out_shape=(
            shaped(BF, experts_local, expert_slots, full_width),
            shaped(F32, experts_local, expert_slots, inner),
        ),
        scratch_shapes=[vmem(n_exp, tok_rows, full_width)],
        compiler_params=params(),
        cost_estimate=cost(13),
    )(slot_of, *[half for pair in cot_pairs for half in pair], w_down)

    far_rows = {
        k: swap(near_rows[k], "tensor") if k else normed_far for k in order
    }

    def run_experts(number, hold):
        ks = order[number * group : (number + 1) * group]
        token_halves = [half for k in ks for half in (near_rows[k], far_rows[k])]
        token_halves[0] = after(token_halves[0], *hold)
        slots_here = group * capacity
        low_slots = shaped(BF, experts_local, slots_here, inner)
        columns = group * tok_rows
        return pl.pallas_call(
            functools.partial(experts_kernel, group, capacity),
            name="experts",
            grid_spec=prefetch(
                num_scalar_prefetch=1,
                grid=(experts_local,),
                in_specs=[full(group, experts_local, tok_rows)]
                + [full(half_rows, full_width)] * (2 * group)
                + [
                    pl.BlockSpec((total_experts, columns), lambda e, *_: (0, number)),
                    full(total_experts, full_width),
                    pl.BlockSpec((1, slots_here, inner), lambda e, *_: (e, number, 0)),
                    by_expert(full_width, inner),
                    by_expert(full_width, inner),
                ],
                out_specs=(
                    by_expert(slots_here, full_width),
                    by_expert(slots_here, inner),
                    by_expert(slots_here, inner),
                    by_expert(slots_here, inner),
                    full(group, half_rows + 16, full_width),
                    full(group, half_rows + 16, full_width),
                ),
                scratch_shapes=[
                    vmem(group, tok_rows, full_width),
                    pltpu.VMEM((total_experts, columns), F32),
                    vmem(group, experts_local * capacity, full_width),
                    vmem(group, experts_local * capacity, tok_rows),
                    pltpu.VMEM((2 * group, full_width), F32),
                ],
            ),
            out_shape=(
                shaped(BF, experts_local, slots_here, full_width),
                low_slots,
                low_slots,
                low_slots,
                shaped(BF, group, half_rows + 16, full_width),
                shaped(BF, group, half_rows + 16, full_width),
            ),
            compiler_params=params(),
            cost_estimate=cost(18),
        )(
            place[None], slot_of[number * group : (number + 1) * group], *token_halves,
            hot_rows, w_router.T, raw_grad, w_gate, w_up,
        )

    first = run_experts(0, [far_rows[k] for k in order[group:]])
    second = run_experts(1, [first[4]])

    def pair_sum(made, got):
        return pl.pallas_call(
            pair_sum_kernel,
            name="pair_sum",
            out_shape=(shaped(BF, half_rows + 16, full_width),) * group,
            compiler_params=params(),
            cost_estimate=cost(1),
        )(made[4], got)

    first_sums = pair_sum(first, swap(first[5], "tensor"))
    second_got = swap(second[5], "tensor")

    out_dims = (n_exp, tok_rows, half_width)

    def combine(*hold):
        return pl.pallas_call(
            functools.partial(combine_kernel, capacity, order),
            name="combine",
            grid_spec=prefetch(
                num_scalar_prefetch=1,
                grid=(experts_local,),
                in_specs=[
                    whole(slot_of),
                    by_expert(group * capacity, inner),
                    by_expert(group * capacity, inner),
                    by_expert(inner, full_width),
                ],
                out_specs=(full(*out_dims), full(*out_dims)),
                scratch_shapes=[
                    vmem(n_exp, experts_local * capacity, full_width),
                    vmem(n_exp, experts_local * capacity, tok_rows),
                ],
            ),
            out_shape=(shaped(BF, *out_dims), shaped(BF, *out_dims)),
            compiler_params=params(),
            cost_estimate=cost(12),
        )(after(jnp.stack([side, place]), *hold), slot_of, first[1], second[1], w_down)

    out_mine, out_else = combine(*first_sums, second[4])
    terms = {k: deliver(first_sums[i], k) for i, k in enumerate(order[:group])}
    second_got, *arrived = lax.optimization_barrier((second_got, out_mine, *terms.values()))
    terms = dict(zip(terms, arrived[1:]))
    second_sums = pair_sum(second, second_got)
    for i, k in enumerate(order[group:]):
        terms[k] = deliver(second_sums[i], k) if k else second_sums[i]
    out_got = swap(after(out_else, second_sums[0]), "tensor")
    out_low = (out_mine.astype(F32) + out_got.astype(F32)).astype(BF)

    slice_width = full_width // n_dp
    pairs = [*first[:4], *second[:4]]
    crossing = 2 if n_dp == 4 and experts_local > 3 and slice_width % 128 == 0 else 0
    summed = experts_local - crossing

    def weights(base, count, outs, *hold):
        some = lambda *tail: pl.BlockSpec((1,) + tail, lambda e, *_: (base + e,) + (0,) * len(tail))
        shape = (n_dp // outs, count, 3, slice_width, inner)
        return pl.pallas_call(
            weights_kernel,
            name="weights",
            grid_spec=prefetch(
                num_scalar_prefetch=1,
                grid=(count,),
                in_specs=[some(expert_slots, full_width)] + [some(*array.shape[1:]) for array in pairs],
                out_specs=(pl.BlockSpec((shape[0], 1) + shape[2:], lambda e, *_: (0, e, 0, 0, 0)),) * outs,
            ),
            out_shape=(shaped(BF, *shape),) * outs,
            compiler_params=params(),
            cost_estimate=cost(12),
        )(after(own_dp[None], *hold), cot_slots, *pairs)

    weight_grads = weights(0, summed, 1, *second_sums)[0]
    keep, send = weights(summed, crossing, 2, weight_grads) if crossing else (second_sums[0],) * 2
    half_sum = pl.pallas_call(
        gather_sum_kernel,
        name="gather_sum",
        out_shape=shaped(BF, half_rows + 16, full_width),
        compiler_params=params(),
        cost_estimate=cost(1),
    )(after(terms[0], weight_grads, keep, out_low), *[terms[k] for k in range(1, n_exp)])
    weight_sum = lax.psum_scatter(
        after(weight_grads, half_sum), "dp", scatter_dimension=0, tiled=False
    )
    half_other = swap(half_sum, "tensor")
    if crossing:
        near = swap(after(send, half_other), "dp", 1)
        half_grads = (keep[1].astype(F32) + near[1].astype(F32)).astype(BF)
    out_home = exchange(after(out_low, half_sum))

    back_in = (
        half_sum, half_other, normed_two, chosen_wide, router_wide, hidden_one, scale_two, norm2_gain[None], out_grad, w_out,
    )
    hidden_grad, branch_cot, gain_two_term, attended_grad, logit_grads = pl.pallas_call(
        functools.partial(norm_grad_kernel, experts_local, top_count),
        name="norm_grad",
        grid_spec=prefetch(
            num_scalar_prefetch=1,
            grid=(1,),
            in_specs=[whole(array) for array in back_in],
            out_specs=(
                full(tok_rows, full_width),
                full(tok_rows, full_width),
                full(tok_rows, full_width),
                full(tok_rows, q_width),
                full(tok_rows, tail_lanes),
            ),
            scratch_shapes=[vmem(tok_rows, full_width), pltpu.VMEM((2, tail_lanes, half_rows), F32)],
        ),
        out_shape=(
            shaped(F32, tok_rows, full_width),
            shaped(BF, tok_rows, full_width),
            shaped(BF, tok_rows, full_width),
            shaped(BF, tok_rows, q_width),
            shaped(BF, tok_rows, tail_lanes),
        ),
        compiler_params=params(),
        cost_estimate=cost(4),
    )(jnp.stack([side, place]), *back_in)

    back_args = (query_rot, *kv_blocks, attended_grad, attended, log_totals, bias)
    query_grads, kv_parts = pl.pallas_call(
        functools.partial(attend_grad_kernel, groups, n_exp),
        name="attend_grad",
        grid_spec=prefetch(
            num_scalar_prefetch=1,
            grid=(1,),
            in_specs=[whole(array) for array in back_args],
            out_specs=(full(tok_rows, q_width), full(n_exp, 2 * kv_width, tok_rows)),
            scratch_shapes=[vmem(seq_length, 2 * kv_width)],
        ),
        out_shape=(shaped(F32, tok_rows, q_width), shaped(BF, n_exp, 2 * kv_width, tok_rows)),
        compiler_params=params(),
        cost_estimate=cost(10),
    )(place[None], *back_args)
    kv_terms = exchange(after(kv_parts, out_home))

    slice_rows = full_width // (n_dp * n_exp)

    def slices_of(kernel, name, width, more, *arrays):
        dims = (n_exp, n_dp // 2, slice_rows, width)
        return pl.pallas_call(
            kernel,
            name=name,
            grid_spec=prefetch(
                num_scalar_prefetch=1,
                grid=(1,),
                in_specs=[whole(array) for array in arrays],
                out_specs=(full(*dims), full(*dims)) + tuple(full(*dim) for dim in more),
                scratch_shapes=[pltpu.VMEM((full_width, width), F32)],
            ),
            out_shape=(shaped(BF, *dims), shaped(BF, *dims)) + tuple(shaped(BF, *dim) for dim in more),
            compiler_params=params(),
            cost_estimate=cost(5),
        )(own_dp[None], *arrays)

    early_keep, early_send, query_low = slices_of(
        early_kernel, "early", 2 * q_width + tail_lanes, [(tok_rows, q_width)],
        branch_cot, attended_low, normed_two, logit_grads, gain_two_term, normed_one, query_grads, cosine, sine,
    )
    early = near_sum(early_keep, early_send).astype(BF)
    if crossing:
        kv_terms, half_grads = lax.optimization_barrier((kv_terms, half_grads))
        far = swap(half_grads, "dp", 2)
    kv_terms, early = lax.optimization_barrier((kv_terms, early))
    grads_low, partial_low, gain_one_term = pl.pallas_call(
        input_kernel,
        name="input",
        out_shape=(
            shaped(BF, tok_rows, 2 * kv_width),
            shaped(BF, tok_rows, full_width),
            shaped(F32, 16, full_width),
        ),
        compiler_params=params(),
        cost_estimate=cost(4),
    )(query_low, kv_terms, cosine, sine, w_query, w_key, w_value, x_in, scale_one)
    partial_other = swap(partial_low, "tensor")
    late_keep, late_send = slices_of(
        late_kernel, "late", 2 * kv_width + 128, (), normed_one, grads_low, gain_one_term, swap(gain_one_term, "tensor")
    )
    late = near_sum(late_keep, late_send).astype(BF)
    early = place_sum(early)
    if crossing:
        partial_other, far = lax.optimization_barrier((partial_other, far))
    late, partial_other, early = lax.optimization_barrier((late, partial_other, early))
    late_parts = exchange(late)
    early = far_sum(early, 0)

    def finish(base, count, totals, specs, earlier):
        some = lambda *tail: pl.BlockSpec((1,) + tail, lambda e: (base + e,) + (0,) * len(tail))
        return pl.pallas_call(
            functools.partial(finish_kernel, len(totals)),
            name="finish",
            grid=(count,),
            in_specs=specs + [pl.BlockSpec(memory_space=pl.ANY)] * len(earlier),
            out_specs=(some(slice_width, inner), some(slice_width, inner), some(inner, slice_width)),
            out_shape=(
                shaped(F32, experts_local, slice_width, inner),
                shaped(F32, experts_local, slice_width, inner),
                shaped(F32, experts_local, inner, slice_width),
            ),
            input_output_aliases={len(totals) + i: i for i in range(len(earlier))},
            compiler_params=params(),
            cost_estimate=cost(3),
        )(*totals, *earlier)

    one = by_expert(3, slice_width, inner)
    finals = ()
    if crossing:
        lead = pl.BlockSpec((1, 1, 3, slice_width, inner), lambda e: (0, e, 0, 0, 0))
        finals = finish(summed, crossing, (keep, near, far), [lead, lead, one], ())
    grad_gate, grad_up, grad_down = finish(0, summed, (weight_sum,), [one], finals)
    late = far_sum(jnp.sum(after(late_parts, grad_gate).astype(F32), axis=0), 0)

    mixture_half = jnp.sum(out_home.astype(F32), axis=0)
    mixture_half = jnp.where(side == 0, mixture_half, jnp.roll(mixture_half, half_rows, axis=0))
    residual_half = lax.dynamic_slice_in_dim(hidden_one, side * half_width, half_width, 1)
    block_out = (residual_half + mixture_half).astype(BF)

    normed_one_grad = partial_low.astype(F32) + partial_other.astype(F32)
    inputs = x_in.astype(F32)
    input_part, _ = norm_backward(inputs, scale_one, norm1_gain, normed_one_grad)
    input_grad = hidden_grad + input_part
    gain_one = late[:, -1]
    return (
        block_out,
        input_grad,
        gain_one,
        early[:, q_width + tail_lanes :],
        late[:, :kv_width],
        late[:, kv_width : 2 * kv_width],
        early[:, :q_width].T,
        early[:, q_width + tail_lanes - 1],
        early[:, q_width : q_width + total_experts],
        grad_gate,
        grad_up,
        grad_down,
    )


def solution(mesh):
    return jax.shard_map(
        body,
        mesh=mesh,
        in_specs=(
            P(("dp", "expert"), None),
            P("dp"),
            P(("dp", "expert"), None),
            P(("dp", "expert"), None),
            P(),
            P(None, "tensor"),
            P(None, "tensor"),
            P(None, "tensor"),
            P("tensor", None),
            P(),
            P(),
            P("expert", None, "tensor"),
            P("expert", None, "tensor"),
            P("expert", "tensor", None),
        ),
        out_specs=(
            P(("dp", "expert"), "tensor"),
            P(("dp", "expert"), None),
            P(("dp", "expert")),
            P(("dp", "expert"), "tensor"),
            P(("dp", "expert"), "tensor"),
            P(("dp", "expert"), "tensor"),
            P("tensor", ("dp", "expert")),
            P(("dp", "expert")),
            P(("dp", "expert"), None),
            P("expert", "dp", "tensor"),
            P("expert", "dp", "tensor"),
            P("expert", "tensor", "dp"),
        ),
        check_vma=False,
    )
```

```python
import functools

import jax
import jax.numpy as jnp
import numpy as np
from jax import lax
from jax.experimental import pallas as pl
from jax.experimental.pallas import tpu as pltpu
from jax.sharding import PartitionSpec as P

HEAD_DIM = 64
EPSILON = 1e-05
ROPE_BASE = 10000.0
MASKED = -1e30
BF = jnp.bfloat16
F32 = jnp.float32
MIB = 1024 * 1024


def swap(values, axis, bit=1):
    count = lax.axis_size(axis)
    return lax.ppermute(values, axis, [(i, i ^ bit) for i in range(count)])


def fetch(values, offset):
    count = lax.axis_size("expert")
    return lax.ppermute(values, "expert", [(i, (i - offset) % count) for i in range(count)])


def deliver(values, offset):
    count = lax.axis_size("expert")
    return lax.ppermute(values, "expert", [(i, (i + offset) % count) for i in range(count)])


def halve(parts, bit_axis, bit):
    pairs = parts.reshape((parts.shape[0] // 2, 2) + parts.shape[1:])
    own = (lax.axis_index(bit_axis) // bit) % 2
    keep = lax.dynamic_index_in_dim(pairs, own, 1, keepdims=False)
    send = lax.dynamic_index_in_dim(pairs, 1 - own, 1, keepdims=False)
    got = swap(send, bit_axis, bit)
    return keep.astype(F32) + got.astype(F32)


def sum_over_dp(parts):
    bit = 1
    while parts.shape[0] > 1:
        parts = halve(parts.astype(BF), "dp", bit)
        bit *= 2
    return parts[0]


def exchange(parts):
    return lax.all_to_all(parts, "expert", split_axis=0, concat_axis=0, tiled=True)


def nn(left, right):
    return jnp.dot(left, right, preferred_element_type=F32)


def nt(left, right):
    return lax.dot_general(left, right, (((1,), (1,)), ((), ())), preferred_element_type=F32)


def tn(left, right):
    return lax.dot_general(left, right, (((0,), (0,)), ((), ())), preferred_element_type=F32)


def params(mib=60):
    return pltpu.CompilerParams(vmem_limit_bytes=mib * MIB)


def cost(micros):
    return pl.CostEstimate(flops=int(micros * 1e3), bytes_accessed=0, transcendentals=0)


def shaped(kind, *dims):
    return jax.ShapeDtypeStruct(dims, kind)


def full(*shape):
    return pl.BlockSpec(shape, lambda *_: (0,) * len(shape))


def after(values, *others):
    return lax.optimization_barrier((values,) + others)[0]


def turned(values, cosine, sine):
    lane = lax.broadcasted_iota(jnp.int32, values.shape, 1)
    quarter = HEAD_DIM // 2
    later = pltpu.roll(values, 2 * HEAD_DIM - quarter, 1)
    earlier = pltpu.roll(values, quarter, 1)
    return values * cosine + jnp.where(lane % HEAD_DIM < quarter, later, earlier) * sine


def project_kernel(x_ref, gain_ref, wq_ref, wk_ref, wv_ref, cos_ref, sin_ref, n_ref, q_ref, kv_ref, s_ref):
    values = x_ref[...].astype(F32)
    scale = lax.rsqrt(jnp.mean(values * values, axis=1, keepdims=True) + EPSILON)
    s_ref[...] = scale
    normed = (values * scale * gain_ref[...]).astype(BF)
    n_ref[...] = normed
    cosine, sine = cos_ref[...], sin_ref[...]
    lanes = 2 * HEAD_DIM
    kv = wk_ref.shape[1]
    keys = nn(normed, wk_ref[...])
    for i in range(0, kv, lanes):
        kv_ref[:, i : i + lanes] = turned(keys[:, i : i + lanes], cosine, sine).astype(BF)
    kv_ref[:, kv:] = nn(normed, wv_ref[...]).astype(BF)
    query = nn(normed, wq_ref[...])
    for i in range(0, query.shape[1], lanes):
        q_ref[:, i : i + lanes] = turned(query[:, i : i + lanes], cosine, sine).astype(BF)


def attend_kernel(groups, blocks, *refs):
    q_ref, kv_refs, bias_ref = refs[0], refs[1 : 1 + blocks], refs[1 + blocks]
    o_ref, low_ref, lse_ref, kv_ref = refs[2 + blocks :]
    h = HEAD_DIM
    rows = kv_refs[0].shape[0]
    for k in range(blocks):
        kv_ref[k * rows : (k + 1) * rows, :] = kv_refs[k][...]
    heads = kv_ref.shape[1] // (2 * h)
    for kv in range(heads):
        key = kv_ref[:, kv * h : kv * h + h]
        value = kv_ref[:, (heads + kv) * h : (heads + kv) * h + h]
        for g in range(groups):
            head = kv * groups + g
            span = slice(head * h, head * h + h)
            scores = nt(q_ref[:, span], key) * h**-0.5 + bias_ref[...]
            peak = jnp.max(scores, axis=1, keepdims=True)
            raw = jnp.exp(scores - peak)
            total = jnp.sum(raw, axis=1, keepdims=True)
            out = nn((raw * (1.0 / total)).astype(BF), value)
            o_ref[:, span] = out
            low_ref[:, span] = out.astype(BF)
            lse_ref[:, head : head + 1] = peak + jnp.log(total)


def attend_grad_kernel(groups, blocks, place_ref, *refs):
    q_ref, kv_refs, d_ref, o_ref, lse_ref, bias_ref = refs[0], refs[1 : 1 + blocks], *refs[1 + blocks : 5 + blocks]
    dq_ref, dkv_ref, kv_ref = refs[5 + blocks :]
    h = HEAD_DIM
    rows = kv_refs[0].shape[0]
    for k in range(blocks):
        kv_ref[k * rows : (k + 1) * rows, :] = kv_refs[k][...]
    heads = kv_ref.shape[1] // (2 * h)
    for kv in range(heads):
        key = kv_ref[:, kv * h : kv * h + h]
        value = kv_ref[:, (heads + kv) * h : (heads + kv) * h + h]
        key_grad = value_grad = None
        for g in range(groups):
            head = kv * groups + g
            span = slice(head * h, head * h + h)
            query = q_ref[:, span]
            cot = d_ref[:, span]
            scores = nt(query, key) * h**-0.5 + bias_ref[...]
            probs = jnp.exp(scores - lse_ref[:, head : head + 1])
            delta = jnp.sum(cot.astype(F32) * o_ref[:, span], axis=1, keepdims=True)
            slope = (probs * (nt(cot, value) - delta)).astype(BF)
            value_part = tn(cot, probs.astype(BF))
            key_part = tn(query, slope)
            dq_ref[:, span] = nn(slope, key) * h**-0.5
            value_grad = value_part if value_grad is None else value_grad + value_part
            key_grad = key_part if key_grad is None else key_grad + key_part
        key_low = (key_grad * h**-0.5).astype(BF)
        value_low = value_grad.astype(BF)
        for k in range(blocks):
            to = lax.rem(place_ref[0] + k, blocks)
            dkv_ref[to, kv * h : kv * h + h, :] = key_low[:, k * rows : (k + 1) * rows]
            dkv_ref[to, (heads + kv) * h : (heads + kv) * h + h, :] = value_low[:, k * rows : (k + 1) * rows]


def middle_kernel(
    side_ref, x_ref, mine_ref, other_ref, w_ref, w_near, w_far, gain_ref, h_ref, s_ref, n_ref, own_ref, far_ref
):
    part = w_near.shape[0]
    hidden = x_ref[...].astype(F32) + nn(mine_ref[...], w_ref[...])
    for w, number in ((w_near, side_ref[1]), (w_far, 1 - side_ref[1])):
        hidden += nn(other_ref[:, pl.ds(pl.multiple_of(number * part, part), part)], w[...])
    h_ref[...] = hidden
    scale = lax.rsqrt(jnp.mean(hidden * hidden, axis=1, keepdims=True) + EPSILON)
    s_ref[...] = scale
    n_ref[...] = (hidden * scale * gain_ref[...]).astype(BF)
    half = own_ref.shape[0]
    own_ref[...] = n_ref[pl.ds(pl.multiple_of(side_ref[0] * half, half), half), :]
    far_ref[...] = n_ref[pl.ds(pl.multiple_of((1 - side_ref[0]) * half, half), half), :]


def make_pick(slot_ref, k, expert, slots):
    row = slot_ref[k, pl.ds(expert, 1), :]
    lines = lax.broadcasted_iota(jnp.int32, (slots, row.shape[1]), 0)
    return jnp.where(lines == row, 1.0, 0.0)


def cotangent_kernel(blocks, slots, *refs):
    slot_ref, halves, wd_ref = refs[0], refs[1 : 1 + 2 * blocks], refs[1 + 2 * blocks]
    cg_ref, dm_ref, x_ref = refs[2 + 2 * blocks :]
    half = x_ref.shape[1] // 2
    step = pl.program_id(0)

    @pl.when(step == 0)
    def _():
        for k in range(blocks):
            x_ref[k, :half, :] = halves[2 * k][:half, :]
            x_ref[k, half:, :] = halves[2 * k + 1][:half, :]

    for k in range(blocks):
        pick = make_pick(slot_ref, k, step, slots).astype(BF)
        cg_ref[0, k * slots : (k + 1) * slots, :] = nn(pick, x_ref[k]).astype(BF)
    dm_ref[0] = nt(cg_ref[0], wd_ref[0])


def split_rows(values):
    line = lax.broadcasted_iota(jnp.int32, (16, values[0].shape[1]), 0)
    out = jnp.zeros(line.shape, F32)
    for i, value in enumerate(values):
        high = value.astype(BF).astype(F32)
        out = jnp.where(line == 2 * i, high, jnp.where(line == 2 * i + 1, value - high, out))
    return out.astype(BF)


def pair_sum_kernel(mine_ref, got_ref, *outs):
    half = mine_ref.shape[1] - 16
    for k, out in enumerate(outs):
        total = mine_ref[k].astype(F32) + got_ref[k].astype(F32)
        out[:half, :] = total[:half].astype(BF)
        out[half:, :] = split_rows([total[half : half + 1] + total[half + 1 : half + 2]])


def gather_sum_kernel(*refs):
    parts, out = refs[:-1], refs[-1]
    half = out.shape[0] - 16
    total = parts[0][...].astype(F32)
    rows = [total[half : half + 1] + total[half + 1 : half + 2]]
    total = total[:half]
    for part in parts[1:]:
        more = part[...].astype(F32)
        total = total + more[:half]
        rows.append(more[half : half + 1] + more[half + 1 : half + 2])
    out[:half, :] = total.astype(BF)
    out[half:, :] = split_rows(rows)


def experts_kernel(blocks, slots, place_ref, slot_ref, *refs):
    halves, (hot_ref, router_ref, dm_ref, wg_ref, wu_ref) = refs[: 2 * blocks], refs[2 * blocks : 5 + 2 * blocks]
    (xg_ref, gm_ref, da_ref, db_ref, mine_ref, else_ref,
     x_ref, gates_ref, n_ref, pick_ref, dg_ref) = refs[5 + 2 * blocks :]
    rows = x_ref.shape[1]
    half = rows // 2
    step, steps = pl.program_id(0), pl.num_programs(0)

    @pl.when(step == 0)
    def _():
        for k in range(blocks):
            x_ref[k, :half, :] = halves[2 * k][...]
            x_ref[k, half:, :] = halves[2 * k + 1][...]
        tokens = x_ref[...].reshape(blocks * rows, x_ref.shape[2])
        hot = hot_ref[...] > 0.0
        logits = jnp.where(hot, nt(router_ref[...], tokens), MASKED)
        raw = jnp.where(hot, jnp.exp(logits - jnp.max(logits, axis=0, keepdims=True)), 0.0)
        gates_ref[...] = raw / jnp.sum(raw, axis=0, keepdims=True)
        dg_ref[...] = jnp.zeros_like(dg_ref)

    gate_row = gates_ref[pl.ds(place_ref[0] * steps + step, 1), :]
    at = pl.multiple_of(step * slots, slots)
    gate_parts, picks = [], []
    for k in range(blocks):
        pick = make_pick(slot_ref, k, step, slots)
        picks.append(pick)
        low = pick.astype(BF)
        pick_ref[k, pl.ds(at, slots), :] = low
        xg_ref[0, k * slots : (k + 1) * slots, :] = nn(low, x_ref[k]).astype(BF)
        gate_parts.append(jnp.sum(pick * gate_row[:, k * rows : (k + 1) * rows], axis=1, keepdims=True))
    gates = jnp.concatenate(gate_parts, axis=0)
    own = xg_ref[0]
    gate_pre = nn(own, wg_ref[0])
    up_pre = nn(own, wu_ref[0])
    raw_grad = dm_ref[0]
    sigmoid = 1.0 / (1.0 + jnp.exp(-gate_pre))
    swish = gate_pre * sigmoid
    active = swish * up_pre
    dgate = jnp.sum(active * raw_grad, axis=1, keepdims=True)
    gm_ref[0] = (gates * active).astype(BF)
    grad = gates * raw_grad
    da = (grad * up_pre * sigmoid * (1.0 + gate_pre * (1.0 - sigmoid))).astype(BF)
    db = (grad * swish).astype(BF)
    da_ref[0] = da
    db_ref[0] = db
    low = (nt(da, wg_ref[0]) + nt(db, wu_ref[0])).astype(BF)
    for k in range(blocks):
        part = slice(k * slots, (k + 1) * slots)
        n_ref[k, pl.ds(at, slots), :] = low[part]
        dg_row = jnp.sum(picks[k] * dgate[part], axis=0, keepdims=True)
        lanes = pl.ds(pl.multiple_of(step * half, half), half)
        dg_ref[2 * k : 2 * k + 1, lanes] = dg_row[:, :half]
        dg_ref[2 * k + 1 : 2 * k + 2, lanes] = dg_row[:, half:]

    @pl.when(step == steps - 1)
    def _():
        for k in range(blocks):
            out = tn(pick_ref[k], n_ref[k]).astype(BF)
            mine_ref[k, :half, :] = out[:half]
            else_ref[k, :half, :] = out[half:]
            mine_ref[k, half:, :] = split_rows([dg_ref[2 * k : 2 * k + 1, :]])
            else_ref[k, half:, :] = split_rows([dg_ref[2 * k + 1 : 2 * k + 2, :]])


def weights_kernel(own_ref, cg_ref, *refs):
    pairs, outs = refs[:8], refs[8:]
    count, width = len(outs) * outs[0].shape[0], outs[0].shape[3]
    split = pairs[0].shape[1]
    for number in range(count):
        if len(outs) == 1:
            out, place, span = outs[0], number, slice(number * width, (number + 1) * width)
        else:
            out, place = outs[number % 2], number // 2
            span = pl.ds(pl.multiple_of((own_ref[0] ^ number) * width, 128), width)
        gate = up = down = None
        for i in range(2):
            xg_ref, gm_ref, da_ref, db_ref = pairs[4 * i : 4 * i + 4]
            rows = xg_ref[0, :, span]
            cots = cg_ref[0, i * split : (i + 1) * split, span]
            parts = tn(rows, da_ref[0]), tn(rows, db_ref[0]), tn(cots, gm_ref[0])
            gate, up, down = parts if i == 0 else (gate + parts[0], up + parts[1], down + parts[2])
        out[place, 0, 0] = gate.astype(BF)
        out[place, 0, 1] = up.astype(BF)
        out[place, 0, 2] = down.astype(BF)


def finish_kernel(parts, *refs):
    gate_ref, up_ref, down_ref = refs[-3:]
    total = None
    for ref in refs[:parts]:
        term = ref[(0,) * (len(ref.shape) - 3)].astype(F32)
        total = term if total is None else total + term
    gate_ref[0] = total[0]
    up_ref[0] = total[1]
    down_ref[0] = total[2].T


def combine_kernel(slots, offsets, where_ref, slot_ref, ga_ref, gb_ref, wd_ref, mine_ref, else_ref, r_ref, pick_ref):
    blocks = mine_ref.shape[0]
    group = blocks // 2
    step, steps = pl.program_id(0), pl.num_programs(0)
    at = pl.multiple_of(step * slots, slots)
    for i, ref in enumerate((ga_ref, gb_ref)):
        low = nn(ref[0], wd_ref[0]).astype(BF)
        for j in range(group):
            k = i * group + j
            r_ref[k, pl.ds(at, slots), :] = low[j * slots : (j + 1) * slots]
            pick_ref[k, pl.ds(at, slots), :] = make_pick(slot_ref, k, step, slots).astype(BF)

    @pl.when(step == steps - 1)
    def _():
        width = mine_ref.shape[2]
        half = mine_ref.shape[1] // 2
        own = pl.ds(pl.multiple_of(where_ref[0] * width, width), width)
        far = pl.ds(pl.multiple_of((1 - where_ref[0]) * width, width), width)
        for k in range(blocks):
            to = lax.rem(where_ref[1] + offsets[k], blocks)
            mine_ref[to] = tn(pick_ref[k], r_ref[k, :, own]).astype(BF)
            out = tn(pick_ref[k], r_ref[k, :, far]).astype(BF)
            else_ref[to, :half] = out[half:]
            else_ref[to, half:] = out[:half]


def norm_grad_kernel(
    local, top, where_ref, own_ref, far_ref, n_ref, chosen_ref, router_ref, h_ref, s_ref, gain_ref, c_ref, w_ref,
    grad_ref, low_ref, term_ref, do_ref, dl_ref, e_ref, g_ref,
):
    side, place = where_ref[0], where_ref[1]
    half = own_ref.shape[0] - 16
    lanes = router_ref.shape[1]
    sources = 4
    g_ref[...] = jnp.zeros_like(g_ref)
    for part, ref in ((side, own_ref), (1 - side, far_ref)):
        e_ref[pl.ds(pl.multiple_of(part * half, half), half), :] = ref[:half, :]
        tail = ref[half:, :].astype(F32)
        for k in range(sources):
            row = tail[2 * k : 2 * k + 1] + tail[2 * k + 1 : 2 * k + 2]
            source = lax.rem(place + sources - k, sources)
            for e in range(local):
                g_ref[part, pl.ds(source * local + e, 1), :] = row[:, e * half : (e + 1) * half]
    dgate = jnp.concatenate([g_ref[0].T, g_ref[1].T], axis=0)
    lane = lax.broadcasted_iota(jnp.int32, dgate.shape, 1)
    hot = chosen_ref[:, 0:1] == lane
    for i in range(1, top):
        hot = hot | (chosen_ref[:, i : i + 1] == lane)
    logits = jnp.where(hot, nn(n_ref[...], router_ref[...]), MASKED)
    raw = jnp.where(hot, jnp.exp(logits - jnp.max(logits, axis=1, keepdims=True)), 0.0)
    gates = raw / jnp.sum(raw, axis=1, keepdims=True)
    logit_grads = (gates * (dgate - jnp.sum(gates * dgate, axis=1, keepdims=True))).astype(BF)
    dl_ref[...] = logit_grads
    grad = nt(logit_grads, router_ref[...]) + e_ref[...].astype(F32)
    hidden, scale = h_ref[...], s_ref[...]
    term_ref[...] = (grad * hidden * scale).astype(BF)
    weighted = grad * gain_ref[...]
    inner = jnp.mean(weighted * hidden, axis=1, keepdims=True)
    total = scale * weighted - hidden * (scale * scale * scale) * inner + c_ref[...].astype(F32)
    grad_ref[...] = total
    low = total.astype(BF)
    low_ref[...] = low
    do_ref[...] = nt(low, w_ref[...]).astype(BF)


def place_direct(own, blocks_z, scratch, keep_ref, send_ref):
    blocks, rows, _ = keep_ref.shape
    core = lax.rem(own, 2)
    for out, bit in ((keep_ref, core), (send_ref, 1 - core)):
        for number in range(blocks):
            at = ((2 * (number // blocks_z) + bit) * blocks_z + number % blocks_z) * rows
            out[number] = scratch[pl.ds(pl.multiple_of(at, 8), rows), :].astype(BF)


def place_slices(own, scratch, keep_ref, send_ref):
    blocks, pairs, rows, _ = keep_ref.shape
    for a in range(2 * pairs):
        out = send_ref if a % 2 else keep_ref
        for b in range(blocks):
            number = (own ^ a) * blocks + b
            out[b, a // 2] = scratch[pl.ds(pl.multiple_of(number * rows, 8), rows), :].astype(BF)


def early_kernel(
    where_ref, low_ref, o_ref, n_ref, dl_ref, term_ref, first_ref, dq_ref, cos_ref, sin_ref,
    keep_ref, send_ref, turned_ref, scratch,
):
    width, lanes = o_ref.shape[1], 2 * HEAD_DIM
    tail = dl_ref.shape[1]
    for i in range(0, width, lanes):
        turned_ref[:, i : i + lanes] = turned(dq_ref[:, i : i + lanes], cos_ref[...], -sin_ref[...]).astype(BF)
    scratch[:, :width] = tn(low_ref[...], o_ref[...])
    lane = lax.broadcasted_iota(jnp.int32, dl_ref.shape, 1)
    ones = jnp.where(lane == tail - 1, 1.0, 0.0).astype(BF)
    scratch[:, width : width + tail] = tn(n_ref[...], dl_ref[...]) + tn(term_ref[...], ones)
    scratch[:, width + tail :] = tn(first_ref[...], turned_ref[...])
    place_slices(where_ref[0], scratch, keep_ref, send_ref)


def input_kernel(dq_ref, kv_ref, cos_ref, sin_ref, wq_ref, wk_ref, wv_ref, x_ref, s_ref,
                 grads_ref, part_ref, term_ref):
    lanes = 2 * HEAD_DIM
    kv_width = wk_ref.shape[1]
    total = jnp.sum(kv_ref[...].astype(F32), axis=0).T
    for i in range(0, kv_width, lanes):
        grads_ref[:, i : i + lanes] = turned(total[:, i : i + lanes], cos_ref[...], -sin_ref[...]).astype(BF)
    grads_ref[:, kv_width:] = total[:, kv_width:].astype(BF)
    part = (
        nt(dq_ref[...], wq_ref[...])
        + nt(grads_ref[:, :kv_width], wk_ref[...])
        + nt(grads_ref[:, kv_width:], wv_ref[...])
    )
    part_ref[...] = part.astype(BF)
    term = jnp.sum(part * x_ref[...].astype(F32) * s_ref[...], axis=0, keepdims=True)
    line = lax.broadcasted_iota(jnp.int32, term_ref.shape, 0)
    term_ref[...] = jnp.where(line == 0, term, 0.0)


def late_kernel(blocks_z, where_ref, n_ref, grads_ref, term_ref, other_ref, keep_ref, send_ref, scratch):
    width = grads_ref.shape[1]
    scratch[:, :width] = tn(n_ref[...], grads_ref[...])
    ones = jnp.ones((term_ref.shape[0], scratch.shape[1] - width), BF)
    scratch[:, width:] = tn((term_ref[...] + other_ref[...]).astype(BF), ones)
    place_direct(where_ref[0], blocks_z, scratch, keep_ref, send_ref)


def near_sum(keep, send):
    return keep.astype(F32) + swap(send, "dp", 1).astype(F32)


def place_sum(total):
    return jnp.sum(exchange(total.astype(BF)).astype(F32), axis=0)


def far_sum(total, axis):
    bit = 1
    while total.shape[axis] > 1:
        bit *= 2
        lead = total.shape[:axis]
        pairs = total.reshape(lead + (total.shape[axis] // 2, 2) + total.shape[axis + 1 :])
        keep = lax.index_in_dim(pairs, 0, axis + 1, keepdims=False)
        send = lax.index_in_dim(pairs, 1, axis + 1, keepdims=False)
        total = keep + swap(send.astype(BF), "dp", bit).astype(F32)
    return jnp.squeeze(total, axis)


def norm_backward(values, norm_scale, gain, grad_normed):
    weighted = grad_normed * gain
    inner = jnp.mean(weighted * values, axis=1, keepdims=True)
    grad_values = norm_scale * weighted - values * (norm_scale * norm_scale * norm_scale) * inner
    grad_gain = jnp.sum(grad_normed * values * norm_scale, axis=0)
    return (grad_values, grad_gain)


def rotary_tables(length):
    half = HEAD_DIM // 2
    inverse = ROPE_BASE ** (-2.0 * np.arange(half) / HEAD_DIM)
    angles = np.arange(length)[:, None] * inverse[None, :]
    cosine, sine = np.cos(angles), np.sin(angles)
    return (
        np.concatenate([cosine, cosine, cosine, cosine], axis=1).astype(np.float32),
        np.concatenate([-sine, sine, -sine, sine], axis=1).astype(np.float32),
    )


def body(
    x_in,
    segments,
    chosen,
    out_grad,
    norm1_gain,
    w_query,
    w_key,
    w_value,
    w_out,
    norm2_gain,
    w_router,
    w_gate,
    w_up,
    w_down,
):
    tok_rows, full_width = x_in.shape
    h = HEAD_DIM
    q_width, kv_width = w_query.shape[1], w_key.shape[1]
    groups = q_width // kv_width
    experts_local, _, inner = w_gate.shape
    n_exp, n_dp = lax.axis_size("expert"), lax.axis_size("dp")
    total_experts = experts_local * n_exp
    top_count = chosen.shape[1]
    capacity = tok_rows * top_count * 25 // (16 * total_experts)
    place, side = lax.axis_index("expert"), lax.axis_index("tensor")
    half_width = full_width // lax.axis_size("tensor")
    row_start = place * tok_rows
    seq_length = segments.shape[0]
    half_rows = tok_rows // 2

    own_dp = lax.axis_index("dp")
    order = [1, 3, 2, 0] if n_exp == 4 else [*range(1, n_exp), 0]
    group = n_exp // 2
    vmem = lambda *shape: pltpu.VMEM(shape, BF)
    prefetch = pltpu.PrefetchScalarGridSpec

    tables = [
        lax.dynamic_slice_in_dim(jnp.asarray(table), row_start, tok_rows)
        for table in rotary_tables(seq_length)
    ]
    cosine, sine = tables
    normed_one, query_rot, kv_own, scale_one = pl.pallas_call(
        project_kernel,
        name="project",
        out_shape=(
            shaped(BF, tok_rows, full_width),
            shaped(BF, tok_rows, q_width),
            shaped(BF, tok_rows, 2 * kv_width),
            shaped(F32, tok_rows, 1),
        ),
        compiler_params=params(),
        cost_estimate=cost(2),
    )(x_in, norm1_gain[None], w_query, w_key, w_value, cosine, sine)
    kv_blocks = [kv_own] + [fetch(kv_own, k) for k in range(1, n_exp)]

    turned_segments = lax.dynamic_slice_in_dim(
        jnp.concatenate([segments, segments]), row_start, seq_length
    )
    key_positions = (row_start + jnp.arange(seq_length, dtype=jnp.int32)) % seq_length
    allowed = (turned_segments[:tok_rows, None] == turned_segments[None, :]) & (
        key_positions[:tok_rows, None] >= key_positions[None, :]
    )
    bias = jnp.where(allowed, 0.0, MASKED).astype(F32)
    heads = q_width // h
    out_half = w_out.shape[0] // 2
    own_core = own_dp % 2
    w_near = swap(lax.dynamic_slice_in_dim(w_out, own_core * out_half, out_half), "tensor")
    w_far = swap(w_near, "dp", 1)
    tail_lanes = -(-(total_experts + 1) // 128) * 128
    router_wide = jnp.pad(w_router, ((0, 0), (0, tail_lanes - total_experts)))
    chosen_wide = jnp.pad(chosen, ((0, 0), (0, 128 - top_count)))
    query_rot, router_wide, chosen_wide = lax.optimization_barrier((query_rot, router_wide, chosen_wide))
    attended, attended_low, log_totals = pl.pallas_call(
        functools.partial(attend_kernel, groups, n_exp),
        name="attend",
        out_shape=(
            shaped(F32, tok_rows, q_width),
            shaped(BF, tok_rows, q_width),
            shaped(F32, tok_rows, heads),
        ),
        scratch_shapes=[vmem(seq_length, 2 * kv_width)],
        compiler_params=params(),
        cost_estimate=cost(10),
    )(after(query_rot, w_near), *kv_blocks, bias)

    cot_in, chosen_in = out_grad, chosen
    cot_half = lambda s: lax.dynamic_slice_in_dim(cot_in, s * half_rows, half_rows)
    chosen_half = lambda s: jnp.pad(
        lax.dynamic_slice_in_dim(chosen_in, s * half_rows, half_rows).T.astype(BF),
        ((0, 16 - top_count), (0, full_width - half_rows)),
    )
    payload = lambda s: jnp.concatenate([cot_half(s), chosen_half(s)], axis=0)
    cot_own, cot_other = payload(side), payload(1 - side)
    cot_near = {}
    for k in order:
        cot_near[k] = fetch(after(cot_own, *kv_blocks[1:]), k) if k else cot_own
    expert_slots = n_exp * capacity
    by_expert = lambda *tail: pl.BlockSpec((1,) + tail, lambda e, *_: (e,) + (0,) * len(tail))

    middle_in = (x_in, attended_low, swap(attended_low, "tensor"), w_out, w_near, w_far, norm2_gain[None])
    whole = lambda array: full(*array.shape)
    hidden_one, scale_two, normed_two, normed_own, normed_far = pl.pallas_call(
        middle_kernel,
        name="middle",
        grid_spec=prefetch(
            num_scalar_prefetch=1,
            grid=(1,),
            in_specs=[whole(array) for array in middle_in],
            out_specs=(
                full(tok_rows, full_width),
                full(tok_rows, 1),
                full(tok_rows, full_width),
                full(half_rows, full_width),
                full(half_rows, full_width),
            ),
        ),
        out_shape=(
            shaped(F32, tok_rows, full_width),
            shaped(F32, tok_rows, 1),
            shaped(BF, tok_rows, full_width),
            shaped(BF, half_rows, full_width),
            shaped(BF, half_rows, full_width),
        ),
        compiler_params=params(),
        cost_estimate=cost(2),
    )(jnp.stack([side, own_core]), *middle_in)
    near_rows = {k: fetch(normed_own, k) for k in order[:group]}
    for k in order[group:]:
        near_rows[k] = fetch(after(normed_own, *near_rows.values()), k) if k else normed_own

    cot_pairs = [
        (cot_near[k], swap(after(cot_near[k], normed_own), "tensor") if k else cot_other)
        for k in order
    ]
    chosen_blocks = jnp.stack(
        [
            jnp.concatenate([part[half_rows : half_rows + top_count, :half_rows] for part in pair], axis=1)
            for pair in cot_pairs
        ]
    ).astype(jnp.int32)
    expert_ids = jnp.arange(total_experts, dtype=jnp.int32)
    hot_all = jnp.any(chosen_blocks[:, :, None, :] == expert_ids[:, None], axis=1)
    hot_rows = hot_all.transpose(1, 0, 2).reshape(total_experts, n_exp * tok_rows).astype(F32)
    hot_local = lax.dynamic_slice_in_dim(hot_all, place * experts_local, experts_local, 1)
    token_row = jnp.arange(tok_rows, dtype=jnp.int32)
    before = (token_row[:, None] < token_row[None, :]).astype(BF)
    rank = jnp.einsum("kes,st->ket", hot_local.astype(BF), before, preferred_element_type=F32)
    slot_of = jnp.where(hot_local, rank.astype(jnp.int32), -1)

    cot_slots, raw_grad = pl.pallas_call(
        functools.partial(cotangent_kernel, n_exp, capacity),
        name="cotangent",
        grid=(experts_local,),
        in_specs=[whole(slot_of)]
        + [full(*cot_own.shape)] * (2 * n_exp)
        + [by_expert(inner, full_width)],
        out_specs=(by_expert(expert_slots, full_width), by_expert(expert_slots, inner)),
        out_shape=(
            shaped(BF, experts_local, expert_slots, full_width),
            shaped(F32, experts_local, expert_slots, inner),
        ),
        scratch_shapes=[vmem(n_exp, tok_rows, full_width)],
        compiler_params=params(),
        cost_estimate=cost(13),
    )(slot_of, *[half for pair in cot_pairs for half in pair], w_down)

    far_rows = {
        k: swap(near_rows[k], "tensor") if k else normed_far for k in order
    }

    def run_experts(number, hold):
        ks = order[number * group : (number + 1) * group]
        token_halves = [half for k in ks for half in (near_rows[k], far_rows[k])]
        token_halves[0] = after(token_halves[0], *hold)
        slots_here = group * capacity
        low_slots = shaped(BF, experts_local, slots_here, inner)
        columns = group * tok_rows
        return pl.pallas_call(
            functools.partial(experts_kernel, group, capacity),
            name="experts",
            grid_spec=prefetch(
                num_scalar_prefetch=1,
                grid=(experts_local,),
                in_specs=[full(group, experts_local, tok_rows)]
                + [full(half_rows, full_width)] * (2 * group)
                + [
                    pl.BlockSpec((total_experts, columns), lambda e, *_: (0, number)),
                    full(total_experts, full_width),
                    pl.BlockSpec((1, slots_here, inner), lambda e, *_: (e, number, 0)),
                    by_expert(full_width, inner),
                    by_expert(full_width, inner),
                ],
                out_specs=(
                    by_expert(slots_here, full_width),
                    by_expert(slots_here, inner),
                    by_expert(slots_here, inner),
                    by_expert(slots_here, inner),
                    full(group, half_rows + 16, full_width),
                    full(group, half_rows + 16, full_width),
                ),
                scratch_shapes=[
                    vmem(group, tok_rows, full_width),
                    pltpu.VMEM((total_experts, columns), F32),
                    vmem(group, experts_local * capacity, full_width),
                    vmem(group, experts_local * capacity, tok_rows),
                    pltpu.VMEM((2 * group, full_width), F32),
                ],
            ),
            out_shape=(
                shaped(BF, experts_local, slots_here, full_width),
                low_slots,
                low_slots,
                low_slots,
                shaped(BF, group, half_rows + 16, full_width),
                shaped(BF, group, half_rows + 16, full_width),
            ),
            compiler_params=params(),
            cost_estimate=cost(18),
        )(
            place[None], slot_of[number * group : (number + 1) * group], *token_halves,
            hot_rows, w_router.T, raw_grad, w_gate, w_up,
        )

    first = run_experts(0, [far_rows[k] for k in order[group:]])
    second = run_experts(1, [first[4]])

    def pair_sum(made, got):
        return pl.pallas_call(
            pair_sum_kernel,
            name="pair_sum",
            out_shape=(shaped(BF, half_rows + 16, full_width),) * group,
            compiler_params=params(24),
            cost_estimate=cost(1),
        )(made[4], got)

    first_sums = pair_sum(first, swap(first[5], "tensor"))
    second_got = swap(second[5], "tensor")

    out_dims = (n_exp, tok_rows, half_width)

    def combine(*hold):
        return pl.pallas_call(
            functools.partial(combine_kernel, capacity, order),
            name="combine",
            grid_spec=prefetch(
                num_scalar_prefetch=1,
                grid=(experts_local,),
                in_specs=[
                    whole(slot_of),
                    by_expert(group * capacity, inner),
                    by_expert(group * capacity, inner),
                    by_expert(inner, full_width),
                ],
                out_specs=(full(*out_dims), full(*out_dims)),
                scratch_shapes=[
                    vmem(n_exp, experts_local * capacity, full_width),
                    vmem(n_exp, experts_local * capacity, tok_rows),
                ],
            ),
            out_shape=(shaped(BF, *out_dims), shaped(BF, *out_dims)),
            compiler_params=params(),
            cost_estimate=cost(12),
        )(after(jnp.stack([side, place]), *hold), slot_of, first[1], second[1], w_down)

    slice_width = full_width // n_dp
    pairs = [*first[:4], *second[:4]]
    crossing = 0
    summed = experts_local - crossing

    def weights(base, count, outs, *hold):
        some = lambda *tail: pl.BlockSpec((1,) + tail, lambda e, *_: (base + e,) + (0,) * len(tail))
        shape = (n_dp // outs, count, 3, slice_width, inner)
        return pl.pallas_call(
            weights_kernel,
            name="weights",
            grid_spec=prefetch(
                num_scalar_prefetch=1,
                grid=(count,),
                in_specs=[some(expert_slots, full_width)] + [some(*array.shape[1:]) for array in pairs],
                out_specs=(pl.BlockSpec((shape[0], 1) + shape[2:], lambda e, *_: (0, e, 0, 0, 0)),) * outs,
            ),
            out_shape=(shaped(BF, *shape),) * outs,
            compiler_params=params(),
            cost_estimate=cost(12),
        )(after(own_dp[None], *hold), cot_slots, *pairs)

    early_experts = summed // 4
    out_mine, out_else = combine(*first_sums, second[4])
    first_grads = weights(0, early_experts, 1, out_mine)[0]
    terms = {k: deliver(first_sums[i], k) for i, k in enumerate(order[:group])}
    second_got, *arrived = lax.optimization_barrier((second_got, first_grads, *terms.values()))
    terms = dict(zip(terms, arrived[1:]))
    second_sums = pair_sum(second, second_got)
    for i, k in enumerate(order[group:]):
        terms[k] = deliver(second_sums[i], k) if k else second_sums[i]
    out_got = swap(after(out_else, second_sums[0]), "tensor")
    out_low = (out_mine.astype(F32) + out_got.astype(F32)).astype(BF)

    first_sum = lax.psum_scatter(
        after(first_grads, *second_sums), "dp", scatter_dimension=0, tiled=False
    )
    weight_grads = weights(early_experts, summed - early_experts, 1, *second_sums)[0]
    keep, send = weights(summed, crossing, 2, weight_grads) if crossing else (second_sums[0],) * 2
    half_sum = pl.pallas_call(
        gather_sum_kernel,
        name="gather_sum",
        out_shape=shaped(BF, half_rows + 16, full_width),
        compiler_params=params(24),
        cost_estimate=cost(1),
    )(after(terms[0], weight_grads, keep, out_low), *[terms[k] for k in range(1, n_exp)])
    weight_sum = lax.psum_scatter(
        after(weight_grads, half_sum), "dp", scatter_dimension=0, tiled=False
    )
    half_other = swap(half_sum, "tensor")
    if crossing:
        near = swap(after(send, half_other), "dp", 1)
        half_grads = (keep[1].astype(F32) + near[1].astype(F32)).astype(BF)
    out_home = exchange(after(out_low, half_sum))

    back_in = (
        half_sum, half_other, normed_two, chosen_wide, router_wide, hidden_one, scale_two, norm2_gain[None], out_grad, w_out,
    )
    hidden_grad, branch_cot, gain_two_term, attended_grad, logit_grads = pl.pallas_call(
        functools.partial(norm_grad_kernel, experts_local, top_count),
        name="norm_grad",
        grid_spec=prefetch(
            num_scalar_prefetch=1,
            grid=(1,),
            in_specs=[whole(array) for array in back_in],
            out_specs=(
                full(tok_rows, full_width),
                full(tok_rows, full_width),
                full(tok_rows, full_width),
                full(tok_rows, q_width),
                full(tok_rows, tail_lanes),
            ),
            scratch_shapes=[vmem(tok_rows, full_width), pltpu.VMEM((2, tail_lanes, half_rows), F32)],
        ),
        out_shape=(
            shaped(F32, tok_rows, full_width),
            shaped(BF, tok_rows, full_width),
            shaped(BF, tok_rows, full_width),
            shaped(BF, tok_rows, q_width),
            shaped(BF, tok_rows, tail_lanes),
        ),
        compiler_params=params(),
        cost_estimate=cost(4),
    )(jnp.stack([side, place]), *back_in)

    back_args = (query_rot, *kv_blocks, attended_grad, attended, log_totals, bias)
    query_grads, kv_parts = pl.pallas_call(
        functools.partial(attend_grad_kernel, groups, n_exp),
        name="attend_grad",
        grid_spec=prefetch(
            num_scalar_prefetch=1,
            grid=(1,),
            in_specs=[whole(array) for array in back_args],
            out_specs=(full(tok_rows, q_width), full(n_exp, 2 * kv_width, tok_rows)),
            scratch_shapes=[vmem(seq_length, 2 * kv_width)],
        ),
        out_shape=(shaped(F32, tok_rows, q_width), shaped(BF, n_exp, 2 * kv_width, tok_rows)),
        compiler_params=params(),
        cost_estimate=cost(10),
    )(place[None], *back_args)
    kv_terms = exchange(after(kv_parts, out_home))

    slice_rows = full_width // (n_dp * n_exp)

    def slices_of(kernel, name, width, more, *arrays):
        dims = (n_exp, n_dp // 2, slice_rows, width)
        dims = dims if more else (n_exp * n_dp // 2, slice_rows, width)
        return pl.pallas_call(
            kernel,
            name=name,
            grid_spec=prefetch(
                num_scalar_prefetch=1,
                grid=(1,),
                in_specs=[whole(array) for array in arrays],
                out_specs=(full(*dims), full(*dims)) + tuple(full(*dim) for dim in more),
                scratch_shapes=[pltpu.VMEM((full_width, width), F32)],
            ),
            out_shape=(shaped(BF, *dims), shaped(BF, *dims)) + tuple(shaped(BF, *dim) for dim in more),
            compiler_params=params(),
            cost_estimate=cost(5),
        )(own_dp[None], *arrays)

    early_keep, early_send, query_low = slices_of(
        early_kernel, "early", 2 * q_width + tail_lanes, [(tok_rows, q_width)],
        branch_cot, attended_low, normed_two, logit_grads, gain_two_term, normed_one, query_grads, cosine, sine,
    )
    early = near_sum(early_keep, early_send).astype(BF)
    if crossing:
        kv_terms, half_grads = lax.optimization_barrier((kv_terms, half_grads))
        far = swap(half_grads, "dp", 2)
    kv_terms, early = lax.optimization_barrier((kv_terms, early))
    grads_low, partial_low, gain_one_term = pl.pallas_call(
        input_kernel,
        name="input",
        out_shape=(
            shaped(BF, tok_rows, 2 * kv_width),
            shaped(BF, tok_rows, full_width),
            shaped(F32, 16, full_width),
        ),
        compiler_params=params(),
        cost_estimate=cost(4),
    )(query_low, kv_terms, cosine, sine, w_query, w_key, w_value, x_in, scale_one)
    partial_other = swap(partial_low, "tensor")
    late_keep, late_send = slices_of(
        functools.partial(late_kernel, n_exp), "late", 2 * kv_width + 128, (), normed_one, grads_low, gain_one_term, swap(gain_one_term, "tensor")
    )
    late_send, partial_other = lax.optimization_barrier((late_send, partial_other))
    late = near_sum(late_keep, late_send).astype(BF)
    early = place_sum(early)
    if crossing:
        partial_other, far = lax.optimization_barrier((partial_other, far))
    late, partial_other, early = lax.optimization_barrier((late, partial_other, early))
    same_core = [
        [dp * n_exp + z for dp in range(core, n_dp, 2) for z in range(n_exp)] for core in range(2)
    ]
    late_parts = lax.all_to_all(
        late, ("dp", "expert"), split_axis=0, concat_axis=0, tiled=True, axis_index_groups=same_core
    )
    early = far_sum(early, 0)

    def finish(base, count, totals, specs, earlier):
        some = lambda *tail: pl.BlockSpec((1,) + tail, lambda e: (base + e,) + (0,) * len(tail))
        return pl.pallas_call(
            functools.partial(finish_kernel, len(totals)),
            name="finish",
            grid=(count,),
            in_specs=specs + [pl.BlockSpec(memory_space=pl.ANY)] * len(earlier),
            out_specs=(some(slice_width, inner), some(slice_width, inner), some(inner, slice_width)),
            out_shape=(
                shaped(F32, experts_local, slice_width, inner),
                shaped(F32, experts_local, slice_width, inner),
                shaped(F32, experts_local, inner, slice_width),
            ),
            input_output_aliases={len(totals) + i: i for i in range(len(earlier))},
            compiler_params=params(),
            cost_estimate=cost(3),
        )(*totals, *earlier)

    one = by_expert(3, slice_width, inner)
    finals = ()
    if crossing:
        lead = pl.BlockSpec((1, 1, 3, slice_width, inner), lambda e: (0, e, 0, 0, 0))
        finals = finish(summed, crossing, (keep, near, far), [lead, lead, one], ())
    finals = finish(0, early_experts, (after(first_sum, partial_other),), [one], finals)
    grad_gate, grad_up, grad_down = finish(
        early_experts, summed - early_experts, (weight_sum,), [one], finals
    )
    late = jnp.sum(after(late_parts, grad_gate).astype(F32), axis=0)

    mixture_half = jnp.sum(out_home.astype(F32), axis=0)
    mixture_half = jnp.where(side == 0, mixture_half, jnp.roll(mixture_half, half_rows, axis=0))
    residual_half = lax.dynamic_slice_in_dim(hidden_one, side * half_width, half_width, 1)
    block_out = (residual_half + mixture_half).astype(BF)

    normed_one_grad = partial_low.astype(F32) + partial_other.astype(F32)
    inputs = x_in.astype(F32)
    input_part, _ = norm_backward(inputs, scale_one, norm1_gain, normed_one_grad)
    input_grad = hidden_grad + input_part
    gain_one = late[:, -1]
    return (
        block_out,
        input_grad,
        gain_one,
        early[:, q_width + tail_lanes :],
        late[:, :kv_width],
        late[:, kv_width : 2 * kv_width],
        early[:, :q_width].T,
        early[:, q_width + tail_lanes - 1],
        early[:, q_width : q_width + total_experts],
        grad_gate,
        grad_up,
        grad_down,
    )


def solution(mesh):
    return jax.shard_map(
        body,
        mesh=mesh,
        in_specs=(
            P(("dp", "expert"), None),
            P("dp"),
            P(("dp", "expert"), None),
            P(("dp", "expert"), None),
            P(),
            P(None, "tensor"),
            P(None, "tensor"),
            P(None, "tensor"),
            P("tensor", None),
            P(),
            P(),
            P("expert", None, "tensor"),
            P("expert", None, "tensor"),
            P("expert", "tensor", None),
        ),
        out_specs=(
            P(("dp", "expert"), "tensor"),
            P(("dp", "expert"), None),
            P(("dp", "expert")),
            P(("dp", "expert"), "tensor"),
            P(("dp", "expert"), "tensor"),
            P(("dp", "expert"), "tensor"),
            P("tensor", ("dp", "expert")),
            P(("dp", "expert")),
            P(("dp", "expert"), None),
            P("expert", "dp", "tensor"),
            P("expert", "dp", "tensor"),
            P("expert", "tensor", "dp"),
        ),
        check_vma=False,
    )
```

```python
import functools

import jax
import jax.numpy as jnp
import numpy as np
from jax import lax
from jax.experimental import pallas as pl
from jax.experimental.pallas import tpu as pltpu
from jax.sharding import PartitionSpec as P

HEAD_DIM = 64
EPSILON = 1e-05
ROPE_BASE = 10000.0
MASKED = -1e30
BF = jnp.bfloat16
F32 = jnp.float32
MIB = 1024 * 1024


def swap(values, axis, bit=1):
    count = lax.axis_size(axis)
    return lax.ppermute(values, axis, [(i, i ^ bit) for i in range(count)])


def fetch(values, offset):
    count = lax.axis_size("expert")
    return lax.ppermute(values, "expert", [(i, (i - offset) % count) for i in range(count)])


def deliver(values, offset):
    count = lax.axis_size("expert")
    return lax.ppermute(values, "expert", [(i, (i + offset) % count) for i in range(count)])


def halve(parts, bit_axis, bit):
    pairs = parts.reshape((parts.shape[0] // 2, 2) + parts.shape[1:])
    own = (lax.axis_index(bit_axis) // bit) % 2
    keep = lax.dynamic_index_in_dim(pairs, own, 1, keepdims=False)
    send = lax.dynamic_index_in_dim(pairs, 1 - own, 1, keepdims=False)
    got = swap(send, bit_axis, bit)
    return keep.astype(F32) + got.astype(F32)


def sum_over_dp(parts):
    bit = 1
    while parts.shape[0] > 1:
        parts = halve(parts.astype(BF), "dp", bit)
        bit *= 2
    return parts[0]


def exchange(parts):
    return lax.all_to_all(parts, "expert", split_axis=0, concat_axis=0, tiled=True)


def nn(left, right):
    return jnp.dot(left, right, preferred_element_type=F32)


def nt(left, right):
    return lax.dot_general(left, right, (((1,), (1,)), ((), ())), preferred_element_type=F32)


def tn(left, right):
    return lax.dot_general(left, right, (((0,), (0,)), ((), ())), preferred_element_type=F32)


def params(mib=60):
    return pltpu.CompilerParams(vmem_limit_bytes=mib * MIB)


def cost(micros):
    return pl.CostEstimate(flops=int(micros * 1e3), bytes_accessed=0, transcendentals=0)


def shaped(kind, *dims):
    return jax.ShapeDtypeStruct(dims, kind)


def full(*shape):
    return pl.BlockSpec(shape, lambda *_: (0,) * len(shape))


def after(values, *others):
    return lax.optimization_barrier((values,) + others)[0]


def turned(values, cosine, sine):
    lane = lax.broadcasted_iota(jnp.int32, values.shape, 1)
    quarter = HEAD_DIM // 2
    later = pltpu.roll(values, 2 * HEAD_DIM - quarter, 1)
    earlier = pltpu.roll(values, quarter, 1)
    return values * cosine + jnp.where(lane % HEAD_DIM < quarter, later, earlier) * sine


def project_kernel(x_ref, gain_ref, wq_ref, wk_ref, wv_ref, cos_ref, sin_ref, n_ref, q_ref, kv_ref, s_ref):
    values = x_ref[...].astype(F32)
    scale = lax.rsqrt(jnp.mean(values * values, axis=1, keepdims=True) + EPSILON)
    s_ref[...] = scale
    normed = (values * scale * gain_ref[...]).astype(BF)
    n_ref[...] = normed
    cosine, sine = cos_ref[...], sin_ref[...]
    lanes = 2 * HEAD_DIM
    kv = wk_ref.shape[1]
    keys = nn(normed, wk_ref[...])
    for i in range(0, kv, lanes):
        kv_ref[:, i : i + lanes] = turned(keys[:, i : i + lanes], cosine, sine).astype(BF)
    kv_ref[:, kv:] = nn(normed, wv_ref[...]).astype(BF)
    query = nn(normed, wq_ref[...])
    for i in range(0, query.shape[1], lanes):
        q_ref[:, i : i + lanes] = turned(query[:, i : i + lanes], cosine, sine).astype(BF)


def attend_kernel(groups, blocks, *refs):
    q_ref, kv_refs, bias_ref = refs[0], refs[1 : 1 + blocks], refs[1 + blocks]
    o_ref, low_ref, lse_ref, kv_ref = refs[2 + blocks :]
    h = HEAD_DIM
    rows = kv_refs[0].shape[0]
    for k in range(blocks):
        kv_ref[k * rows : (k + 1) * rows, :] = kv_refs[k][...]
    heads = kv_ref.shape[1] // (2 * h)
    for kv in range(heads):
        key = kv_ref[:, kv * h : kv * h + h]
        value = kv_ref[:, (heads + kv) * h : (heads + kv) * h + h]
        for g in range(groups):
            head = kv * groups + g
            span = slice(head * h, head * h + h)
            scores = nt(q_ref[:, span] * h**-0.5, key) + bias_ref[...]
            peak = jnp.max(scores, axis=1, keepdims=True)
            raw = jnp.exp(scores - peak)
            total = jnp.sum(raw, axis=1, keepdims=True)
            out = nn((raw * (1.0 / total)).astype(BF), value)
            o_ref[:, span] = out
            low_ref[:, span] = out.astype(BF)
            lse_ref[:, head : head + 1] = peak + jnp.log(total)


def attend_grad_kernel(groups, blocks, place_ref, *refs):
    q_ref, kv_refs, d_ref, o_ref, lse_ref, bias_ref = refs[0], refs[1 : 1 + blocks], *refs[1 + blocks : 5 + blocks]
    dq_ref, dkv_ref, kv_ref = refs[5 + blocks :]
    h = HEAD_DIM
    rows = kv_refs[0].shape[0]
    for k in range(blocks):
        kv_ref[k * rows : (k + 1) * rows, :] = kv_refs[k][...]
    heads = kv_ref.shape[1] // (2 * h)
    for kv in range(heads):
        key = kv_ref[:, kv * h : kv * h + h]
        value = kv_ref[:, (heads + kv) * h : (heads + kv) * h + h]
        key_grad = value_grad = None
        for g in range(groups):
            head = kv * groups + g
            span = slice(head * h, head * h + h)
            query = q_ref[:, span] * h**-0.5
            cot = d_ref[:, span]
            scores = nt(query, key) + bias_ref[...]
            probs = jnp.exp(scores - lse_ref[:, head : head + 1])
            delta = jnp.sum(cot.astype(F32) * o_ref[:, span], axis=1, keepdims=True)
            slope = (probs * (nt(cot, value) - delta)).astype(BF)
            value_part = tn(cot, probs.astype(BF))
            key_part = tn(query, slope)
            dq_ref[:, span] = nn(slope, key) * h**-0.5
            value_grad = value_part if value_grad is None else value_grad + value_part
            key_grad = key_part if key_grad is None else key_grad + key_part
        key_low = key_grad.astype(BF)
        value_low = value_grad.astype(BF)
        for k in range(blocks):
            to = lax.rem(place_ref[0] + k, blocks)
            dkv_ref[to, kv * h : kv * h + h, :] = key_low[:, k * rows : (k + 1) * rows]
            dkv_ref[to, (heads + kv) * h : (heads + kv) * h + h, :] = value_low[:, k * rows : (k + 1) * rows]


def middle_kernel(
    side_ref, x_ref, mine_ref, other_ref, w_ref, w_near, w_far, gain_ref, h_ref, s_ref, n_ref, own_ref, far_ref
):
    part = w_near.shape[0]
    hidden = x_ref[...].astype(F32) + nn(mine_ref[...], w_ref[...])
    for w, number in ((w_near, side_ref[1]), (w_far, 1 - side_ref[1])):
        hidden += nn(other_ref[:, pl.ds(pl.multiple_of(number * part, part), part)], w[...])
    h_ref[...] = hidden
    scale = lax.rsqrt(jnp.mean(hidden * hidden, axis=1, keepdims=True) + EPSILON)
    s_ref[...] = scale
    n_ref[...] = (hidden * scale * gain_ref[...]).astype(BF)
    half = own_ref.shape[0]
    own_ref[...] = n_ref[pl.ds(pl.multiple_of(side_ref[0] * half, half), half), :]
    far_ref[...] = n_ref[pl.ds(pl.multiple_of((1 - side_ref[0]) * half, half), half), :]


def make_pick(slot_ref, k, expert, slots):
    row = slot_ref[k, pl.ds(expert, 1), :]
    lines = lax.broadcasted_iota(jnp.int32, (slots, row.shape[1]), 0)
    return jnp.where(lines == row, 1.0, 0.0)


def cotangent_kernel(blocks, slots, *refs):
    slot_ref, halves, wd_ref = refs[0], refs[1 : 1 + 2 * blocks], refs[1 + 2 * blocks]
    cg_ref, dm_ref, x_ref = refs[2 + 2 * blocks :]
    half = x_ref.shape[1] // 2
    step = pl.program_id(0)

    @pl.when(step == 0)
    def _():
        for k in range(blocks):
            x_ref[k, :half, :] = halves[2 * k][:half, :]
            x_ref[k, half:, :] = halves[2 * k + 1][:half, :]

    for k in range(blocks):
        pick = make_pick(slot_ref, k, step, slots).astype(BF)
        cg_ref[0, k * slots : (k + 1) * slots, :] = nn(pick, x_ref[k]).astype(BF)
    dm_ref[0] = nt(cg_ref[0], wd_ref[0])


def split_rows(values):
    line = lax.broadcasted_iota(jnp.int32, (16, values[0].shape[1]), 0)
    out = jnp.zeros(line.shape, F32)
    for i, value in enumerate(values):
        high = value.astype(BF).astype(F32)
        out = jnp.where(line == 2 * i, high, jnp.where(line == 2 * i + 1, value - high, out))
    return out.astype(BF)


def pair_sum_kernel(mine_ref, got_ref, *outs):
    half = mine_ref.shape[1] - 16
    for k, out in enumerate(outs):
        total = mine_ref[k].astype(F32) + got_ref[k].astype(F32)
        out[:half, :] = total[:half].astype(BF)
        out[half:, :] = split_rows([total[half : half + 1] + total[half + 1 : half + 2]])


def gather_sum_kernel(*refs):
    parts, out = refs[:-1], refs[-1]
    half = out.shape[0] - 16
    total = parts[0][...].astype(F32)
    rows = [total[half : half + 1] + total[half + 1 : half + 2]]
    total = total[:half]
    for part in parts[1:]:
        more = part[...].astype(F32)
        total = total + more[:half]
        rows.append(more[half : half + 1] + more[half + 1 : half + 2])
    out[:half, :] = total.astype(BF)
    out[half:, :] = split_rows(rows)


def experts_kernel(blocks, slots, place_ref, slot_ref, *refs):
    halves, (hot_ref, router_ref, dm_ref, wg_ref, wu_ref) = refs[: 2 * blocks], refs[2 * blocks : 5 + 2 * blocks]
    (xg_ref, gm_ref, da_ref, db_ref, mine_ref, else_ref,
     x_ref, gates_ref, n_ref, pick_ref, dg_ref) = refs[5 + 2 * blocks :]
    rows = x_ref.shape[1]
    half = rows // 2
    step, steps = pl.program_id(0), pl.num_programs(0)

    @pl.when(step == 0)
    def _():
        for k in range(blocks):
            x_ref[k, :half, :] = halves[2 * k][...]
            x_ref[k, half:, :] = halves[2 * k + 1][...]
        tokens = x_ref[...].reshape(blocks * rows, x_ref.shape[2])
        hot = hot_ref[...] > 0.0
        logits = jnp.where(hot, nt(router_ref[...], tokens), MASKED)
        raw = jnp.where(hot, jnp.exp(logits - jnp.max(logits, axis=0, keepdims=True)), 0.0)
        gates_ref[...] = raw / jnp.sum(raw, axis=0, keepdims=True)
        dg_ref[...] = jnp.zeros_like(dg_ref)

    gate_row = gates_ref[pl.ds(place_ref[0] * steps + step, 1), :]
    at = pl.multiple_of(step * slots, slots)
    gate_parts, picks = [], []
    for k in range(blocks):
        pick = make_pick(slot_ref, k, step, slots)
        picks.append(pick)
        low = pick.astype(BF)
        pick_ref[k, pl.ds(at, slots), :] = low
        xg_ref[0, k * slots : (k + 1) * slots, :] = nn(low, x_ref[k]).astype(BF)
        gate_parts.append(jnp.sum(pick * gate_row[:, k * rows : (k + 1) * rows], axis=1, keepdims=True))
    gates = jnp.concatenate(gate_parts, axis=0)
    own = xg_ref[0]
    gate_pre = nn(own, wg_ref[0])
    up_pre = nn(own, wu_ref[0])
    raw_grad = dm_ref[0]
    sigmoid = 1.0 / (1.0 + jnp.exp(-gate_pre))
    swish = gate_pre * sigmoid
    active = swish * up_pre
    dgate = jnp.sum(active * raw_grad, axis=1, keepdims=True)
    gm_ref[0] = (gates * active).astype(BF)
    grad = gates * raw_grad
    da = (grad * up_pre * sigmoid * (1.0 + gate_pre * (1.0 - sigmoid))).astype(BF)
    db = (grad * swish).astype(BF)
    da_ref[0] = da
    db_ref[0] = db
    low = (nt(da, wg_ref[0]) + nt(db, wu_ref[0])).astype(BF)
    for k in range(blocks):
        part = slice(k * slots, (k + 1) * slots)
        n_ref[k, pl.ds(at, slots), :] = low[part]
        dg_row = jnp.sum(picks[k] * dgate[part], axis=0, keepdims=True)
        lanes = pl.ds(pl.multiple_of(step * half, half), half)
        dg_ref[2 * k : 2 * k + 1, lanes] = dg_row[:, :half]
        dg_ref[2 * k + 1 : 2 * k + 2, lanes] = dg_row[:, half:]

    @pl.when(step == steps - 1)
    def _():
        for k in range(blocks):
            out = tn(pick_ref[k], n_ref[k]).astype(BF)
            mine_ref[k, :half, :] = out[:half]
            else_ref[k, :half, :] = out[half:]
            mine_ref[k, half:, :] = split_rows([dg_ref[2 * k : 2 * k + 1, :]])
            else_ref[k, half:, :] = split_rows([dg_ref[2 * k + 1 : 2 * k + 2, :]])


def weights_kernel(own_ref, cg_ref, *refs):
    pairs, outs = refs[:8], refs[8:]
    count, width = len(outs) * outs[0].shape[0], outs[0].shape[3]
    split = pairs[0].shape[1]
    for number in range(count):
        if len(outs) == 1:
            out, place, span = outs[0], number, slice(number * width, (number + 1) * width)
        else:
            out, place = outs[number % 2], number // 2
            span = pl.ds(pl.multiple_of((own_ref[0] ^ number) * width, 128), width)
        gate = up = down = None
        for i in range(2):
            xg_ref, gm_ref, da_ref, db_ref = pairs[4 * i : 4 * i + 4]
            rows = xg_ref[0, :, span]
            cots = cg_ref[0, i * split : (i + 1) * split, span]
            parts = tn(rows, da_ref[0]), tn(rows, db_ref[0]), tn(cots, gm_ref[0])
            gate, up, down = parts if i == 0 else (gate + parts[0], up + parts[1], down + parts[2])
        out[place, 0, 0] = gate.astype(BF)
        out[place, 0, 1] = up.astype(BF)
        out[place, 0, 2] = down.astype(BF)


def finish_kernel(parts, *refs):
    gate_ref, up_ref, down_ref = refs[-3:]
    total = None
    for ref in refs[:parts]:
        term = ref[(0,) * (len(ref.shape) - 3)].astype(F32)
        total = term if total is None else total + term
    gate_ref[0] = total[0]
    up_ref[0] = total[1]
    down_ref[0] = total[2].T


def combine_kernel(slots, offsets, where_ref, slot_ref, ga_ref, gb_ref, wd_ref, mine_ref, else_ref, r_ref, pick_ref):
    blocks = mine_ref.shape[0]
    group = blocks // 2
    step, steps = pl.program_id(0), pl.num_programs(0)
    at = pl.multiple_of(step * slots, slots)
    for i, ref in enumerate((ga_ref, gb_ref)):
        low = nn(ref[0], wd_ref[0]).astype(BF)
        for j in range(group):
            k = i * group + j
            r_ref[k, pl.ds(at, slots), :] = low[j * slots : (j + 1) * slots]
            pick_ref[k, pl.ds(at, slots), :] = make_pick(slot_ref, k, step, slots).astype(BF)

    @pl.when(step == steps - 1)
    def _():
        width = mine_ref.shape[2]
        half = mine_ref.shape[1] // 2
        own = pl.ds(pl.multiple_of(where_ref[0] * width, width), width)
        far = pl.ds(pl.multiple_of((1 - where_ref[0]) * width, width), width)
        for k in range(blocks):
            to = lax.rem(where_ref[1] + offsets[k], blocks)
            mine_ref[to] = tn(pick_ref[k], r_ref[k, :, own]).astype(BF)
            out = tn(pick_ref[k], r_ref[k, :, far]).astype(BF)
            else_ref[to, :half] = out[half:]
            else_ref[to, half:] = out[:half]


def norm_grad_kernel(
    local, top, where_ref, own_ref, far_ref, n_ref, chosen_ref, router_ref, h_ref, s_ref, gain_ref, c_ref, w_ref,
    grad_ref, low_ref, term_ref, do_ref, dl_ref, e_ref, g_ref,
):
    side, place = where_ref[0], where_ref[1]
    half = own_ref.shape[0] - 16
    lanes = router_ref.shape[1]
    sources = 4
    g_ref[...] = jnp.zeros_like(g_ref)
    for part, ref in ((side, own_ref), (1 - side, far_ref)):
        e_ref[pl.ds(pl.multiple_of(part * half, half), half), :] = ref[:half, :]
        tail = ref[half:, :].astype(F32)
        for k in range(sources):
            row = tail[2 * k : 2 * k + 1] + tail[2 * k + 1 : 2 * k + 2]
            source = lax.rem(place + sources - k, sources)
            for e in range(local):
                g_ref[part, pl.ds(source * local + e, 1), :] = row[:, e * half : (e + 1) * half]
    dgate = jnp.concatenate([g_ref[0].T, g_ref[1].T], axis=0)
    lane = lax.broadcasted_iota(jnp.int32, dgate.shape, 1)
    hot = chosen_ref[:, 0:1] == lane
    for i in range(1, top):
        hot = hot | (chosen_ref[:, i : i + 1] == lane)
    logits = jnp.where(hot, nn(n_ref[...], router_ref[...]), MASKED)
    raw = jnp.where(hot, jnp.exp(logits - jnp.max(logits, axis=1, keepdims=True)), 0.0)
    gates = raw / jnp.sum(raw, axis=1, keepdims=True)
    logit_grads = (gates * (dgate - jnp.sum(gates * dgate, axis=1, keepdims=True))).astype(BF)
    dl_ref[...] = logit_grads
    grad = nt(logit_grads, router_ref[...]) + e_ref[...].astype(F32)
    hidden, scale = h_ref[...], s_ref[...]
    term_ref[...] = (grad * hidden * scale).astype(BF)
    weighted = grad * gain_ref[...]
    inner = jnp.mean(weighted * hidden, axis=1, keepdims=True)
    total = scale * weighted - hidden * (scale * scale * scale) * inner + c_ref[...].astype(F32)
    grad_ref[...] = total
    low = total.astype(BF)
    low_ref[...] = low
    do_ref[...] = nt(low, w_ref[...]).astype(BF)


def place_direct(own, blocks_z, scratch, keep_ref, send_ref):
    blocks, rows, _ = keep_ref.shape
    core = lax.rem(own, 2)
    for out, bit in ((keep_ref, core), (send_ref, 1 - core)):
        for number in range(blocks):
            at = ((2 * (number // blocks_z) + bit) * blocks_z + number % blocks_z) * rows
            out[number] = scratch[pl.ds(pl.multiple_of(at, 8), rows), :].astype(BF)


def place_slices(own, scratch, keep_ref, send_ref):
    blocks, pairs, rows, _ = keep_ref.shape
    for a in range(2 * pairs):
        out = send_ref if a % 2 else keep_ref
        for b in range(blocks):
            number = (own ^ a) * blocks + b
            out[b, a // 2] = scratch[pl.ds(pl.multiple_of(number * rows, 8), rows), :].astype(BF)


def early_kernel(
    where_ref, low_ref, o_ref, n_ref, dl_ref, term_ref, first_ref, dq_ref, cos_ref, sin_ref,
    keep_ref, send_ref, turned_ref, scratch,
):
    width, lanes = o_ref.shape[1], 2 * HEAD_DIM
    tail = dl_ref.shape[1]
    for i in range(0, width, lanes):
        turned_ref[:, i : i + lanes] = turned(dq_ref[:, i : i + lanes], cos_ref[...], -sin_ref[...]).astype(BF)
    scratch[:, :width] = tn(low_ref[...], o_ref[...])
    lane = lax.broadcasted_iota(jnp.int32, dl_ref.shape, 1)
    ones = jnp.where(lane == tail - 1, 1.0, 0.0).astype(BF)
    scratch[:, width : width + tail] = tn(n_ref[...], dl_ref[...]) + tn(term_ref[...], ones)
    scratch[:, width + tail :] = tn(first_ref[...], turned_ref[...])
    place_slices(where_ref[0], scratch, keep_ref, send_ref)


def input_kernel(dq_ref, kv_ref, cos_ref, sin_ref, wq_ref, wk_ref, wv_ref, x_ref, s_ref,
                 grads_ref, part_ref, term_ref):
    lanes = 2 * HEAD_DIM
    kv_width = wk_ref.shape[1]
    total = jnp.sum(kv_ref[...].astype(F32), axis=0).T
    for i in range(0, kv_width, lanes):
        grads_ref[:, i : i + lanes] = turned(total[:, i : i + lanes], cos_ref[...], -sin_ref[...]).astype(BF)
    grads_ref[:, kv_width:] = total[:, kv_width:].astype(BF)
    part = (
        nt(dq_ref[...], wq_ref[...])
        + nt(grads_ref[:, :kv_width], wk_ref[...])
        + nt(grads_ref[:, kv_width:], wv_ref[...])
    )
    part_ref[...] = part.astype(BF)
    term = jnp.sum(part * x_ref[...].astype(F32) * s_ref[...], axis=0, keepdims=True)
    line = lax.broadcasted_iota(jnp.int32, term_ref.shape, 0)
    term_ref[...] = jnp.where(line == 0, term, 0.0)


def late_kernel(blocks_z, where_ref, n_ref, grads_ref, term_ref, other_ref, keep_ref, send_ref, scratch):
    width = grads_ref.shape[1]
    scratch[:, :width] = tn(n_ref[...], grads_ref[...])
    ones = jnp.ones((term_ref.shape[0], scratch.shape[1] - width), BF)
    scratch[:, width:] = tn((term_ref[...] + other_ref[...]).astype(BF), ones)
    place_direct(where_ref[0], blocks_z, scratch, keep_ref, send_ref)


def near_sum(keep, send):
    return keep.astype(F32) + swap(send, "dp", 1).astype(F32)


def place_sum(total):
    return jnp.sum(exchange(total.astype(BF)).astype(F32), axis=0)


def far_sum(total, axis):
    bit = 1
    while total.shape[axis] > 1:
        bit *= 2
        lead = total.shape[:axis]
        pairs = total.reshape(lead + (total.shape[axis] // 2, 2) + total.shape[axis + 1 :])
        keep = lax.index_in_dim(pairs, 0, axis + 1, keepdims=False)
        send = lax.index_in_dim(pairs, 1, axis + 1, keepdims=False)
        total = keep + swap(send.astype(BF), "dp", bit).astype(F32)
    return jnp.squeeze(total, axis)


def norm_backward(values, norm_scale, gain, grad_normed):
    weighted = grad_normed * gain
    inner = jnp.mean(weighted * values, axis=1, keepdims=True)
    grad_values = norm_scale * weighted - values * (norm_scale * norm_scale * norm_scale) * inner
    grad_gain = jnp.sum(grad_normed * values * norm_scale, axis=0)
    return (grad_values, grad_gain)


def rotary_tables(length):
    half = HEAD_DIM // 2
    inverse = ROPE_BASE ** (-2.0 * np.arange(half) / HEAD_DIM)
    angles = np.arange(length)[:, None] * inverse[None, :]
    cosine, sine = np.cos(angles), np.sin(angles)
    return (
        np.concatenate([cosine, cosine, cosine, cosine], axis=1).astype(np.float32),
        np.concatenate([-sine, sine, -sine, sine], axis=1).astype(np.float32),
    )


def body(
    x_in,
    segments,
    chosen,
    out_grad,
    norm1_gain,
    w_query,
    w_key,
    w_value,
    w_out,
    norm2_gain,
    w_router,
    w_gate,
    w_up,
    w_down,
):
    tok_rows, full_width = x_in.shape
    h = HEAD_DIM
    q_width, kv_width = w_query.shape[1], w_key.shape[1]
    groups = q_width // kv_width
    experts_local, _, inner = w_gate.shape
    n_exp, n_dp = lax.axis_size("expert"), lax.axis_size("dp")
    total_experts = experts_local * n_exp
    top_count = chosen.shape[1]
    capacity = tok_rows * top_count * 25 // (16 * total_experts)
    place, side = lax.axis_index("expert"), lax.axis_index("tensor")
    half_width = full_width // lax.axis_size("tensor")
    row_start = place * tok_rows
    seq_length = segments.shape[0]
    half_rows = tok_rows // 2

    own_dp = lax.axis_index("dp")
    order = [1, 3, 2, 0] if n_exp == 4 else [*range(1, n_exp), 0]
    group = n_exp // 2
    vmem = lambda *shape: pltpu.VMEM(shape, BF)
    prefetch = pltpu.PrefetchScalarGridSpec

    tables = [
        lax.dynamic_slice_in_dim(jnp.asarray(table), row_start, tok_rows)
        for table in rotary_tables(seq_length)
    ]
    cosine, sine = tables
    normed_one, query_rot, kv_own, scale_one = pl.pallas_call(
        project_kernel,
        name="project",
        out_shape=(
            shaped(BF, tok_rows, full_width),
            shaped(BF, tok_rows, q_width),
            shaped(BF, tok_rows, 2 * kv_width),
            shaped(F32, tok_rows, 1),
        ),
        compiler_params=params(),
        cost_estimate=cost(2),
    )(x_in, norm1_gain[None], w_query, w_key, w_value, cosine, sine)
    kv_blocks = [kv_own] + [fetch(kv_own, k) for k in range(1, n_exp)]

    turned_segments = lax.dynamic_slice_in_dim(
        jnp.concatenate([segments, segments]), row_start, seq_length
    )
    key_positions = (row_start + jnp.arange(seq_length, dtype=jnp.int32)) % seq_length
    allowed = (turned_segments[:tok_rows, None] == turned_segments[None, :]) & (
        key_positions[:tok_rows, None] >= key_positions[None, :]
    )
    bias = jnp.where(allowed, 0.0, MASKED).astype(F32)
    heads = q_width // h
    out_half = w_out.shape[0] // 2
    own_core = own_dp % 2
    w_near = swap(lax.dynamic_slice_in_dim(w_out, own_core * out_half, out_half), "tensor")
    w_far = swap(w_near, "dp", 1)
    tail_lanes = -(-(total_experts + 1) // 128) * 128
    router_wide = jnp.pad(w_router, ((0, 0), (0, tail_lanes - total_experts)))
    chosen_wide = jnp.pad(chosen, ((0, 0), (0, 128 - top_count)))
    query_rot, router_wide, chosen_wide = lax.optimization_barrier((query_rot, router_wide, chosen_wide))
    attended, attended_low, log_totals = pl.pallas_call(
        functools.partial(attend_kernel, groups, n_exp),
        name="attend",
        out_shape=(
            shaped(F32, tok_rows, q_width),
            shaped(BF, tok_rows, q_width),
            shaped(F32, tok_rows, heads),
        ),
        scratch_shapes=[vmem(seq_length, 2 * kv_width)],
        compiler_params=params(),
        cost_estimate=cost(10),
    )(after(query_rot, w_near), *kv_blocks, bias)

    cot_in, chosen_in = out_grad, chosen
    cot_half = lambda s: lax.dynamic_slice_in_dim(cot_in, s * half_rows, half_rows)
    chosen_half = lambda s: jnp.pad(
        lax.dynamic_slice_in_dim(chosen_in, s * half_rows, half_rows).T.astype(BF),
        ((0, 16 - top_count), (0, full_width - half_rows)),
    )
    payload = lambda s: jnp.concatenate([cot_half(s), chosen_half(s)], axis=0)
    cot_own, cot_other = payload(side), payload(1 - side)
    cot_near = {}
    for k in order:
        cot_near[k] = fetch(after(cot_own, *kv_blocks[1:]), k) if k else cot_own
    expert_slots = n_exp * capacity
    by_expert = lambda *tail: pl.BlockSpec((1,) + tail, lambda e, *_: (e,) + (0,) * len(tail))

    middle_in = (x_in, attended_low, swap(attended_low, "tensor"), w_out, w_near, w_far, norm2_gain[None])
    whole = lambda array: full(*array.shape)
    hidden_one, scale_two, normed_two, normed_own, normed_far = pl.pallas_call(
        middle_kernel,
        name="middle",
        grid_spec=prefetch(
            num_scalar_prefetch=1,
            grid=(1,),
            in_specs=[whole(array) for array in middle_in],
            out_specs=(
                full(tok_rows, full_width),
                full(tok_rows, 1),
                full(tok_rows, full_width),
                full(half_rows, full_width),
                full(half_rows, full_width),
            ),
        ),
        out_shape=(
            shaped(F32, tok_rows, full_width),
            shaped(F32, tok_rows, 1),
            shaped(BF, tok_rows, full_width),
            shaped(BF, half_rows, full_width),
            shaped(BF, half_rows, full_width),
        ),
        compiler_params=params(24),
        cost_estimate=cost(2),
    )(jnp.stack([side, own_core]), *middle_in)
    near_rows = {k: fetch(normed_own, k) for k in order[:group]}
    for k in order[group:]:
        near_rows[k] = fetch(after(normed_own, *near_rows.values()), k) if k else normed_own

    cot_pairs = [
        (cot_near[k], swap(after(cot_near[k], normed_own), "tensor") if k else cot_other)
        for k in order
    ]
    chosen_blocks = jnp.stack(
        [
            jnp.concatenate([part[half_rows : half_rows + top_count, :half_rows] for part in pair], axis=1)
            for pair in cot_pairs
        ]
    ).astype(jnp.int32)
    expert_ids = jnp.arange(total_experts, dtype=jnp.int32)
    hot_all = jnp.any(chosen_blocks[:, :, None, :] == expert_ids[:, None], axis=1)
    hot_rows = hot_all.transpose(1, 0, 2).reshape(total_experts, n_exp * tok_rows).astype(F32)
    hot_local = lax.dynamic_slice_in_dim(hot_all, place * experts_local, experts_local, 1)
    token_row = jnp.arange(tok_rows, dtype=jnp.int32)
    before = (token_row[:, None] < token_row[None, :]).astype(BF)
    rank = jnp.einsum("kes,st->ket", hot_local.astype(BF), before, preferred_element_type=F32)
    slot_of = jnp.where(hot_local, rank.astype(jnp.int32), -1)

    cot_slots, raw_grad = pl.pallas_call(
        functools.partial(cotangent_kernel, n_exp, capacity),
        name="cotangent",
        grid=(experts_local,),
        in_specs=[whole(slot_of)]
        + [full(*cot_own.shape)] * (2 * n_exp)
        + [by_expert(inner, full_width)],
        out_specs=(by_expert(expert_slots, full_width), by_expert(expert_slots, inner)),
        out_shape=(
            shaped(BF, experts_local, expert_slots, full_width),
            shaped(F32, experts_local, expert_slots, inner),
        ),
        scratch_shapes=[vmem(n_exp, tok_rows, full_width)],
        compiler_params=params(),
        cost_estimate=cost(13),
    )(slot_of, *[half for pair in cot_pairs for half in pair], w_down)

    far_rows = {
        k: swap(near_rows[k], "tensor") if k else normed_far for k in order
    }

    def run_experts(number, hold):
        ks = order[number * group : (number + 1) * group]
        token_halves = [half for k in ks for half in (near_rows[k], far_rows[k])]
        token_halves[0] = after(token_halves[0], *hold)
        slots_here = group * capacity
        low_slots = shaped(BF, experts_local, slots_here, inner)
        columns = group * tok_rows
        return pl.pallas_call(
            functools.partial(experts_kernel, group, capacity),
            name="experts",
            grid_spec=prefetch(
                num_scalar_prefetch=1,
                grid=(experts_local,),
                in_specs=[full(group, experts_local, tok_rows)]
                + [full(half_rows, full_width)] * (2 * group)
                + [
                    pl.BlockSpec((total_experts, columns), lambda e, *_: (0, number)),
                    full(total_experts, full_width),
                    pl.BlockSpec((1, slots_here, inner), lambda e, *_: (e, number, 0)),
                    by_expert(full_width, inner),
                    by_expert(full_width, inner),
                ],
                out_specs=(
                    by_expert(slots_here, full_width),
                    by_expert(slots_here, inner),
                    by_expert(slots_here, inner),
                    by_expert(slots_here, inner),
                    full(group, half_rows + 16, full_width),
                    full(group, half_rows + 16, full_width),
                ),
                scratch_shapes=[
                    vmem(group, tok_rows, full_width),
                    pltpu.VMEM((total_experts, columns), F32),
                    vmem(group, experts_local * capacity, full_width),
                    vmem(group, experts_local * capacity, tok_rows),
                    pltpu.VMEM((2 * group, full_width), F32),
                ],
            ),
            out_shape=(
                shaped(BF, experts_local, slots_here, full_width),
                low_slots,
                low_slots,
                low_slots,
                shaped(BF, group, half_rows + 16, full_width),
                shaped(BF, group, half_rows + 16, full_width),
            ),
            compiler_params=params(),
            cost_estimate=cost(18),
        )(
            place[None], slot_of[number * group : (number + 1) * group], *token_halves,
            hot_rows, w_router.T, raw_grad, w_gate, w_up,
        )

    first = run_experts(0, [far_rows[k] for k in order[group:]])
    second = run_experts(1, [first[4]])

    def pair_sum(made, got):
        return pl.pallas_call(
            pair_sum_kernel,
            name="pair_sum",
            out_shape=(shaped(BF, half_rows + 16, full_width),) * group,
            compiler_params=params(24),
            cost_estimate=cost(1),
        )(made[4], got)

    first_sums = pair_sum(first, swap(first[5], "tensor"))
    second_got = swap(second[5], "tensor")

    out_dims = (n_exp, tok_rows, half_width)

    def combine(*hold):
        return pl.pallas_call(
            functools.partial(combine_kernel, capacity, order),
            name="combine",
            grid_spec=prefetch(
                num_scalar_prefetch=1,
                grid=(experts_local,),
                in_specs=[
                    whole(slot_of),
                    by_expert(group * capacity, inner),
                    by_expert(group * capacity, inner),
                    by_expert(inner, full_width),
                ],
                out_specs=(full(*out_dims), full(*out_dims)),
                scratch_shapes=[
                    vmem(n_exp, experts_local * capacity, full_width),
                    vmem(n_exp, experts_local * capacity, tok_rows),
                ],
            ),
            out_shape=(shaped(BF, *out_dims), shaped(BF, *out_dims)),
            compiler_params=params(),
            cost_estimate=cost(12),
        )(after(jnp.stack([side, place]), *hold), slot_of, first[1], second[1], w_down)

    slice_width = full_width // n_dp
    pairs = [*first[:4], *second[:4]]
    crossing = 1 if n_dp == 4 and experts_local > 3 and slice_width % 128 == 0 else 0
    summed = experts_local - crossing

    def weights(base, count, outs, *hold):
        some = lambda *tail: pl.BlockSpec((1,) + tail, lambda e, *_: (base + e,) + (0,) * len(tail))
        shape = (n_dp // outs, count, 3, slice_width, inner)
        return pl.pallas_call(
            weights_kernel,
            name="weights",
            grid_spec=prefetch(
                num_scalar_prefetch=1,
                grid=(count,),
                in_specs=[some(expert_slots, full_width)] + [some(*array.shape[1:]) for array in pairs],
                out_specs=(pl.BlockSpec((shape[0], 1) + shape[2:], lambda e, *_: (0, e, 0, 0, 0)),) * outs,
            ),
            out_shape=(shaped(BF, *shape),) * outs,
            compiler_params=params(),
            cost_estimate=cost(12),
        )(after(own_dp[None], *hold), cot_slots, *pairs)

    early_experts = summed // 4
    out_mine, out_else = combine(*first_sums, second[4])
    first_grads = weights(0, early_experts, 1, out_mine)[0]
    terms = {k: deliver(first_sums[i], k) for i, k in enumerate(order[:group])}
    second_got, *arrived = lax.optimization_barrier((second_got, first_grads, *terms.values()))
    terms = dict(zip(terms, arrived[1:]))
    second_sums = pair_sum(second, second_got)
    for i, k in enumerate(order[group:]):
        terms[k] = deliver(second_sums[i], k) if k else second_sums[i]
    out_got = swap(after(out_else, second_sums[0]), "tensor")
    out_low = (out_mine.astype(F32) + out_got.astype(F32)).astype(BF)

    first_sum = lax.psum_scatter(
        after(first_grads, *second_sums), "dp", scatter_dimension=0, tiled=False
    )
    weight_grads = weights(early_experts, summed - early_experts, 1, *second_sums)[0]
    keep, send = weights(summed, crossing, 2, weight_grads) if crossing else (second_sums[0],) * 2
    half_sum = pl.pallas_call(
        gather_sum_kernel,
        name="gather_sum",
        out_shape=shaped(BF, half_rows + 16, full_width),
        compiler_params=params(24),
        cost_estimate=cost(1),
    )(after(terms[0], weight_grads, keep, out_low), *[terms[k] for k in range(1, n_exp)])
    weight_sum = lax.psum_scatter(
        after(weight_grads, half_sum), "dp", scatter_dimension=0, tiled=False
    )
    half_other = swap(half_sum, "tensor")
    if crossing:
        near = swap(after(send, half_other), "dp", 1)
        half_grads = (keep[1].astype(F32) + near[1].astype(F32)).astype(BF)
    out_home = exchange(after(out_low, half_sum))

    back_in = (
        half_sum, half_other, normed_two, chosen_wide, router_wide, hidden_one, scale_two, norm2_gain[None], out_grad, w_out,
    )
    hidden_grad, branch_cot, gain_two_term, attended_grad, logit_grads = pl.pallas_call(
        functools.partial(norm_grad_kernel, experts_local, top_count),
        name="norm_grad",
        grid_spec=prefetch(
            num_scalar_prefetch=1,
            grid=(1,),
            in_specs=[whole(array) for array in back_in],
            out_specs=(
                full(tok_rows, full_width),
                full(tok_rows, full_width),
                full(tok_rows, full_width),
                full(tok_rows, q_width),
                full(tok_rows, tail_lanes),
            ),
            scratch_shapes=[vmem(tok_rows, full_width), pltpu.VMEM((2, tail_lanes, half_rows), F32)],
        ),
        out_shape=(
            shaped(F32, tok_rows, full_width),
            shaped(BF, tok_rows, full_width),
            shaped(BF, tok_rows, full_width),
            shaped(BF, tok_rows, q_width),
            shaped(BF, tok_rows, tail_lanes),
        ),
        compiler_params=params(),
        cost_estimate=cost(4),
    )(jnp.stack([side, place]), *back_in)

    back_args = (query_rot, *kv_blocks, attended_grad, attended, log_totals, bias)
    query_grads, kv_parts = pl.pallas_call(
        functools.partial(attend_grad_kernel, groups, n_exp),
        name="attend_grad",
        grid_spec=prefetch(
            num_scalar_prefetch=1,
            grid=(1,),
            in_specs=[whole(array) for array in back_args],
            out_specs=(full(tok_rows, q_width), full(n_exp, 2 * kv_width, tok_rows)),
            scratch_shapes=[vmem(seq_length, 2 * kv_width)],
        ),
        out_shape=(shaped(F32, tok_rows, q_width), shaped(BF, n_exp, 2 * kv_width, tok_rows)),
        compiler_params=params(),
        cost_estimate=cost(10),
    )(place[None], *back_args)
    kv_terms = exchange(after(kv_parts, out_home))

    slice_rows = full_width // (n_dp * n_exp)

    def slices_of(kernel, name, width, more, *arrays):
        dims = (n_exp, n_dp // 2, slice_rows, width)
        dims = dims if more else (n_exp * n_dp // 2, slice_rows, width)
        return pl.pallas_call(
            kernel,
            name=name,
            grid_spec=prefetch(
                num_scalar_prefetch=1,
                grid=(1,),
                in_specs=[whole(array) for array in arrays],
                out_specs=(full(*dims), full(*dims)) + tuple(full(*dim) for dim in more),
                scratch_shapes=[pltpu.VMEM((full_width, width), F32)],
            ),
            out_shape=(shaped(BF, *dims), shaped(BF, *dims)) + tuple(shaped(BF, *dim) for dim in more),
            compiler_params=params(),
            cost_estimate=cost(5),
        )(own_dp[None], *arrays)

    early_keep, early_send, query_low = slices_of(
        early_kernel, "early", 2 * q_width + tail_lanes, [(tok_rows, q_width)],
        branch_cot, attended_low, normed_two, logit_grads, gain_two_term, normed_one, query_grads, cosine, sine,
    )
    early = near_sum(early_keep, early_send).astype(BF)
    if crossing:
        kv_terms, half_grads = lax.optimization_barrier((kv_terms, half_grads))
    kv_terms, early = lax.optimization_barrier((kv_terms, early))
    grads_low, partial_low, gain_one_term = pl.pallas_call(
        input_kernel,
        name="input",
        out_shape=(
            shaped(BF, tok_rows, 2 * kv_width),
            shaped(BF, tok_rows, full_width),
            shaped(F32, 16, full_width),
        ),
        compiler_params=params(),
        cost_estimate=cost(4),
    )(query_low, kv_terms, cosine, sine, w_query, w_key, w_value, x_in, scale_one)
    partial_other = swap(partial_low, "tensor")
    late_keep, late_send = slices_of(
        functools.partial(late_kernel, n_exp), "late", 2 * kv_width + 128, (), normed_one, grads_low, gain_one_term, swap(gain_one_term, "tensor")
    )
    late_send, partial_other = lax.optimization_barrier((late_send, partial_other))
    late = near_sum(late_keep, late_send).astype(BF)
    early = place_sum(early)
    late, partial_other, early = lax.optimization_barrier((late, partial_other, early))
    same_core = [
        [dp * n_exp + z for dp in range(core, n_dp, 2) for z in range(n_exp)] for core in range(2)
    ]
    late_parts = lax.all_to_all(
        late, ("dp", "expert"), split_axis=0, concat_axis=0, tiled=True, axis_index_groups=same_core
    )
    if crossing:
        far = swap(after(half_grads, early), "dp", 2)
    early = far_sum(early, 0)

    def finish(base, count, totals, specs, earlier):
        some = lambda *tail: pl.BlockSpec((1,) + tail, lambda e: (base + e,) + (0,) * len(tail))
        return pl.pallas_call(
            functools.partial(finish_kernel, len(totals)),
            name="finish",
            grid=(count,),
            in_specs=specs + [pl.BlockSpec(memory_space=pl.ANY)] * len(earlier),
            out_specs=(some(slice_width, inner), some(slice_width, inner), some(inner, slice_width)),
            out_shape=(
                shaped(F32, experts_local, slice_width, inner),
                shaped(F32, experts_local, slice_width, inner),
                shaped(F32, experts_local, inner, slice_width),
            ),
            input_output_aliases={len(totals) + i: i for i in range(len(earlier))},
            compiler_params=params(24),
            cost_estimate=cost(3),
        )(*totals, *earlier)

    one = by_expert(3, slice_width, inner)
    finals = finish(0, early_experts, (after(first_sum, partial_other),), [one], ())
    finals = finish(early_experts, summed - early_experts, (weight_sum,), [one], finals)
    if crossing:
        lead = pl.BlockSpec((1, 1, 3, slice_width, inner), lambda e: (0, e, 0, 0, 0))
        finals = finish(summed, crossing, (keep, near, far), [lead, lead, one], finals)
    grad_gate, grad_up, grad_down = finals
    late = jnp.sum(after(late_parts, grad_gate).astype(F32), axis=0)

    mixture_half = jnp.sum(out_home.astype(F32), axis=0)
    mixture_half = jnp.where(side == 0, mixture_half, jnp.roll(mixture_half, half_rows, axis=0))
    residual_half = lax.dynamic_slice_in_dim(hidden_one, side * half_width, half_width, 1)
    block_out = (residual_half + mixture_half).astype(BF)

    normed_one_grad = partial_low.astype(F32) + partial_other.astype(F32)
    inputs = x_in.astype(F32)
    input_part, _ = norm_backward(inputs, scale_one, norm1_gain, normed_one_grad)
    input_grad = hidden_grad + input_part
    gain_one = late[:, -1]
    return (
        block_out,
        input_grad,
        gain_one,
        early[:, q_width + tail_lanes :],
        late[:, :kv_width],
        late[:, kv_width : 2 * kv_width],
        early[:, :q_width].T,
        early[:, q_width + tail_lanes - 1],
        early[:, q_width : q_width + total_experts],
        grad_gate,
        grad_up,
        grad_down,
    )


def solution(mesh):
    return jax.shard_map(
        body,
        mesh=mesh,
        in_specs=(
            P(("dp", "expert"), None),
            P("dp"),
            P(("dp", "expert"), None),
            P(("dp", "expert"), None),
            P(),
            P(None, "tensor"),
            P(None, "tensor"),
            P(None, "tensor"),
            P("tensor", None),
            P(),
            P(),
            P("expert", None, "tensor"),
            P("expert", None, "tensor"),
            P("expert", "tensor", None),
        ),
        out_specs=(
            P(("dp", "expert"), "tensor"),
            P(("dp", "expert"), None),
            P(("dp", "expert")),
            P(("dp", "expert"), "tensor"),
            P(("dp", "expert"), "tensor"),
            P(("dp", "expert"), "tensor"),
            P("tensor", ("dp", "expert")),
            P(("dp", "expert")),
            P(("dp", "expert"), None),
            P("expert", "dp", "tensor"),
            P("expert", "dp", "tensor"),
            P("expert", "tensor", "dp"),
        ),
        check_vma=False,
    )
```

```python
import functools

import jax
import jax.numpy as jnp
import numpy as np
from jax import lax
from jax.experimental import pallas as pl
from jax.experimental.pallas import tpu as pltpu
from jax.sharding import PartitionSpec as P

HEAD_DIM = 64
EPSILON = 1e-05
ROPE_BASE = 10000.0
MASKED = -1e30
BF = jnp.bfloat16
F32 = jnp.float32
MIB = 1024 * 1024


def swap(values, axis, bit=1):
    count = lax.axis_size(axis)
    return lax.ppermute(values, axis, [(i, i ^ bit) for i in range(count)])


def fetch(values, offset):
    count = lax.axis_size("expert")
    return lax.ppermute(values, "expert", [(i, (i - offset) % count) for i in range(count)])


def deliver(values, offset):
    count = lax.axis_size("expert")
    return lax.ppermute(values, "expert", [(i, (i + offset) % count) for i in range(count)])


def halve(parts, bit_axis, bit):
    pairs = parts.reshape((parts.shape[0] // 2, 2) + parts.shape[1:])
    own = (lax.axis_index(bit_axis) // bit) % 2
    keep = lax.dynamic_index_in_dim(pairs, own, 1, keepdims=False)
    send = lax.dynamic_index_in_dim(pairs, 1 - own, 1, keepdims=False)
    got = swap(send, bit_axis, bit)
    return keep.astype(F32) + got.astype(F32)


def sum_over_dp(parts):
    bit = 1
    while parts.shape[0] > 1:
        parts = halve(parts.astype(BF), "dp", bit)
        bit *= 2
    return parts[0]


def exchange(parts):
    return lax.all_to_all(parts, "expert", split_axis=0, concat_axis=0, tiled=True)


def nn(left, right):
    return jnp.dot(left, right, preferred_element_type=F32)


def nt(left, right):
    return lax.dot_general(left, right, (((1,), (1,)), ((), ())), preferred_element_type=F32)


def tn(left, right):
    return lax.dot_general(left, right, (((0,), (0,)), ((), ())), preferred_element_type=F32)


def params(mib=60):
    return pltpu.CompilerParams(vmem_limit_bytes=mib * MIB)


def cost(micros):
    return pl.CostEstimate(flops=int(micros * 1e3), bytes_accessed=0, transcendentals=0)


def shaped(kind, *dims):
    return jax.ShapeDtypeStruct(dims, kind)


def full(*shape):
    return pl.BlockSpec(shape, lambda *_: (0,) * len(shape))


def after(values, *others):
    return lax.optimization_barrier((values,) + others)[0]


def turned(values, cosine, sine):
    lane = lax.broadcasted_iota(jnp.int32, values.shape, 1)
    quarter = HEAD_DIM // 2
    later = pltpu.roll(values, 2 * HEAD_DIM - quarter, 1)
    earlier = pltpu.roll(values, quarter, 1)
    return values * cosine + jnp.where(lane % HEAD_DIM < quarter, later, earlier) * sine


def project_kernel(x_ref, gain_ref, wq_ref, wk_ref, wv_ref, cos_ref, sin_ref, n_ref, q_ref, kv_ref, s_ref):
    values = x_ref[...].astype(F32)
    scale = lax.rsqrt(jnp.mean(values * values, axis=1, keepdims=True) + EPSILON)
    s_ref[...] = scale
    normed = (values * scale * gain_ref[...]).astype(BF)
    n_ref[...] = normed
    cosine, sine = cos_ref[...], sin_ref[...]
    lanes = 2 * HEAD_DIM
    kv = wk_ref.shape[1]
    keys = nn(normed, wk_ref[...])
    for i in range(0, kv, lanes):
        kv_ref[:, i : i + lanes] = turned(keys[:, i : i + lanes], cosine, sine).astype(BF)
    kv_ref[:, kv:] = nn(normed, wv_ref[...]).astype(BF)
    query = nn(normed, wq_ref[...])
    for i in range(0, query.shape[1], lanes):
        q_ref[:, i : i + lanes] = turned(query[:, i : i + lanes], cosine, sine).astype(BF)


def attend_kernel(groups, blocks, *refs):
    q_ref, kv_refs, bias_ref = refs[0], refs[1 : 1 + blocks], refs[1 + blocks]
    o_ref, low_ref, lse_ref, kv_ref = refs[2 + blocks :]
    h = HEAD_DIM
    rows = kv_refs[0].shape[0]
    for k in range(blocks):
        kv_ref[k * rows : (k + 1) * rows, :] = kv_refs[k][...]
    heads = kv_ref.shape[1] // (2 * h)
    for kv in range(heads):
        key = kv_ref[:, kv * h : kv * h + h]
        value = kv_ref[:, (heads + kv) * h : (heads + kv) * h + h]
        for g in range(groups):
            head = kv * groups + g
            span = slice(head * h, head * h + h)
            scores = nt(q_ref[:, span] * h**-0.5, key) + bias_ref[...]
            peak = jnp.max(scores, axis=1, keepdims=True)
            raw = jnp.exp(scores - peak)
            total = jnp.sum(raw, axis=1, keepdims=True)
            out = nn((raw * (1.0 / total)).astype(BF), value)
            o_ref[:, span] = out
            low_ref[:, span] = out.astype(BF)
            lse_ref[:, head : head + 1] = peak + jnp.log(total)


def attend_grad_kernel(groups, blocks, place_ref, *refs):
    q_ref, kv_refs, d_ref, o_ref, lse_ref, bias_ref = refs[0], refs[1 : 1 + blocks], *refs[1 + blocks : 5 + blocks]
    dq_ref, dkv_ref, kv_ref = refs[5 + blocks :]
    h = HEAD_DIM
    rows = kv_refs[0].shape[0]
    for k in range(blocks):
        kv_ref[k * rows : (k + 1) * rows, :] = kv_refs[k][...]
    heads = kv_ref.shape[1] // (2 * h)
    for kv in range(heads):
        key = kv_ref[:, kv * h : kv * h + h]
        value = kv_ref[:, (heads + kv) * h : (heads + kv) * h + h]
        key_grad = value_grad = None
        for g in range(groups):
            head = kv * groups + g
            span = slice(head * h, head * h + h)
            query = q_ref[:, span] * h**-0.5
            cot = d_ref[:, span]
            scores = nt(query, key) + bias_ref[...]
            probs = jnp.exp(scores - lse_ref[:, head : head + 1])
            delta = jnp.sum(cot.astype(F32) * o_ref[:, span], axis=1, keepdims=True)
            slope = (probs * (nt(cot, value) - delta)).astype(BF)
            value_part = tn(cot, probs.astype(BF))
            key_part = tn(query, slope)
            dq_ref[:, span] = nn(slope, key) * h**-0.5
            value_grad = value_part if value_grad is None else value_grad + value_part
            key_grad = key_part if key_grad is None else key_grad + key_part
        key_low = key_grad.astype(BF)
        value_low = value_grad.astype(BF)
        for k in range(blocks):
            to = lax.rem(place_ref[0] + k, blocks)
            dkv_ref[to, kv * h : kv * h + h, :] = key_low[:, k * rows : (k + 1) * rows]
            dkv_ref[to, (heads + kv) * h : (heads + kv) * h + h, :] = value_low[:, k * rows : (k + 1) * rows]


def middle_kernel(
    side_ref, x_ref, mine_ref, other_ref, w_ref, w_near, w_far, gain_ref, h_ref, s_ref, n_ref, own_ref, far_ref
):
    part = w_near.shape[0]
    hidden = x_ref[...].astype(F32) + nn(mine_ref[...], w_ref[...])
    for w, number in ((w_near, side_ref[1]), (w_far, 1 - side_ref[1])):
        hidden += nn(other_ref[:, pl.ds(pl.multiple_of(number * part, part), part)], w[...])
    h_ref[...] = hidden
    scale = lax.rsqrt(jnp.mean(hidden * hidden, axis=1, keepdims=True) + EPSILON)
    s_ref[...] = scale
    n_ref[...] = (hidden * scale * gain_ref[...]).astype(BF)
    half = own_ref.shape[0]
    own_ref[...] = n_ref[pl.ds(pl.multiple_of(side_ref[0] * half, half), half), :]
    far_ref[...] = n_ref[pl.ds(pl.multiple_of((1 - side_ref[0]) * half, half), half), :]


def make_pick(slot_ref, k, expert, slots):
    row = slot_ref[k, pl.ds(expert, 1), :]
    lines = lax.broadcasted_iota(jnp.int32, (slots, row.shape[1]), 0)
    return jnp.where(lines == row, 1.0, 0.0)


def cotangent_kernel(blocks, slots, *refs):
    slot_ref, halves, wd_ref = refs[0], refs[1 : 1 + 2 * blocks], refs[1 + 2 * blocks]
    cg_ref, dm_ref, x_ref = refs[2 + 2 * blocks :]
    half = x_ref.shape[1] // 2
    step = pl.program_id(0)

    @pl.when(step == 0)
    def _():
        for k in range(blocks):
            x_ref[k, :half, :] = halves[2 * k][:half, :]
            x_ref[k, half:, :] = halves[2 * k + 1][:half, :]

    for k in range(blocks):
        pick = make_pick(slot_ref, k, step, slots).astype(BF)
        cg_ref[0, k * slots : (k + 1) * slots, :] = nn(pick, x_ref[k]).astype(BF)
    dm_ref[0] = nt(cg_ref[0], wd_ref[0])


def split_rows(values):
    line = lax.broadcasted_iota(jnp.int32, (16, values[0].shape[1]), 0)
    out = jnp.zeros(line.shape, F32)
    for i, value in enumerate(values):
        high = value.astype(BF).astype(F32)
        out = jnp.where(line == 2 * i, high, jnp.where(line == 2 * i + 1, value - high, out))
    return out.astype(BF)


def pair_sum_kernel(mine_ref, got_ref, *outs):
    half = mine_ref.shape[1] - 16
    for k, out in enumerate(outs):
        total = mine_ref[k].astype(F32) + got_ref[k].astype(F32)
        out[:half, :] = total[:half].astype(BF)
        out[half:, :] = split_rows([total[half : half + 1] + total[half + 1 : half + 2]])


def gather_sum_kernel(*refs):
    parts, out = refs[:-1], refs[-1]
    half = out.shape[0] - 16
    total = parts[0][...].astype(F32)
    rows = [total[half : half + 1] + total[half + 1 : half + 2]]
    total = total[:half]
    for part in parts[1:]:
        more = part[...].astype(F32)
        total = total + more[:half]
        rows.append(more[half : half + 1] + more[half + 1 : half + 2])
    out[:half, :] = total.astype(BF)
    out[half:, :] = split_rows(rows)


def experts_kernel(blocks, slots, place_ref, slot_ref, *refs):
    halves, (hot_ref, router_ref, dm_ref, wg_ref, wu_ref) = refs[: 2 * blocks], refs[2 * blocks : 5 + 2 * blocks]
    (xg_ref, gm_ref, da_ref, db_ref, mine_ref, else_ref,
     x_ref, gates_ref, n_ref, pick_ref, dg_ref) = refs[5 + 2 * blocks :]
    rows = x_ref.shape[1]
    half = rows // 2
    step, steps = pl.program_id(0), pl.num_programs(0)

    @pl.when(step == 0)
    def _():
        for k in range(blocks):
            x_ref[k, :half, :] = halves[2 * k][...]
            x_ref[k, half:, :] = halves[2 * k + 1][...]
        tokens = x_ref[...].reshape(blocks * rows, x_ref.shape[2])
        hot = hot_ref[...] > 0.0
        logits = jnp.where(hot, nt(router_ref[...], tokens), MASKED)
        raw = jnp.where(hot, jnp.exp(logits - jnp.max(logits, axis=0, keepdims=True)), 0.0)
        gates_ref[...] = raw / jnp.sum(raw, axis=0, keepdims=True)
        dg_ref[...] = jnp.zeros_like(dg_ref)

    gate_row = gates_ref[pl.ds(place_ref[0] * steps + step, 1), :]
    at = pl.multiple_of(step * slots, slots)
    gate_parts, picks = [], []
    for k in range(blocks):
        pick = make_pick(slot_ref, k, step, slots)
        picks.append(pick)
        low = pick.astype(BF)
        pick_ref[k, pl.ds(at, slots), :] = low
        xg_ref[0, k * slots : (k + 1) * slots, :] = nn(low, x_ref[k]).astype(BF)
        gate_parts.append(jnp.sum(pick * gate_row[:, k * rows : (k + 1) * rows], axis=1, keepdims=True))
    gates = jnp.concatenate(gate_parts, axis=0)
    own = xg_ref[0]
    gate_pre = nn(own, wg_ref[0])
    up_pre = nn(own, wu_ref[0])
    raw_grad = dm_ref[0]
    sigmoid = 1.0 / (1.0 + jnp.exp(-gate_pre))
    swish = gate_pre * sigmoid
    active = swish * up_pre
    dgate = jnp.sum(active * raw_grad, axis=1, keepdims=True)
    gm_ref[0] = (gates * active).astype(BF)
    grad = gates * raw_grad
    da = (grad * up_pre * sigmoid * (1.0 + gate_pre * (1.0 - sigmoid))).astype(BF)
    db = (grad * swish).astype(BF)
    da_ref[0] = da
    db_ref[0] = db
    low = (nt(da, wg_ref[0]) + nt(db, wu_ref[0])).astype(BF)
    for k in range(blocks):
        part = slice(k * slots, (k + 1) * slots)
        n_ref[k, pl.ds(at, slots), :] = low[part]
        dg_row = jnp.sum(picks[k] * dgate[part], axis=0, keepdims=True)
        lanes = pl.ds(pl.multiple_of(step * half, half), half)
        dg_ref[2 * k : 2 * k + 1, lanes] = dg_row[:, :half]
        dg_ref[2 * k + 1 : 2 * k + 2, lanes] = dg_row[:, half:]

    @pl.when(step == steps - 1)
    def _():
        for k in range(blocks):
            out = tn(pick_ref[k], n_ref[k]).astype(BF)
            mine_ref[k, :half, :] = out[:half]
            else_ref[k, :half, :] = out[half:]
            mine_ref[k, half:, :] = split_rows([dg_ref[2 * k : 2 * k + 1, :]])
            else_ref[k, half:, :] = split_rows([dg_ref[2 * k + 1 : 2 * k + 2, :]])


def weights_kernel(own_ref, cg_ref, *refs):
    pairs, outs = refs[:8], refs[8:]
    count, width = len(outs) * outs[0].shape[0], outs[0].shape[3]
    split = pairs[0].shape[1]
    for number in range(count):
        if len(outs) == 1:
            out, place, span = outs[0], number, slice(number * width, (number + 1) * width)
        else:
            out, place = outs[number % 2], number // 2
            span = pl.ds(pl.multiple_of((own_ref[0] ^ number) * width, 128), width)
        gate = up = down = None
        for i in range(2):
            xg_ref, gm_ref, da_ref, db_ref = pairs[4 * i : 4 * i + 4]
            rows = xg_ref[0, :, span]
            cots = cg_ref[0, i * split : (i + 1) * split, span]
            parts = tn(rows, da_ref[0]), tn(rows, db_ref[0]), tn(cots, gm_ref[0])
            gate, up, down = parts if i == 0 else (gate + parts[0], up + parts[1], down + parts[2])
        out[place, 0, 0] = gate.astype(BF)
        out[place, 0, 1] = up.astype(BF)
        out[place, 0, 2] = down.astype(BF)


def finish_kernel(parts, *refs):
    gate_ref, up_ref, down_ref = refs[-3:]
    total = None
    for ref in refs[:parts]:
        term = ref[(0,) * (len(ref.shape) - 3)].astype(F32)
        total = term if total is None else total + term
    gate_ref[0] = total[0]
    up_ref[0] = total[1]
    down_ref[0] = total[2].T


def combine_kernel(slots, offsets, where_ref, slot_ref, ga_ref, gb_ref, wd_ref, mine_ref, else_ref, r_ref, pick_ref):
    blocks = mine_ref.shape[0]
    group = blocks // 2
    step, steps = pl.program_id(0), pl.num_programs(0)
    at = pl.multiple_of(step * slots, slots)
    for i, ref in enumerate((ga_ref, gb_ref)):
        low = nn(ref[0], wd_ref[0]).astype(BF)
        for j in range(group):
            k = i * group + j
            r_ref[k, pl.ds(at, slots), :] = low[j * slots : (j + 1) * slots]
            pick_ref[k, pl.ds(at, slots), :] = make_pick(slot_ref, k, step, slots).astype(BF)

    @pl.when(step == steps - 1)
    def _():
        width = mine_ref.shape[2]
        half = mine_ref.shape[1] // 2
        own = pl.ds(pl.multiple_of(where_ref[0] * width, width), width)
        far = pl.ds(pl.multiple_of((1 - where_ref[0]) * width, width), width)
        for k in range(blocks):
            to = lax.rem(where_ref[1] + offsets[k], blocks)
            mine_ref[to] = tn(pick_ref[k], r_ref[k, :, own]).astype(BF)
            out = tn(pick_ref[k], r_ref[k, :, far]).astype(BF)
            else_ref[to, :half] = out[half:]
            else_ref[to, half:] = out[:half]


def norm_grad_kernel(
    local, top, where_ref, own_ref, far_ref, n_ref, chosen_ref, router_ref, h_ref, s_ref, gain_ref, c_ref, w_ref,
    grad_ref, low_ref, term_ref, do_ref, dl_ref, e_ref, g_ref,
):
    side, place = where_ref[0], where_ref[1]
    half = own_ref.shape[0] - 16
    lanes = router_ref.shape[1]
    sources = 4
    g_ref[...] = jnp.zeros_like(g_ref)
    for part, ref in ((side, own_ref), (1 - side, far_ref)):
        e_ref[pl.ds(pl.multiple_of(part * half, half), half), :] = ref[:half, :]
        tail = ref[half:, :].astype(F32)
        for k in range(sources):
            row = tail[2 * k : 2 * k + 1] + tail[2 * k + 1 : 2 * k + 2]
            source = lax.rem(place + sources - k, sources)
            for e in range(local):
                g_ref[part, pl.ds(source * local + e, 1), :] = row[:, e * half : (e + 1) * half]
    dgate = jnp.concatenate([g_ref[0].T, g_ref[1].T], axis=0)
    lane = lax.broadcasted_iota(jnp.int32, dgate.shape, 1)
    hot = chosen_ref[:, 0:1] == lane
    for i in range(1, top):
        hot = hot | (chosen_ref[:, i : i + 1] == lane)
    logits = jnp.where(hot, nn(n_ref[...], router_ref[...]), MASKED)
    raw = jnp.where(hot, jnp.exp(logits - jnp.max(logits, axis=1, keepdims=True)), 0.0)
    gates = raw / jnp.sum(raw, axis=1, keepdims=True)
    logit_grads = (gates * (dgate - jnp.sum(gates * dgate, axis=1, keepdims=True))).astype(BF)
    dl_ref[...] = logit_grads
    grad = nt(logit_grads, router_ref[...]) + e_ref[...].astype(F32)
    hidden, scale = h_ref[...], s_ref[...]
    term_ref[...] = (grad * hidden * scale).astype(BF)
    weighted = grad * gain_ref[...]
    inner = jnp.mean(weighted * hidden, axis=1, keepdims=True)
    total = scale * weighted - hidden * (scale * scale * scale) * inner + c_ref[...].astype(F32)
    grad_ref[...] = total
    low = total.astype(BF)
    low_ref[...] = low
    do_ref[...] = nt(low, w_ref[...]).astype(BF)


def place_direct(own, blocks_z, scratch, keep_ref, send_ref):
    blocks, rows, _ = keep_ref.shape
    core = lax.rem(own, 2)
    for out, bit in ((keep_ref, core), (send_ref, 1 - core)):
        for number in range(blocks):
            at = ((2 * (number // blocks_z) + bit) * blocks_z + number % blocks_z) * rows
            out[number] = scratch[pl.ds(pl.multiple_of(at, 8), rows), :].astype(BF)


def place_slices(own, scratch, keep_ref, send_ref):
    blocks, pairs, rows, _ = keep_ref.shape
    for a in range(2 * pairs):
        out = send_ref if a % 2 else keep_ref
        for b in range(blocks):
            number = (own ^ a) * blocks + b
            out[b, a // 2] = scratch[pl.ds(pl.multiple_of(number * rows, 8), rows), :].astype(BF)


def early_kernel(
    where_ref, low_ref, o_ref, n_ref, dl_ref, term_ref, first_ref, dq_ref, cos_ref, sin_ref,
    keep_ref, send_ref, turned_ref, scratch,
):
    width, lanes = o_ref.shape[1], 2 * HEAD_DIM
    tail = dl_ref.shape[1]
    for i in range(0, width, lanes):
        turned_ref[:, i : i + lanes] = turned(dq_ref[:, i : i + lanes], cos_ref[...], -sin_ref[...]).astype(BF)
    scratch[:, :width] = tn(low_ref[...], o_ref[...])
    lane = lax.broadcasted_iota(jnp.int32, dl_ref.shape, 1)
    ones = jnp.where(lane == tail - 1, 1.0, 0.0).astype(BF)
    scratch[:, width : width + tail] = tn(n_ref[...], dl_ref[...]) + tn(term_ref[...], ones)
    scratch[:, width + tail :] = tn(first_ref[...], turned_ref[...])
    place_slices(where_ref[0], scratch, keep_ref, send_ref)


def input_kernel(dq_ref, kv_ref, cos_ref, sin_ref, wq_ref, wk_ref, wv_ref, x_ref, s_ref,
                 grads_ref, part_ref, term_ref):
    lanes = 2 * HEAD_DIM
    kv_width = wk_ref.shape[1]
    total = jnp.sum(kv_ref[...].astype(F32), axis=0).T
    for i in range(0, kv_width, lanes):
        grads_ref[:, i : i + lanes] = turned(total[:, i : i + lanes], cos_ref[...], -sin_ref[...]).astype(BF)
    grads_ref[:, kv_width:] = total[:, kv_width:].astype(BF)
    part = (
        nt(dq_ref[...], wq_ref[...])
        + nt(grads_ref[:, :kv_width], wk_ref[...])
        + nt(grads_ref[:, kv_width:], wv_ref[...])
    )
    part_ref[...] = part.astype(BF)
    term = jnp.sum(part * x_ref[...].astype(F32) * s_ref[...], axis=0, keepdims=True)
    line = lax.broadcasted_iota(jnp.int32, term_ref.shape, 0)
    term_ref[...] = jnp.where(line == 0, term, 0.0)


def late_kernel(blocks_z, where_ref, n_ref, grads_ref, term_ref, other_ref, keep_ref, send_ref, scratch):
    width = grads_ref.shape[1]
    scratch[:, :width] = tn(n_ref[...], grads_ref[...])
    ones = jnp.ones((term_ref.shape[0], scratch.shape[1] - width), BF)
    scratch[:, width:] = tn((term_ref[...] + other_ref[...]).astype(BF), ones)
    place_direct(where_ref[0], blocks_z, scratch, keep_ref, send_ref)


def near_sum(keep, send):
    return keep.astype(F32) + swap(send, "dp", 1).astype(F32)


def place_sum(total):
    return jnp.sum(exchange(total.astype(BF)).astype(F32), axis=0)


def far_sum(total, axis):
    bit = 1
    while total.shape[axis] > 1:
        bit *= 2
        lead = total.shape[:axis]
        pairs = total.reshape(lead + (total.shape[axis] // 2, 2) + total.shape[axis + 1 :])
        keep = lax.index_in_dim(pairs, 0, axis + 1, keepdims=False)
        send = lax.index_in_dim(pairs, 1, axis + 1, keepdims=False)
        total = keep + swap(send.astype(BF), "dp", bit).astype(F32)
    return jnp.squeeze(total, axis)


def norm_backward(values, norm_scale, gain, grad_normed):
    weighted = grad_normed * gain
    inner = jnp.mean(weighted * values, axis=1, keepdims=True)
    grad_values = norm_scale * weighted - values * (norm_scale * norm_scale * norm_scale) * inner
    grad_gain = jnp.sum(grad_normed * values * norm_scale, axis=0)
    return (grad_values, grad_gain)


def rotary_tables(length):
    half = HEAD_DIM // 2
    inverse = ROPE_BASE ** (-2.0 * np.arange(half) / HEAD_DIM)
    angles = np.arange(length)[:, None] * inverse[None, :]
    cosine, sine = np.cos(angles), np.sin(angles)
    return (
        np.concatenate([cosine, cosine, cosine, cosine], axis=1).astype(np.float32),
        np.concatenate([-sine, sine, -sine, sine], axis=1).astype(np.float32),
    )


def body(
    x_in,
    segments,
    chosen,
    out_grad,
    norm1_gain,
    w_query,
    w_key,
    w_value,
    w_out,
    norm2_gain,
    w_router,
    w_gate,
    w_up,
    w_down,
):
    tok_rows, full_width = x_in.shape
    h = HEAD_DIM
    q_width, kv_width = w_query.shape[1], w_key.shape[1]
    groups = q_width // kv_width
    experts_local, _, inner = w_gate.shape
    n_exp, n_dp = lax.axis_size("expert"), lax.axis_size("dp")
    total_experts = experts_local * n_exp
    top_count = chosen.shape[1]
    capacity = tok_rows * top_count * 25 // (16 * total_experts)
    place, side = lax.axis_index("expert"), lax.axis_index("tensor")
    half_width = full_width // lax.axis_size("tensor")
    row_start = place * tok_rows
    seq_length = segments.shape[0]
    half_rows = tok_rows // 2

    own_dp = lax.axis_index("dp")
    order = [1, 3, 2, 0] if n_exp == 4 else [*range(1, n_exp), 0]
    group = n_exp // 2
    vmem = lambda *shape: pltpu.VMEM(shape, BF)
    prefetch = pltpu.PrefetchScalarGridSpec

    tables = [
        lax.dynamic_slice_in_dim(jnp.asarray(table), row_start, tok_rows)
        for table in rotary_tables(seq_length)
    ]
    cosine, sine = tables
    normed_one, query_rot, kv_own, scale_one = pl.pallas_call(
        project_kernel,
        name="project",
        out_shape=(
            shaped(BF, tok_rows, full_width),
            shaped(BF, tok_rows, q_width),
            shaped(BF, tok_rows, 2 * kv_width),
            shaped(F32, tok_rows, 1),
        ),
        compiler_params=params(),
        cost_estimate=cost(2),
    )(x_in, norm1_gain[None], w_query, w_key, w_value, cosine, sine)
    kv_blocks = [kv_own] + [fetch(kv_own, k) for k in range(1, n_exp)]

    turned_segments = lax.dynamic_slice_in_dim(
        jnp.concatenate([segments, segments]), row_start, seq_length
    )
    key_positions = (row_start + jnp.arange(seq_length, dtype=jnp.int32)) % seq_length
    allowed = (turned_segments[:tok_rows, None] == turned_segments[None, :]) & (
        key_positions[:tok_rows, None] >= key_positions[None, :]
    )
    bias = jnp.where(allowed, 0.0, MASKED).astype(F32)
    heads = q_width // h
    out_half = w_out.shape[0] // 2
    own_core = own_dp % 2
    w_near = swap(lax.dynamic_slice_in_dim(w_out, own_core * out_half, out_half), "tensor")
    w_far = swap(w_near, "dp", 1)
    tail_lanes = -(-(total_experts + 1) // 128) * 128
    router_wide = jnp.pad(w_router, ((0, 0), (0, tail_lanes - total_experts)))
    chosen_wide = jnp.pad(chosen, ((0, 0), (0, 128 - top_count)))
    query_rot, router_wide, chosen_wide = lax.optimization_barrier((query_rot, router_wide, chosen_wide))
    attended, attended_low, log_totals = pl.pallas_call(
        functools.partial(attend_kernel, groups, n_exp),
        name="attend",
        out_shape=(
            shaped(F32, tok_rows, q_width),
            shaped(BF, tok_rows, q_width),
            shaped(F32, tok_rows, heads),
        ),
        scratch_shapes=[vmem(seq_length, 2 * kv_width)],
        compiler_params=params(),
        cost_estimate=cost(10),
    )(after(query_rot, w_near), *kv_blocks, bias)

    cot_in, chosen_in = out_grad, chosen
    cot_half = lambda s: lax.dynamic_slice_in_dim(cot_in, s * half_rows, half_rows)
    chosen_half = lambda s: jnp.pad(
        lax.dynamic_slice_in_dim(chosen_in, s * half_rows, half_rows).T.astype(BF),
        ((0, 16 - top_count), (0, full_width - half_rows)),
    )
    payload = lambda s: jnp.concatenate([cot_half(s), chosen_half(s)], axis=0)
    cot_own, cot_other = payload(side), payload(1 - side)
    cot_near = {}
    for k in order:
        cot_near[k] = fetch(after(cot_own, *kv_blocks[1:]), k) if k else cot_own
    expert_slots = n_exp * capacity
    by_expert = lambda *tail: pl.BlockSpec((1,) + tail, lambda e, *_: (e,) + (0,) * len(tail))

    middle_in = (x_in, attended_low, swap(attended_low, "tensor"), w_out, w_near, w_far, norm2_gain[None])
    whole = lambda array: full(*array.shape)
    hidden_one, scale_two, normed_two, normed_own, normed_far = pl.pallas_call(
        middle_kernel,
        name="middle",
        grid_spec=prefetch(
            num_scalar_prefetch=1,
            grid=(1,),
            in_specs=[whole(array) for array in middle_in],
            out_specs=(
                full(tok_rows, full_width),
                full(tok_rows, 1),
                full(tok_rows, full_width),
                full(half_rows, full_width),
                full(half_rows, full_width),
            ),
        ),
        out_shape=(
            shaped(F32, tok_rows, full_width),
            shaped(F32, tok_rows, 1),
            shaped(BF, tok_rows, full_width),
            shaped(BF, half_rows, full_width),
            shaped(BF, half_rows, full_width),
        ),
        compiler_params=params(24),
        cost_estimate=cost(2),
    )(jnp.stack([side, own_core]), *middle_in)
    near_rows = {k: fetch(normed_own, k) for k in order[:group]}
    for k in order[group:]:
        near_rows[k] = fetch(after(normed_own, *near_rows.values()), k) if k else normed_own

    cot_pairs = [
        (cot_near[k], swap(after(cot_near[k], normed_own), "tensor") if k else cot_other)
        for k in order
    ]
    chosen_blocks = jnp.stack(
        [
            jnp.concatenate([part[half_rows : half_rows + top_count, :half_rows] for part in pair], axis=1)
            for pair in cot_pairs
        ]
    ).astype(jnp.int32)
    expert_ids = jnp.arange(total_experts, dtype=jnp.int32)
    hot_all = jnp.any(chosen_blocks[:, :, None, :] == expert_ids[:, None], axis=1)
    hot_rows = hot_all.transpose(1, 0, 2).reshape(total_experts, n_exp * tok_rows).astype(F32)
    hot_local = lax.dynamic_slice_in_dim(hot_all, place * experts_local, experts_local, 1)
    token_row = jnp.arange(tok_rows, dtype=jnp.int32)
    before = (token_row[:, None] < token_row[None, :]).astype(BF)
    rank = jnp.einsum("kes,st->ket", hot_local.astype(BF), before, preferred_element_type=F32)
    slot_of = jnp.where(hot_local, rank.astype(jnp.int32), -1)

    cot_slots, raw_grad = pl.pallas_call(
        functools.partial(cotangent_kernel, n_exp, capacity),
        name="cotangent",
        grid=(experts_local,),
        in_specs=[whole(slot_of)]
        + [full(*cot_own.shape)] * (2 * n_exp)
        + [by_expert(inner, full_width)],
        out_specs=(by_expert(expert_slots, full_width), by_expert(expert_slots, inner)),
        out_shape=(
            shaped(BF, experts_local, expert_slots, full_width),
            shaped(F32, experts_local, expert_slots, inner),
        ),
        scratch_shapes=[vmem(n_exp, tok_rows, full_width)],
        compiler_params=params(),
        cost_estimate=cost(13),
    )(slot_of, *[half for pair in cot_pairs for half in pair], w_down)

    far_rows = {
        k: swap(near_rows[k], "tensor") if k else normed_far for k in order
    }

    def run_experts(number, hold):
        ks = order[number * group : (number + 1) * group]
        token_halves = [half for k in ks for half in (near_rows[k], far_rows[k])]
        token_halves[0] = after(token_halves[0], *hold)
        slots_here = group * capacity
        low_slots = shaped(BF, experts_local, slots_here, inner)
        columns = group * tok_rows
        return pl.pallas_call(
            functools.partial(experts_kernel, group, capacity),
            name="experts",
            grid_spec=prefetch(
                num_scalar_prefetch=1,
                grid=(experts_local,),
                in_specs=[full(group, experts_local, tok_rows)]
                + [full(half_rows, full_width)] * (2 * group)
                + [
                    pl.BlockSpec((total_experts, columns), lambda e, *_: (0, number)),
                    full(total_experts, full_width),
                    pl.BlockSpec((1, slots_here, inner), lambda e, *_: (e, number, 0)),
                    by_expert(full_width, inner),
                    by_expert(full_width, inner),
                ],
                out_specs=(
                    by_expert(slots_here, full_width),
                    by_expert(slots_here, inner),
                    by_expert(slots_here, inner),
                    by_expert(slots_here, inner),
                    full(group, half_rows + 16, full_width),
                    full(group, half_rows + 16, full_width),
                ),
                scratch_shapes=[
                    vmem(group, tok_rows, full_width),
                    pltpu.VMEM((total_experts, columns), F32),
                    vmem(group, experts_local * capacity, full_width),
                    vmem(group, experts_local * capacity, tok_rows),
                    pltpu.VMEM((2 * group, full_width), F32),
                ],
            ),
            out_shape=(
                shaped(BF, experts_local, slots_here, full_width),
                low_slots,
                low_slots,
                low_slots,
                shaped(BF, group, half_rows + 16, full_width),
                shaped(BF, group, half_rows + 16, full_width),
            ),
            compiler_params=params(),
            cost_estimate=cost(18),
        )(
            place[None], slot_of[number * group : (number + 1) * group], *token_halves,
            hot_rows, w_router.T, raw_grad, w_gate, w_up,
        )

    first = run_experts(0, [far_rows[k] for k in order[group:]])
    second = run_experts(1, [first[4]])

    def pair_sum(made, got):
        return pl.pallas_call(
            pair_sum_kernel,
            name="pair_sum",
            out_shape=(shaped(BF, half_rows + 16, full_width),) * group,
            compiler_params=params(24),
            cost_estimate=cost(1),
        )(made[4], got)

    first_sums = pair_sum(first, swap(first[5], "tensor"))
    second_got = swap(second[5], "tensor")

    out_dims = (n_exp, tok_rows, half_width)

    def combine(*hold):
        return pl.pallas_call(
            functools.partial(combine_kernel, capacity, order),
            name="combine",
            grid_spec=prefetch(
                num_scalar_prefetch=1,
                grid=(experts_local,),
                in_specs=[
                    whole(slot_of),
                    by_expert(group * capacity, inner),
                    by_expert(group * capacity, inner),
                    by_expert(inner, full_width),
                ],
                out_specs=(full(*out_dims), full(*out_dims)),
                scratch_shapes=[
                    vmem(n_exp, experts_local * capacity, full_width),
                    vmem(n_exp, experts_local * capacity, tok_rows),
                ],
            ),
            out_shape=(shaped(BF, *out_dims), shaped(BF, *out_dims)),
            compiler_params=params(),
            cost_estimate=cost(12),
        )(after(jnp.stack([side, place]), *hold), slot_of, first[1], second[1], w_down)

    slice_width = full_width // n_dp
    pairs = [*first[:4], *second[:4]]
    crossing = 1 if n_dp == 4 and experts_local > 3 and slice_width % 128 == 0 else 0
    summed = experts_local - crossing

    def weights(base, count, outs, *hold):
        some = lambda *tail: pl.BlockSpec((1,) + tail, lambda e, *_: (base + e,) + (0,) * len(tail))
        shape = (n_dp // outs, count, 3, slice_width, inner)
        return pl.pallas_call(
            weights_kernel,
            name="weights",
            grid_spec=prefetch(
                num_scalar_prefetch=1,
                grid=(count,),
                in_specs=[some(expert_slots, full_width)] + [some(*array.shape[1:]) for array in pairs],
                out_specs=(pl.BlockSpec((shape[0], 1) + shape[2:], lambda e, *_: (0, e, 0, 0, 0)),) * outs,
            ),
            out_shape=(shaped(BF, *shape),) * outs,
            compiler_params=params(),
            cost_estimate=cost(12),
        )(after(own_dp[None], *hold), cot_slots, *pairs)

    early_experts = summed // 4
    out_mine, out_else = combine(*first_sums, second[4])
    first_grads = weights(0, early_experts, 1, out_mine)[0]
    terms = {k: deliver(first_sums[i], k) for i, k in enumerate(order[:group])}
    second_got, *arrived = lax.optimization_barrier((second_got, first_grads, *terms.values()))
    terms = dict(zip(terms, arrived[1:]))
    second_sums = pair_sum(second, second_got)
    for i, k in enumerate(order[group:]):
        terms[k] = deliver(second_sums[i], k) if k else second_sums[i]
    out_got = swap(after(out_else, second_sums[0]), "tensor")
    out_low = (out_mine.astype(F32) + out_got.astype(F32)).astype(BF)

    first_sum = lax.psum_scatter(
        after(first_grads, *second_sums), "dp", scatter_dimension=0, tiled=False
    )
    weight_grads = weights(early_experts, summed - early_experts, 1, *second_sums)[0]
    keep, send = weights(summed, crossing, 2, weight_grads) if crossing else (second_sums[0],) * 2
    half_sum = pl.pallas_call(
        gather_sum_kernel,
        name="gather_sum",
        out_shape=shaped(BF, half_rows + 16, full_width),
        compiler_params=params(24),
        cost_estimate=cost(1),
    )(after(terms[0], weight_grads, keep, out_low), *[terms[k] for k in range(1, n_exp)])
    weight_sum = lax.psum_scatter(
        after(weight_grads, half_sum), "dp", scatter_dimension=0, tiled=False
    )
    half_other = swap(half_sum, "tensor")
    if crossing:
        near = swap(after(send, half_other), "dp", 1)
        half_grads = (keep[1].astype(F32) + near[1].astype(F32)).astype(BF)
    out_home = exchange(after(out_low, half_sum))

    back_in = (
        half_sum, half_other, normed_two, chosen_wide, router_wide, hidden_one, scale_two, norm2_gain[None], out_grad, w_out,
    )
    hidden_grad, branch_cot, gain_two_term, attended_grad, logit_grads = pl.pallas_call(
        functools.partial(norm_grad_kernel, experts_local, top_count),
        name="norm_grad",
        grid_spec=prefetch(
            num_scalar_prefetch=1,
            grid=(1,),
            in_specs=[whole(array) for array in back_in],
            out_specs=(
                full(tok_rows, full_width),
                full(tok_rows, full_width),
                full(tok_rows, full_width),
                full(tok_rows, q_width),
                full(tok_rows, tail_lanes),
            ),
            scratch_shapes=[vmem(tok_rows, full_width), pltpu.VMEM((2, tail_lanes, half_rows), F32)],
        ),
        out_shape=(
            shaped(F32, tok_rows, full_width),
            shaped(BF, tok_rows, full_width),
            shaped(BF, tok_rows, full_width),
            shaped(BF, tok_rows, q_width),
            shaped(BF, tok_rows, tail_lanes),
        ),
        compiler_params=params(),
        cost_estimate=cost(4),
    )(jnp.stack([side, place]), *back_in)

    back_args = (query_rot, *kv_blocks, attended_grad, attended, log_totals, bias)
    query_grads, kv_parts = pl.pallas_call(
        functools.partial(attend_grad_kernel, groups, n_exp),
        name="attend_grad",
        grid_spec=prefetch(
            num_scalar_prefetch=1,
            grid=(1,),
            in_specs=[whole(array) for array in back_args],
            out_specs=(full(tok_rows, q_width), full(n_exp, 2 * kv_width, tok_rows)),
            scratch_shapes=[vmem(seq_length, 2 * kv_width)],
        ),
        out_shape=(shaped(F32, tok_rows, q_width), shaped(BF, n_exp, 2 * kv_width, tok_rows)),
        compiler_params=params(),
        cost_estimate=cost(10),
    )(place[None], *back_args)
    kv_terms = exchange(after(kv_parts, out_home))

    slice_rows = full_width // (n_dp * n_exp)

    def slices_of(kernel, name, width, more, *arrays):
        dims = (n_exp, n_dp // 2, slice_rows, width)
        dims = dims if more else (n_exp * n_dp // 2, slice_rows, width)
        return pl.pallas_call(
            kernel,
            name=name,
            grid_spec=prefetch(
                num_scalar_prefetch=1,
                grid=(1,),
                in_specs=[whole(array) for array in arrays],
                out_specs=(full(*dims), full(*dims)) + tuple(full(*dim) for dim in more),
                scratch_shapes=[pltpu.VMEM((full_width, width), F32)],
            ),
            out_shape=(shaped(BF, *dims), shaped(BF, *dims)) + tuple(shaped(BF, *dim) for dim in more),
            compiler_params=params(),
            cost_estimate=cost(5),
        )(own_dp[None], *arrays)

    early_keep, early_send, query_low = slices_of(
        early_kernel, "early", 2 * q_width + tail_lanes, [(tok_rows, q_width)],
        branch_cot, attended_low, normed_two, logit_grads, gain_two_term, normed_one, query_grads, cosine, sine,
    )
    early = near_sum(early_keep, early_send).astype(BF)
    if crossing:
        kv_terms, half_grads = lax.optimization_barrier((kv_terms, half_grads))
    kv_terms, early = lax.optimization_barrier((kv_terms, early))
    grads_low, partial_low, gain_one_term = pl.pallas_call(
        input_kernel,
        name="input",
        out_shape=(
            shaped(BF, tok_rows, 2 * kv_width),
            shaped(BF, tok_rows, full_width),
            shaped(F32, 16, full_width),
        ),
        compiler_params=params(),
        cost_estimate=cost(4),
    )(query_low, kv_terms, cosine, sine, w_query, w_key, w_value, x_in, scale_one)
    partial_other = swap(partial_low, "tensor")
    late_keep, late_send = slices_of(
        functools.partial(late_kernel, n_exp), "late", 2 * kv_width + 128, (), normed_one, grads_low, gain_one_term, swap(gain_one_term, "tensor")
    )
    late_send, partial_other = lax.optimization_barrier((late_send, partial_other))
    late = near_sum(late_keep, late_send).astype(BF)
    early = place_sum(early)
    late, partial_other, early = lax.optimization_barrier((late, partial_other, early))
    same_core = [
        [dp * n_exp + z for dp in range(core, n_dp, 2) for z in range(n_exp)] for core in range(2)
    ]
    late_parts = lax.all_to_all(
        late, ("dp", "expert"), split_axis=0, concat_axis=0, tiled=True, axis_index_groups=same_core
    )
    if crossing:
        far = swap(after(half_grads, early), "dp", 2)
    early = far_sum(early, 0)

    def finish(base, count, totals, specs, earlier):
        some = lambda *tail: pl.BlockSpec((1,) + tail, lambda e: (base + e,) + (0,) * len(tail))
        return pl.pallas_call(
            functools.partial(finish_kernel, len(totals)),
            name="finish",
            grid=(count,),
            in_specs=specs + [pl.BlockSpec(memory_space=pl.ANY)] * len(earlier),
            out_specs=(some(slice_width, inner), some(slice_width, inner), some(inner, slice_width)),
            out_shape=(
                shaped(F32, experts_local, slice_width, inner),
                shaped(F32, experts_local, slice_width, inner),
                shaped(F32, experts_local, inner, slice_width),
            ),
            input_output_aliases={len(totals) + i: i for i in range(len(earlier))},
            compiler_params=params(),
            cost_estimate=cost(3),
        )(*totals, *earlier)

    one = by_expert(3, slice_width, inner)
    finals = finish(0, early_experts, (after(first_sum, partial_other),), [one], ())
    finals = finish(early_experts, summed - early_experts, (weight_sum,), [one], finals)
    if crossing:
        lead = pl.BlockSpec((1, 1, 3, slice_width, inner), lambda e: (0, e, 0, 0, 0))
        finals = finish(summed, crossing, (keep, near, far), [lead, lead, one], finals)
    grad_gate, grad_up, grad_down = finals
    late = jnp.sum(after(late_parts, grad_gate).astype(F32), axis=0)

    mixture_half = jnp.sum(out_home.astype(F32), axis=0)
    mixture_half = jnp.where(side == 0, mixture_half, jnp.roll(mixture_half, half_rows, axis=0))
    residual_half = lax.dynamic_slice_in_dim(hidden_one, side * half_width, half_width, 1)
    block_out = (residual_half + mixture_half).astype(BF)

    normed_one_grad = partial_low.astype(F32) + partial_other.astype(F32)
    inputs = x_in.astype(F32)
    input_part, _ = norm_backward(inputs, scale_one, norm1_gain, normed_one_grad)
    input_grad = hidden_grad + input_part
    gain_one = late[:, -1]
    return (
        block_out,
        input_grad,
        gain_one,
        early[:, q_width + tail_lanes :],
        late[:, :kv_width],
        late[:, kv_width : 2 * kv_width],
        early[:, :q_width].T,
        early[:, q_width + tail_lanes - 1],
        early[:, q_width : q_width + total_experts],
        grad_gate,
        grad_up,
        grad_down,
    )


def solution(mesh):
    return jax.shard_map(
        body,
        mesh=mesh,
        in_specs=(
            P(("dp", "expert"), None),
            P("dp"),
            P(("dp", "expert"), None),
            P(("dp", "expert"), None),
            P(),
            P(None, "tensor"),
            P(None, "tensor"),
            P(None, "tensor"),
            P("tensor", None),
            P(),
            P(),
            P("expert", None, "tensor"),
            P("expert", None, "tensor"),
            P("expert", "tensor", None),
        ),
        out_specs=(
            P(("dp", "expert"), "tensor"),
            P(("dp", "expert"), None),
            P(("dp", "expert")),
            P(("dp", "expert"), "tensor"),
            P(("dp", "expert"), "tensor"),
            P(("dp", "expert"), "tensor"),
            P("tensor", ("dp", "expert")),
            P(("dp", "expert")),
            P(("dp", "expert"), None),
            P("expert", "dp", "tensor"),
            P("expert", "dp", "tensor"),
            P("expert", "tensor", "dp"),
        ),
        check_vma=False,
    )
```
